128 devices in a mesh: section: 2 (over x_lo), dp: 64 (over x_hi, z, y, core).
Axes of the slice: x: 4 (x_hi: 2, x_lo: 2; x = x_hi * 2 + x_lo), y: 4, z: 4, core: 2. Of those that a mesh axis runs over, the one named last changes fastest.
Arguments:
- tokens: bfloat16 [8192, 1024], P('dp'), may hold values from -6 to 6
- segment_ids: int32 [8192], P('dp'), may hold values from 0 to 255, never falling along the last dimension, each value on 1 to 64 neighbouring positions
- gains: bfloat16 [2, 2, 1024], P('section', None, 'dp'), may hold values from 0.5 to 1.5
- biases: bfloat16 [2, 10, 1024], P('section', None, 'dp'), may hold values from -4 to 4
- w_qkv: bfloat16 [2, 1024, 3072], P('section', None, 'dp'), may hold values from -0.1875 to 0.1875
- w_proj: bfloat16 [2, 1024, 1024], P('section', None, 'dp'), may hold values from -0.375 to 0.375
- w_fc: bfloat16 [2, 1024, 4096], P('section', None, 'dp'), may hold values from -0.1875 to 0.1875
- w_out: bfloat16 [2, 4096, 1024], P('section', None, 'dp'), may hold values from -0.09375 to 0.09375
- cotangent: bfloat16 [8192, 1024], P('dp'), may hold values from -16 to 16
Outputs:
- activations: bfloat16 [2, 8192, 1024], P('section', 'dp')
- input_grads: bfloat16 [2, 8192, 1024], P('section', 'dp')
- grad_gains: float32 [2, 2, 1024], P('section', None, 'dp')
- grad_biases: float32 [2, 10, 1024], P('section', None, 'dp')
- grad_qkv: float32 [2, 1024, 3072], P('section', None, 'dp')
- grad_proj: float32 [2, 1024, 1024], P('section', None, 'dp')
- grad_fc: float32 [2, 1024, 4096], P('section', None, 'dp')
- grad_out: float32 [2, 4096, 1024], P('section', None, 'dp')
The draws below stay inside these ranges and needn't reach their ends.
Inputs may be any that keep to these rules, and one draw needn't show every extreme that they name: `segment_ids`: document numbers never fall along the tokens; each document has 1 to 64 tokens and one has exactly 64.
All inputs are finite; a program needn't handle non-finite values.
Results may differ from the reference program's by a relative error of at most 0.015.
Values may be sent and summed in bfloat16 or wider, within the bound.
A program may use at most 256 MiB of HBM per device.

```python
import math
import jax
import jax.numpy as jnp
import numpy as np
from jax import lax

D = 1024
HEAD = 64
FF = 4096
MB_TOK = 64
TOKENS = 8192
DOCS = 256


def with_spikes(values, key, source, target, shards_of, factor):
    owner, partner = [(jnp.arange(values.shape[dim]) // (values.shape[dim] // shards_of)).reshape([-1 if axis == dim else 1 for axis in range(values.ndim)]) for dim in (source, target)]
    chosen = jax.random.permutation(key, shards_of)[partner]
    strong = (owner == chosen) | (owner == (partner + shards_of // 2) % shards_of)
    return jnp.where(strong, factor * values, values)


def shard_levels(rng, extent, cuts, smallest, largest):
    def one(axis_at, shards_of):
        heights = jax.random.uniform(jax.random.fold_in(jax.random.fold_in(rng, 6), axis_at), (shards_of,), jnp.float32, smallest / len(cuts), largest / len(cuts))
        return jnp.repeat(jnp.exp(heights), extent[axis_at] // shards_of).reshape((-1,) + (1,) * (len(extent) - axis_at - 1))

    level = one(*cuts[0])
    for cut in cuts[1:]:
        level = level * one(*cut)
    return level


def split_up(count, total, reach, lean):
    weights = [(1 << 20) // math.isqrt(grade ** lean) + 1 for grade in range(2, count + 1)]
    surplus, counts = total - reach - (count - 1), [1] * (count - 1)
    while surplus > 0:
        movable = [i for i in range(count - 1) if counts[i] < reach]
        whole, remaining = sum([weights[i] for i in movable]), surplus
        for i in movable:
            more = min(reach - counts[i], max(1, remaining * weights[i] // whole), surplus)
            counts[i] = counts[i] + more
            surplus = surplus - more
    return np.array([reach] + counts)


def uneven(rng, count, total, bound, lean):
    if count == 2:
        one = jax.random.randint(rng, (), max(1, total - bound), min(bound, total - 1) + 1)
        return jnp.stack([one, total - one])
    sizes = jnp.asarray(split_up(count, total, bound, lean), jnp.int32)
    pairs = (count - 1) // 2
    donor, taker = sizes[1:1 + 2 * pairs:2], sizes[2:2 + 2 * pairs:2]
    room = jnp.minimum(donor - 1, bound - taker)
    passed = jax.random.randint(jax.random.fold_in(rng, 1), (pairs,), 0, 1 << 20) % (room + 1)
    sizes = sizes.at[1:1 + 2 * pairs:2].set(donor - passed).at[2:2 + 2 * pairs:2].set(taker + passed)
    return sizes[jax.random.permutation(jax.random.fold_in(rng, 2), count)]


def normal_values(stream_key, extent, scale, bound, split=(), dtype=jnp.bfloat16):
    level = shard_levels(stream_key, extent, split, -0.22, 0.18) if split else 1.0
    values = jax.random.normal(stream_key, extent, jnp.float32) * scale * level
    return jnp.minimum(jnp.maximum(values, -bound), bound).astype(dtype)


def bell_draw_with(own_key, extent, scale, most, shards, heavy, kind=jnp.bfloat16):
    entries = scale * jax.random.normal(own_key, extent, jnp.float32)
    if shards:
        entries = entries * shard_levels(own_key, extent, shards, -0.22, 0.18)
    return jnp.clip(with_spikes(entries, jax.random.fold_in(own_key, 3), *heavy), -most, most).astype(kind)


def setup_inputs(seed: int = 0) -> dict:
    key_list = jax.random.split(jax.random.key(seed), 10)
    return {
        "tokens": normal_values(key_list[0], (TOKENS, D), 1.0, 6.0, ((0, 64),)),
        "segment_ids": jnp.searchsorted(jnp.cumsum(uneven(key_list[1], DOCS, TOKENS, MB_TOK, 2)), jnp.arange(TOKENS), side="right").astype(jnp.int32),
        "gains": jnp.clip(1.0 + 0.1 * jax.random.normal(key_list[2], (2, 2, D), jnp.float32), 0.5, 1.5).astype(jnp.bfloat16),
        "biases": normal_values(key_list[3], (2, 10, D), 0.3, 4.0, ((0, 2), (2, 64))),
        "w_qkv": normal_values(key_list[4], (2, D, 3 * D), D ** -0.5, 0.1875, ((0, 2), (2, 64))),
        "w_proj": normal_values(key_list[5], (2, D, D), (D // 4) ** -0.5, 0.375, ((0, 2), (2, 64))),
        "w_fc": normal_values(key_list[6], (2, D, FF), D ** -0.5, 0.1875, ((0, 2), (2, 64))),
        "w_out": normal_values(key_list[7], (2, FF, D), FF ** -0.5, 0.09375, ((0, 2), (2, 64))),
        "cotangent": bell_draw_with(key_list[8], (TOKENS, D), 1.0, 16.0, ((0, 64),), (0, 1, 64, 4.0)),
    }


EPS = 1e-05

@jax.custom_vjp
def low(v):
    return lax.optimization_barrier(v.astype(jnp.bfloat16)).astype(jnp.float32)

@jax.custom_vjp
def low_back(v):
    return v

def low_keep(v):
    return (low(v), None)

def low_pass(kept, grad):
    return (grad,)

def back_keep(v):
    return (v, None)

def back_low(kept, grad):
    return (low(grad),)
low.defvjp(low_keep, low_pass)
low_back.defvjp(back_keep, back_low)

def norm_rows(values, gain, shift):
    centre = values - lax.optimization_barrier(jnp.mean(values, axis=-1, keepdims=True))
    spread = lax.optimization_barrier(jnp.mean(centre * centre, axis=-1, keepdims=True))
    return centre * lax.rsqrt(spread + EPS) * gain + shift

def gelu_tanh(values):
    return jax.nn.gelu(values, approximate=True)

def matmul(left, right):
    return jnp.dot(left, right, precision=lax.Precision.HIGHEST)

def attention(query, keys, values, seg):
    rows, width = query.shape
    heads = width // HEAD
    q_heads = query.reshape(-1, MB_TOK, heads, HEAD)
    k_heads = keys.reshape(-1, MB_TOK, heads, HEAD)
    v_heads = values.reshape(-1, MB_TOK, heads, HEAD)
    packs = seg.reshape(-1, MB_TOK)
    order = jnp.arange(MB_TOK)
    allowed = (packs[:, :, None] == packs[:, None, :]) & (order[None, None, :] <= order[None, :, None])
    raw = jnp.einsum('pqhd,pkhd->phqk', q_heads, k_heads, precision=lax.Precision.HIGHEST) * HEAD ** (-0.5)
    scores = jnp.where(allowed[:, None], low_back(raw), -1e+30)
    probs = low(jax.nn.softmax(scores, axis=-1))
    result = jnp.einsum('phqk,pkhd->pqhd', probs, v_heads, precision=lax.Precision.HIGHEST)
    return result.reshape(rows, width)

def block(inp, seg, gains, biases, w_qkv, w_proj, w_fc, w_out):
    width = inp.shape[1]
    first = low(norm_rows(inp, gains[0], biases[0]))
    mixed = matmul(first, w_qkv)
    query = low(low_back(mixed[:, :width] + biases[1]))
    keys = low(low_back(mixed[:, width:2 * width]))
    values = low(low_back(mixed[:, 2 * width:] + biases[2]))
    attended = low(low_back(attention(query, keys, values, seg)))
    branch = low_back(matmul(attended, w_proj) + biases[3])
    middle = inp + branch
    second = low(norm_rows(middle, gains[1], biases[4]))
    pre = low_back(matmul(second, w_fc) + biases[5:9].reshape(-1))
    act = low(gelu_tanh(pre))
    final = low_back(matmul(act, w_out) + biases[9])
    return middle + final

def reference(tokens, segment_ids, gains, biases, w_qkv, w_proj, w_fc, w_out, cotangent):

    def widen(array):
        return array.astype(jnp.float32)

    def whole(inp, nudge, gain_all, bias_all, qkv_all, proj_all, fc_all, out_all):
        hidden = low_back(low(block(inp, segment_ids, gain_all[0], bias_all[0], qkv_all[0], proj_all[0], fc_all[0], out_all[0])))
        final = block(hidden + nudge, segment_ids, gain_all[1], bias_all[1], qkv_all[1], proj_all[1], fc_all[1], out_all[1])
        return (hidden, final)
    start = widen(tokens)
    nudge = jnp.zeros_like(start)
    (hidden, final), pull = jax.vjp(whole, start, nudge, widen(gains), widen(biases), widen(w_qkv), widen(w_proj), widen(w_fc), widen(w_out))
    grads = pull((jnp.zeros_like(hidden), widen(cotangent)))
    activations = jnp.stack([hidden, final]).astype(jnp.bfloat16)
    input_grads = jnp.stack([grads[0], grads[1]]).astype(jnp.bfloat16)
    return (activations, input_grads, grads[2], grads[3], grads[4], grads[5], grads[6], grads[7])
```

```python
import jax
import jax.numpy as jnp
from jax import lax
from jax.experimental import pallas as pl
from jax.experimental.pallas import tpu as pltpu
from jax.sharding import PartitionSpec as P

MESH = pl.DeviceIdType.MESH
F32 = jnp.float32
BF16 = jnp.bfloat16
EPS = 1e-05
ROWS = 128
WIDTH = 1024
HEAD = 64
GC = 0.7978845608028654
NT = (((1,), (1,)), ((), ()))

PARTS = {"B": (0, 4), "C": (4, 4), "A1": (8, 2), "A2": (10, 2)}
INNER_IS_Y = {"B": False, "C": True, "A1": True, "A2": False}


def remote(src, dst, ssem, rsem, target):
    return pltpu.make_async_remote_copy(
        src_ref=src, dst_ref=dst, send_sem=ssem, recv_sem=rsem, device_id=target, device_id_type=MESH
    )


class Ring:
    def __init__(self, view, pos, left, right, ssem, rsem):
        self.view, self.pos, self.left, self.right = view, pos, left, right
        self.ssem, self.rsem = ssem, rsem

    def at(self, off):
        return lax.rem(self.pos + off, 4)

    def cp(self, off, half, slot, target):
        ref = self.view(self.at(off), half)
        return remote(ref, ref, self.ssem(slot), self.rsem(slot), target)

    def start(self):
        self.cp(0, None, 0, self.right).start()
        self.cp(0, None, 1, self.left).start()

    def mid(self):
        self.cp(3, None, 0, self.right).wait_recv()
        self.cp(3, 0, 2, self.right).start()
        self.cp(1, None, 1, self.left).wait_recv()
        self.cp(1, 1, 3, self.left).start()

    def end(self):
        self.cp(2, 0, 2, self.right).wait_recv()
        self.cp(2, 1, 3, self.left).wait_recv()

    def sent(self):
        self.cp(0, None, 0, self.right).wait_send()
        self.cp(0, None, 1, self.left).wait_send()
        self.cp(3, 0, 2, self.right).wait_send()
        self.cp(1, 1, 3, self.left).wait_send()


class SumRing:
    def __init__(self, view, pos, left, right, bufs, ssem, rsem, add):
        self.view, self.pos, self.left, self.right = view, pos, left, right
        self.half_l, self.half_r, self.full_l, self.full_r = bufs
        self.ssem, self.rsem, self.add = ssem, rsem, add

    def at(self, off):
        return lax.rem(self.pos + off, 4)

    def cp(self, k):
        off, half, buf, target = (
            (2, 0, self.half_l, self.right),
            (2, 1, self.half_r, self.left),
            (1, None, self.full_l, self.right),
            (3, None, self.full_r, self.left),
        )[k]
        return remote(self.view(self.at(off), half), buf, self.ssem(k), self.rsem(k), target)

    def start(self):
        self.cp(0).start()
        self.cp(1).start()

    def mid(self):
        self.cp(0).wait_recv()
        self.add(self.view(self.at(1), 0), (self.half_l,))
        self.cp(2).start()
        self.cp(1).wait_recv()
        self.add(self.view(self.at(3), 1), (self.half_r,))
        self.cp(3).start()

    def end(self):
        self.cp(2).wait_recv()
        self.cp(3).wait_recv()
        self.add(self.view(self.pos, None), (self.full_l, self.full_r))

    def sent(self):
        for k in range(4):
            self.cp(k).wait_send()


def add_into(view, terms):
    lead = view.shape[:-2]
    count = 1
    for size in lead:
        count *= size

    def body(step, carry):
        index, rest = [], step
        for size in reversed(lead):
            index.append(lax.rem(rest, size))
            rest = lax.div(rest, size)
        index = tuple(reversed(index))
        total = view[index].astype(F32)
        for term in terms:
            total = total + term[index].astype(F32)
        view[index] = total.astype(BF16)
        return carry

    lax.fori_loop(0, count, body, 0)


def kernel(
    tok_ref, seg_ref, gains_ref, bias_ref, qkv_ref, proj_ref, fc_ref, wout_ref, cot_ref,
    act_out, grad_out, ggain_out, gbias_out, gqkv_out, gproj_out, gfc_out, gwout_out,
    w, rb_outer, rb_half, rb_inner, rb_ihalf, rb_x, ra_x, ra_outer, ra_half, ra_inner, ra_ihalf,
    xin, x1, x2, x3, x4, qkv, probs, xh1, xh2, rs1, rs2, dgel, gf, dpre, dbr, datt, dmix, dmid, mask, qbias,
    bf, sgb, sb_y, sb_c, sb_x, sbw, sr, sr_c, sr_x, sr_z, sr_y,
    s_out, s_fc, s_proj, s_qkv, t_out, t_fc, t_proj, t_qkv, hb,
    loc_sem, ag_s, ag_r, agx_s, agx_r, sib_s, sib_r, rs_s, rs_r, rsx_s, rsx_r, ex_s, ex_r, sm_s, sm_r, sec_s, sec_r,
):
    sec = lax.axis_index("section")
    dp = lax.axis_index("dp")
    c = lax.rem(dp, 2)
    y = lax.rem(lax.div(dp, 2), 4)
    z = lax.rem(lax.div(dp, 8), 4)
    x = lax.div(dp, 32)
    ox, oc = 1 - x, 1 - c

    def at(px, pz, py, pc):
        return (sec, ((px * 4 + pz) * 4 + py) * 2 + pc)

    ys = [at(x, z, lax.rem(y + k, 4), c) for k in range(4)]
    zs = [at(x, lax.rem(z + k, 4), y, c) for k in range(4)]
    xp = at(ox, z, y, c)
    sib = at(x, z, y, oc)
    other_section = (1 - sec, dp)

    own = w.at[x, z, y, c]
    local = [
        pltpu.make_async_copy(qkv_ref, own.at[pl.ds(0, 3)], loc_sem.at[0]),
        pltpu.make_async_copy(proj_ref, own.at[pl.ds(3, 1)], loc_sem.at[1]),
        pltpu.make_async_copy(fc_ref, own.at[pl.ds(4, 4)], loc_sem.at[2]),
    ] + [
        pltpu.make_async_copy(wout_ref.at[:, pl.ds(1024 * j, 1024)], own.at[8 + j], loc_sem.at[3 + j]) for j in range(4)
    ]
    for cp in local:
        cp.start()
    barrier = pltpu.get_barrier_semaphore()
    partners = ys[1:] + zs[1:] + [xp, sib, other_section]
    for target in partners:
        pl.semaphore_signal(barrier, 1, device_id=target, device_id_type=MESH)
    pl.semaphore_wait(barrier, len(partners))
    for cp in local:
        cp.wait()

    def line(part, xx, o, half=None, core=None):
        base, size = PARTS[part]
        core = c if core is None else core
        inner = slice(None) if half is None else pl.ds(2 * half, 2)
        if INNER_IS_Y[part]:
            return w.at[xx, o, inner, core, pl.ds(base, size)]
        return w.at[xx, inner, o, core, pl.ds(base, size)]

    def single(part, xx, i, half=None):
        base, size = PARTS[part]
        if half is not None:
            size = size // 2
            base = base + half * size
        if INNER_IS_Y[part]:
            return w.at[xx, z, i, c, pl.ds(base, size)]
        return w.at[xx, i, y, c, pl.ds(base, size)]

    def axes(part):
        yy, zz = (y, ys[3], ys[1]), (z, zs[3], zs[1])
        return (yy, zz) if INNER_IS_Y[part] else (zz, yy)

    names = ("B", "C", "A1", "A2")

    def xside(other):
        return ox if other else x

    def gather_rings(part, other):
        inner, outer = axes(part)
        slot = names.index(part) * 2 + other
        xx = xside(other)
        first = Ring(lambda i, h: single(part, xx, i, h), *inner,
                     lambda k: ag_s.at[slot, 0, k], lambda k: ag_r.at[slot, 0, k])
        second = Ring(lambda o, h: line(part, xx, o, h), *outer,
                      lambda k: ag_s.at[slot, 1, k], lambda k: ag_r.at[slot, 1, k])
        return first, second

    rings = {(part, other): gather_rings(part, other) for part in ("B", "C") for other in (0, 1)}
    rings.update({(part, 0): gather_rings(part, 0) for part in ("A1", "A2")})

    def outer_pos(part):
        return z if INNER_IS_Y[part] else y

    def to_sibling(part, other, off, core=None):
        o = lax.rem(outer_pos(part) + off, 4)
        ref = line(part, xside(other), o, None, core)
        k = names.index(part)
        return remote(ref, ref, sib_s.at[k, other, off], sib_r.at[k, other, off], sib)

    def x_line(part, other, off):
        o = lax.rem(outer_pos(part) + off, 4)
        ref = line(part, xside(other), o)
        k = names.index(part) - 2
        return remote(ref, ref, agx_s.at[2 + k * 4 + off], agx_r.at[2 + k * 4 + off], xp)

    def x_single(part, other):
        k = names.index(part)
        ref = single(part, xside(other), z if not INNER_IS_Y[part] else y)
        return remote(ref, ref, agx_s.at[k], agx_r.at[k], xp)

    ring_a1, ring_a2 = rings["A1", 0], rings["A2", 0]
    x_single("B", 0).start()
    x_single("C", 0).start()
    ring_a1[0].start()
    ring_a2[0].start()
    rings["B", 0][0].start()
    rings["C", 0][0].start()

    sgb[...] = jnp.zeros_like(sgb)
    sgb[0:2, :] = gains_ref[...].astype(F32)
    sgb[2:12, :] = bias_ref[...].astype(F32)
    spread = (
        lax.broadcasted_iota(jnp.int32, (16, 128), 1)
        == lax.broadcasted_iota(jnp.int32, (16, 128), 0) + 16 * (y * 2 + c)
    ).astype(F32)
    sb_y[0] = jnp.dot(sgb[...].astype(BF16), spread.astype(BF16), preferred_element_type=F32)

    def small(slot, src, dst, target):
        return remote(src, dst, sm_s.at[slot], sm_r.at[slot], target)

    small_y = [small(k - 1, sb_y.at[0], sb_y.at[k], ys[k]) for k in (1, 2, 3)]
    for cp in small_y:
        cp.start()

    ring_a1[0].mid()
    ring_a2[0].mid()
    rings["B", 0][0].mid()
    rings["C", 0][0].mid()
    ring_a1[0].end()
    ring_a1[1].start()
    x_line("A1", 0, 0).start()
    ring_a2[0].end()
    ring_a2[1].start()
    x_line("A2", 0, 0).start()
    to_sibling("A1", 0, 0).start()
    to_sibling("A2", 0, 0).start()
    x_single("B", 1).wait_recv()
    rings["B", 1][0].start()
    x_single("C", 1).wait_recv()
    rings["C", 1][0].start()

    for cp in small_y:
        cp.wait_recv()
    sb_c[0] = sb_y[0] + sb_y[1] + sb_y[2] + sb_y[3]
    small_c = small(3, sb_c.at[0], sb_c.at[1], sib)
    small_c.start()

    for part in ("B", "C"):
        rings[part, 0][0].end()
        rings[part, 0][1].start()
        to_sibling(part, 0, 0).start()

    seg_col = jnp.broadcast_to(seg_ref[...].astype(F32), (ROWS, ROWS))
    qi = lax.broadcasted_iota(jnp.int32, (ROWS, ROWS), 0)
    ki = lax.broadcasted_iota(jnp.int32, (ROWS, ROWS), 1)
    allowed = (seg_col == seg_col.T) & (ki <= qi) & (lax.div(qi, 64) == lax.div(ki, 64))
    mask[...] = allowed.astype(F32)

    small_c.wait_recv()
    sb_x[x, z] = sb_c[0] + sb_c[1]
    small_z = [small(3 + k, sb_x.at[x, z], sb_x.at[x, z], zs[k]) for k in (1, 2, 3)]
    for cp in small_z:
        cp.start()

    def a_mid(part, ring):
        ring[1].mid()
        for off in (3, 1):
            x_line(part, 0, off).start()
            to_sibling(part, 0, off).start()

    a_mid("A1", ring_a1)
    a_mid("A2", ring_a2)
    rings["B", 1][0].mid()
    rings["C", 1][0].mid()
    for part in ("B", "C"):
        rings[part, 1][0].end()
        rings[part, 1][1].start()
        to_sibling(part, 1, 0).start()
    for part, ring in (("A1", ring_a1), ("A2", ring_a2)):
        ring[1].end()
        x_line(part, 0, 2).start()
        to_sibling(part, 0, 2).start()

    for k in (1, 2, 3):
        from_z = lax.rem(z + 4 - k, 4)
        small(3 + k, sb_x.at[x, from_z], sb_x.at[x, from_z], zs[k]).wait_recv()
    small_x = small(7, sb_x.at[x], sb_x.at[x], xp)
    small_x.start()

    def bulk_mid(part, other):
        rings[part, other][1].mid()
        for off in (3, 1):
            to_sibling(part, other, off).start()

    def bulk_end(part, other):
        rings[part, other][1].end()
        to_sibling(part, other, 2).start()

    bulk_mid("B", 0)
    bulk_mid("C", 0)
    small(7, sb_x.at[ox], sb_x.at[ox], xp).wait_recv()
    for g in range(8):
        bf[:, g * 128 : (g + 1) * 128] = sb_x[g // 4, g % 4]
    qbias[:, 0:WIDTH] = bf[3:4, :]
    qbias[:, WIDTH : 2 * WIDTH] = jnp.zeros((1, WIDTH), F32)
    qbias[:, 2 * WIDTH :] = bf[4:5, :]

    def row(k):
        return bf[k : k + 1, :]

    bulk_end("B", 0)
    bulk_mid("B", 1)
    bulk_end("C", 0)
    bulk_mid("C", 1)

    def a_pass_on(off):
        for part in ("A1", "A2"):
            x_line(part, 1, off).wait_recv()
            to_sibling(part, 1, off).start()

    a_pass_on(0)
    bulk_end("B", 1)
    bulk_end("C", 1)

    def from_sibling(part):
        for other in (0, 1):
            for off in (0, 3, 1, 2):
                to_sibling(part, other, off, oc).wait_recv()

    handed_on = remote(act_out, hb, sec_s, sec_r, other_section)
    handed_back = remote(grad_out, hb, sec_s, sec_r, other_section)

    @pl.when(sec == 0)
    def _():
        xin[...] = tok_ref[...].astype(F32)

    @pl.when(sec == 1)
    def _():
        handed_on.wait_recv()
        xin[...] = hb[...].astype(F32)

    def norm(values, gain, shift):
        centre = values - jnp.mean(values, axis=-1, keepdims=True)
        rs = lax.rsqrt(jnp.mean(centre * centre, axis=-1, keepdims=True) + EPS)
        hat = centre * rs
        return hat, rs, (hat * gain + shift).astype(BF16)

    def exchange(slot, src, dst):
        return remote(src, dst, ex_s.at[slot], ex_r.at[slot], sib)

    xh1[...], rs1[...], x1[0] = norm(xin[...], row(0), row(2))
    ex_first = exchange(0, x1.at[0], x1.at[1])
    ex_first.start()
    from_sibling("B")

    def qkv_weights(k):
        return w[k, :, :, :, 0:3].reshape(1536, WIDTH)

    for k in range(2):
        cols = slice(1536 * k, 1536 * (k + 1))
        mixed = lax.dot_general(x1[0], qkv_weights(k), NT, preferred_element_type=F32)
        qkv[:, cols] = (mixed + qbias[:, cols]).astype(BF16)

    low_lanes = lax.broadcasted_iota(jnp.int32, (ROWS, 128), 1) < HEAD
    zero = jnp.zeros((ROWS, 128), BF16)

    def pair(base, hp):
        return pl.ds(pl.multiple_of(base + hp * 128, 128), 128)

    def attend(hp, carry):
        q, k, v = (qkv[:, pair(base, hp)] for base in (0, WIDTH, 2 * WIDTH))
        parts = []
        for e in range(2):
            qm = jnp.where(low_lanes if e == 0 else ~low_lanes, q, zero)
            scores = lax.dot_general(qm, k, NT, preferred_element_type=F32) * 0.125
            scores = jnp.where(mask[...] > 0.5, scores, -1e30)
            top = jnp.max(scores, axis=-1, keepdims=True)
            ex = jnp.exp(scores - top)
            p = ex / jnp.sum(ex, axis=-1, keepdims=True)
            probs[2 * hp + e] = p
            parts.append(jnp.dot(p.astype(BF16), v, preferred_element_type=F32))
        x2[0, :, pair(0, hp)] = jnp.where(low_lanes, parts[0], parts[1]).astype(BF16)
        return carry

    lax.fori_loop(0, 8, attend, 0)
    ex_att = exchange(1, x2.at[0], x2.at[1])
    ex_att.start()

    a_pass_on(3)
    proj_w = w[:, :, :, :, 3].reshape(WIDTH, WIDTH)
    xin[...] = xin[...] + (lax.dot_general(x2[0], proj_w, NT, preferred_element_type=F32) + row(5))
    xh2[...], rs2[...], x3[0] = norm(xin[...], row(1), row(6))
    ex_second = exchange(2, x3.at[0], x3.at[1])
    ex_second.start()
    from_sibling("C")
    a_pass_on(1)

    def fc_weights(j):
        return w[lax.div(j, 2), pl.ds(2 * lax.rem(j, 2), 2), :, :, 4:8].reshape(WIDTH, WIDTH)

    def up(j, carry):
        pre = lax.dot_general(x3[0], fc_weights(j), NT, preferred_element_type=F32) + bf[pl.ds(7 + j, 1), :]
        square = pre * pre
        t = jnp.tanh(GC * (pre + 0.044715 * (square * pre)))
        half = 0.5 * (1.0 + t)
        x4[0, j] = (pre * half).astype(BF16)
        dgel[j] = half + (0.5 * GC) * pre * (1.0 - t * t) * (1.0 + 0.134145 * square)
        return carry

    lax.fori_loop(0, 4, up, 0)
    ex_act = exchange(3, x4.at[0], x4.at[1])
    ex_act.start()
    a_pass_on(2)
    from_sibling("A1")
    from_sibling("A2")

    def wout_weights(j):
        return w[:, :, :, :, 8 + j].reshape(WIDTH, WIDTH)

    xin[...] = xin[...] + row(11)

    def down(j, carry):
        xin[...] += lax.dot_general(x4[0, j], wout_weights(j), NT, preferred_element_type=F32)
        return carry

    lax.fori_loop(0, 4, down, 0)
    act_out[...] = xin[...].astype(BF16)

    @pl.when(sec == 0)
    def _():
        handed_on.start()

    for key in rings:
        rings[key][0].sent()
        rings[key][1].sent()
    for part in ("B", "C"):
        x_single(part, 0).wait_send()
    for part in names:
        for other in (0, 1):
            for off in range(4):
                to_sibling(part, other, off).wait_send()
                if part in ("A1", "A2") and other == 0:
                    x_line(part, 0, off).wait_send()
    for cp in small_y + [small_c] + small_z + [small_x]:
        cp.wait_send()

    sbw[...] = jnp.zeros_like(sbw)

    @pl.when(sec == 0)
    def _():
        handed_back.wait_recv()
        gf[...] = hb[...]

    @pl.when(sec == 1)
    def _():
        gf[...] = cot_ref[...]

    def column_sum(values):
        return jnp.sum(values.astype(F32), axis=0, keepdims=True)

    sbw[11:12, :] = column_sum(gf[...])
    s_out[...] = gf[...].T.reshape(2, 4, 4, 2, 1, 16, ROWS)

    def swap(slot, src, dst):
        return exchange(slot, src.at[:, :, :, oc], dst)

    ex_gf = swap(4, s_out, t_out)
    ex_gf.start()

    def back_act(j, carry):
        d_act = jnp.dot(gf[...], wout_weights(j), preferred_element_type=F32)
        d_pre = (dgel[j] * d_act).astype(BF16)
        dpre[j] = d_pre
        sbw[pl.ds(7 + j, 1), :] = column_sum(d_pre)
        s_fc[lax.div(j, 2), pl.ds(2 * lax.rem(j, 2), 2)] = d_pre.T.reshape(2, 4, 2, 4, 16, ROWS)
        return carry

    lax.fori_loop(0, 4, back_act, 0)
    ex_dpre = swap(5, s_fc, t_fc)
    ex_dpre.start()

    def lhs(mine, theirs, rows):
        return jnp.concatenate([mine.reshape(rows, ROWS), theirs.reshape(rows, ROWS)], axis=1)

    def sum_rings(part, other):
        inner, outer = axes(part)
        slot = names.index(part) * 2 + other
        xx = xside(other)
        if part in ("B", "C"):
            k = names.index(part) * 2 + other
            ibufs = (rb_ihalf.at[k, 0], rb_ihalf.at[k, 1], rb_inner.at[k, 0], rb_inner.at[k, 1])
            obufs = (rb_half.at[k, 0], rb_half.at[k, 1], rb_outer.at[k, 0], rb_outer.at[k, 1])
        else:
            k = names.index(part) - 2
            ibufs = (ra_ihalf.at[k, 0], ra_ihalf.at[k, 1], ra_inner.at[k, 0], ra_inner.at[k, 1])
            obufs = (ra_half.at[k, 0], ra_half.at[k, 1], ra_outer.at[k, 0], ra_outer.at[k, 1])
        first = SumRing(lambda o, h: line(part, xx, o, h), *outer, obufs,
                        lambda k: rs_s.at[slot, 0, k], lambda k: rs_r.at[slot, 0, k], add_into)
        second = SumRing(lambda i, h: single(part, xx, i, h), *inner, ibufs,
                         lambda k: rs_s.at[slot, 1, k], lambda k: rs_r.at[slot, 1, k], add_into)
        return first, second

    sums = {(part, other): sum_rings(part, other) for part in ("B", "C") for other in (0, 1)}
    sums.update({(part, 0): sum_rings(part, 0) for part in ("A1", "A2")})

    def x_sum(part, off):
        k = names.index(part) - 2
        o = lax.rem(outer_pos(part) + off, 4)
        return remote(line(part, ox, o), ra_x.at[k, off], rsx_s.at[2 + k * 4 + off], rsx_r.at[2 + k * 4 + off], xp)

    def x_last(part):
        k = names.index(part)
        return remote(single(part, ox, y if INNER_IS_Y[part] else z), rb_x.at[k], rsx_s.at[k], rsx_r.at[k], xp)

    def grads_out():
        ex_gf.wait_recv()
        ex_act.wait_recv()
        for other in (1, 0):
            xx = xside(other)
            left = lhs(s_out[xx, :, :, c], t_out[xx], 256)

            def body(j, carry):
                right = x4[:, j].reshape(2 * ROWS, WIDTH)
                w[xx, :, :, c, 8 + j] = (
                    jnp.dot(left, right, preferred_element_type=F32).astype(BF16).reshape(4, 4, 16, WIDTH)
                )
                return carry

            lax.fori_loop(0, 4, body, 0)
            if other:
                for off in (2, 1, 3, 0):
                    for part in ("A1", "A2"):
                        x_sum(part, off).start()

    def grads_fc():
        ex_dpre.wait_recv()
        ex_second.wait_recv()
        right = x3[...].reshape(2 * ROWS, WIDTH)
        for other in (1, 0):
            xx = xside(other)

            def body(k, carry):
                zz = pl.ds(2 * k, 2)
                left = lhs(s_fc[xx, zz, :, c], t_fc[xx, zz], 512)
                w[xx, zz, :, c, 4:8] = (
                    jnp.dot(left, right, preferred_element_type=F32).astype(BF16).reshape(2, 4, 4, 16, WIDTH)
                )
                return carry

            lax.fori_loop(0, 2, body, 0)
            sums["C", other][0].start()

    @pl.when(sec == 0)
    def _():
        grads_out()

    def back_second(j, carry):
        dmid[...] += jnp.dot(dpre[j], fc_weights(j), preferred_element_type=F32)
        return carry

    dmid[...] = jnp.zeros_like(dmid)
    lax.fori_loop(0, 4, back_second, 0)

    def norm_back(d_out, hat, rs, gain):
        d_hat = d_out * gain
        mean_one = jnp.mean(d_hat, axis=-1, keepdims=True)
        mean_two = jnp.mean(d_hat * hat, axis=-1, keepdims=True)
        return rs * (d_hat - mean_one - hat * mean_two)

    d_second = dmid[...]
    sbw[1:2, :] = column_sum(d_second * xh2[...])
    sbw[6:7, :] = column_sum(d_second)
    dmid[...] = gf[...].astype(F32) + norm_back(d_second, xh2[...], rs2[...], row(1))
    dbr[...] = dmid[...].astype(BF16)
    sbw[5:6, :] = column_sum(dbr[...])
    s_proj[...] = dbr[...].T.reshape(2, 4, 4, 2, 1, 16, ROWS)
    ex_dbr = swap(6, s_proj, t_proj)
    ex_dbr.start()

    @pl.when(sec == 0)
    def _():
        grads_fc()

    datt[...] = jnp.dot(dbr[...], proj_back(w), preferred_element_type=F32).astype(BF16)

    def attend_back(hp, carry):
        q, k, v = (qkv[:, pair(base, hp)] for base in (0, WIDTH, 2 * WIDTH))
        da = datt[:, pair(0, hp)]
        dq, dk, dv = [], [], []
        for e in range(2):
            lanes = low_lanes if e == 0 else ~low_lanes
            dam = jnp.where(lanes, da, zero)
            qm = jnp.where(lanes, q, zero)
            p = probs[2 * hp + e]
            dv.append(jnp.dot(p.astype(BF16).T, dam, preferred_element_type=F32))
            dp_ = lax.dot_general(dam, v, NT, preferred_element_type=F32)
            ds = (p * (dp_ - jnp.sum(dp_ * p, axis=-1, keepdims=True))).astype(BF16)
            dq.append(jnp.dot(ds, k, preferred_element_type=F32))
            dk.append(jnp.dot(ds.T, qm, preferred_element_type=F32))
        dmix[:, pair(0, hp)] = (jnp.where(low_lanes, dq[0], dq[1]) * 0.125).astype(BF16)
        dmix[:, pair(WIDTH, hp)] = ((dk[0] + dk[1]) * 0.125).astype(BF16)
        dmix[:, pair(2 * WIDTH, hp)] = (dv[0] + dv[1]).astype(BF16)
        return carry

    lax.fori_loop(0, 8, attend_back, 0)
    for k in range(2):
        s_qkv[k] = dmix[:, 1536 * k : 1536 * (k + 1)].T.reshape(4, 4, 2, 3, 16, ROWS)
    ex_dmix = swap(7, s_qkv, t_qkv)
    ex_dmix.start()
    sbw[3:4, :] = column_sum(dmix[:, 0:WIDTH])
    sbw[4:5, :] = column_sum(dmix[:, 2 * WIDTH :])
    d_first = jnp.dot(dmix[:, 0:1536], qkv_weights(0), preferred_element_type=F32)
    d_first = d_first + jnp.dot(dmix[:, 1536:], qkv_weights(1), preferred_element_type=F32)
    sbw[0:1, :] = column_sum(d_first * xh1[...])
    sbw[2:3, :] = column_sum(d_first)
    grad_out[...] = (dmid[...] + norm_back(d_first, xh1[...], rs1[...], row(0))).astype(BF16)

    @pl.when(sec == 1)
    def _():
        handed_back.start()
        grads_out()
        grads_fc()

    ex_first.wait_recv()
    ex_att.wait_recv()
    ex_dbr.wait_recv()
    ex_dmix.wait_recv()
    first_rows = x1[...].reshape(2 * ROWS, WIDTH)
    att_rows = x2[...].reshape(2 * ROWS, WIDTH)
    for other in (1, 0):
        xx = xside(other)
        left = lhs(s_proj[xx, :, :, c], t_proj[xx], 256)
        w[xx, :, :, c, 3] = jnp.dot(left, att_rows, preferred_element_type=F32).astype(BF16).reshape(4, 4, 16, WIDTH)

        def body(k, carry):
            zz = pl.ds(2 * k, 2)
            left = lhs(s_qkv[xx, zz, :, c], t_qkv[xx, zz], 384)
            w[xx, zz, :, c, 0:3] = (
                jnp.dot(left, first_rows, preferred_element_type=F32).astype(BF16).reshape(2, 4, 3, 16, WIDTH)
            )
            return carry

        lax.fori_loop(0, 2, body, 0)
        sums["B", other][0].start()

    for g in range(8):
        sr[g // 4, g % 4] = sbw[:, g * 128 : (g + 1) * 128]
    sm_core = small(8, sr, sr_c, sib)
    sm_core.start()

    def a_arrive(off):
        for part in ("A1", "A2"):
            x_sum(part, off).wait_recv()
            k = names.index(part) - 2
            add_into(line(part, x, lax.rem(outer_pos(part) + off, 4)), (ra_x.at[k, off],))

    sums["C", 1][0].mid()
    sums["C", 0][0].mid()
    a_arrive(2)
    sums["A1", 0][0].start()
    sums["A2", 0][0].start()
    sm_core.wait_recv()
    sm_core.wait_send()
    sr[...] = sr[...] + sr_c[...]
    sm_xs = small(9, sr.at[ox], sr_x, xp)
    sm_xs.start()
    sums["B", 1][0].mid()
    sums["B", 0][0].mid()
    a_arrive(1)
    a_arrive(3)
    sums["A1", 0][0].mid()
    sums["A2", 0][0].mid()
    sums["C", 1][0].end()
    sums["C", 1][1].start()
    sums["C", 0][0].end()
    sums["C", 0][1].start()
    sm_xs.wait_recv()
    sr[x] = sr[x] + sr_x[...]
    sm_zs = [small(9 + k, sr.at[x, lax.rem(z + k, 4)], sr_z.at[k - 1], zs[k]) for k in (1, 2, 3)]
    for cp in sm_zs:
        cp.start()
    sums["C", 1][1].mid()
    sums["C", 0][1].mid()
    sums["C", 1][1].end()
    x_last("C").start()
    sums["C", 0][1].end()
    for cp in sm_zs:
        cp.wait_recv()
    sr_y[0] = sr[x, z] + sr_z[0] + sr_z[1] + sr_z[2]
    sm_ys = [small(12 + k, sr_y.at[0], sr_y.at[k], ys[k]) for k in (1, 2, 3)]
    for cp in sm_ys:
        cp.start()
    sums["B", 1][0].end()
    sums["B", 1][1].start()
    sums["B", 0][0].end()
    sums["B", 0][1].start()
    a_arrive(0)
    sums["A1", 0][0].end()
    sums["A1", 0][1].start()
    sums["A2", 0][0].end()
    sums["A2", 0][1].start()
    sums["B", 1][1].mid()
    sums["B", 0][1].mid()
    sums["A1", 0][1].mid()
    sums["A2", 0][1].mid()
    sums["B", 1][1].end()
    x_last("B").start()
    sums["B", 0][1].end()
    for cp in sm_ys:
        cp.wait_recv()
    total = sr_y[0] + sr_y[1] + sr_y[2] + sr_y[3]
    picked = lax.dot_general(total, spread, NT, preferred_element_type=F32, precision=lax.Precision.HIGHEST)
    ggain_out[...] = picked[0:2, :]
    gbias_out[...] = picked[2:12, :]
    sums["A1", 0][1].end()
    sums["A2", 0][1].end()
    mine = w.at[x, z, y, c]
    for j in range(4):
        gwout_out[:, 1024 * j : 1024 * (j + 1)] = mine[8 + j].astype(F32)
    x_last("C").wait_recv()
    gfc_out[...] = mine[4:8].astype(F32) + rb_x[1].astype(F32)
    x_last("B").wait_recv()
    gqkv_out[...] = mine[0:3].astype(F32) + rb_x[0, 0:3].astype(F32)
    gproj_out[...] = mine[3:4].astype(F32) + rb_x[0, 3:4].astype(F32)

    for key in sums:
        sums[key][0].sent()
        sums[key][1].sent()
    for part in ("A1", "A2"):
        for off in range(4):
            x_sum(part, off).wait_send()
    for part in ("B", "C"):
        x_last(part).wait_send()
    for cp in [ex_first, ex_att, ex_second, ex_act, ex_gf, ex_dpre, ex_dbr, ex_dmix, sm_xs] + sm_zs + sm_ys:
        cp.wait_send()

    @pl.when(sec == 0)
    def _():
        handed_on.wait_send()

    @pl.when(sec == 1)
    def _():
        handed_back.wait_send()


def proj_back(w):
    return w[:, :, :, :, 3].reshape(WIDTH, WIDTH)


def local(tokens, segment_ids, gains, biases, w_qkv, w_proj, w_fc, w_out, cotangent):
    vmem = pl.BlockSpec(memory_space=pltpu.VMEM)
    hbm = pl.BlockSpec(memory_space=pl.ANY)

    def shape(*dims, dtype=F32):
        return jax.ShapeDtypeStruct(dims, dtype)

    def v(*dims, dtype=BF16):
        return pltpu.VMEM(dims, dtype)

    def dma(*dims):
        return pltpu.SemaphoreType.DMA(dims)

    scratch = [
        v(2, 4, 4, 2, 12, 16, WIDTH),
        v(4, 2, 4, 4, 16, WIDTH), v(4, 2, 2, 4, 16, WIDTH), v(4, 2, 4, 16, WIDTH), v(4, 2, 2, 16, WIDTH),
        v(2, 4, 16, WIDTH),
        v(2, 4, 4, 2, 16, WIDTH), v(2, 2, 4, 2, 16, WIDTH), v(2, 2, 2, 2, 16, WIDTH), v(2, 2, 2, 16, WIDTH),
        v(2, 2, 1, 16, WIDTH),
        v(ROWS, WIDTH, dtype=F32), v(2, ROWS, WIDTH), v(2, ROWS, WIDTH), v(2, ROWS, WIDTH), v(2, 4, ROWS, WIDTH),
        v(ROWS, 3 * WIDTH), v(16, ROWS, ROWS, dtype=F32), v(ROWS, WIDTH, dtype=F32), v(ROWS, WIDTH, dtype=F32),
        v(ROWS, 1, dtype=F32), v(ROWS, 1, dtype=F32), v(4, ROWS, WIDTH, dtype=F32), v(ROWS, WIDTH),
        v(4, ROWS, WIDTH), v(ROWS, WIDTH), v(ROWS, WIDTH), v(ROWS, 3 * WIDTH), v(ROWS, WIDTH, dtype=F32),
        v(ROWS, ROWS, dtype=F32), v(1, 3 * WIDTH, dtype=F32),
        v(16, WIDTH, dtype=F32), v(16, 16, dtype=F32), v(4, 16, 128, dtype=F32), v(2, 16, 128, dtype=F32),
        v(2, 4, 16, 128, dtype=F32), v(16, WIDTH, dtype=F32), v(2, 4, 16, 128, dtype=F32),
        v(2, 4, 16, 128, dtype=F32), v(4, 16, 128, dtype=F32), v(3, 16, 128, dtype=F32), v(4, 16, 128, dtype=F32),
        v(2, 4, 4, 2, 1, 16, ROWS), v(2, 4, 4, 2, 4, 16, ROWS), v(2, 4, 4, 2, 1, 16, ROWS), v(2, 4, 4, 2, 3, 16, ROWS),
        v(2, 4, 4, 1, 16, ROWS), v(2, 4, 4, 4, 16, ROWS), v(2, 4, 4, 1, 16, ROWS), v(2, 4, 4, 3, 16, ROWS),
        v(ROWS, WIDTH),
        dma(7), dma(8, 2, 4), dma(8, 2, 4), dma(10), dma(10), dma(4, 2, 4), dma(4, 2, 4),
        dma(8, 2, 4), dma(8, 2, 4), dma(10), dma(10), dma(8), dma(8), dma(16), dma(16),
        pltpu.SemaphoreType.DMA, pltpu.SemaphoreType.DMA,
    ]
    out = pl.pallas_call(
        kernel,
        out_shape=(
            shape(ROWS, WIDTH, dtype=BF16), shape(ROWS, WIDTH, dtype=BF16), shape(2, 16), shape(10, 16),
            shape(3, 16, WIDTH), shape(1, 16, WIDTH), shape(4, 16, WIDTH), shape(16, 4 * WIDTH),
        ),
        in_specs=[vmem, vmem, vmem, vmem, hbm, hbm, hbm, hbm, vmem],
        out_specs=(vmem,) * 8,
        scratch_shapes=scratch,
        compiler_params=pltpu.CompilerParams(
            collective_id=0, has_side_effects=True, vmem_limit_bytes=63 * 2**20
        ),
        name="relay",
    )(
        tokens,
        segment_ids.reshape(ROWS, 1),
        gains[0],
        biases[0],
        w_qkv[0].T.reshape(3, 16, WIDTH),
        w_proj[0].T.reshape(1, 16, WIDTH),
        w_fc[0].T.reshape(4, 16, WIDTH),
        w_out[0].T,
        cotangent,
    )
    activations, input_grads, g_gains, g_biases, g_qkv, g_proj, g_fc, g_out = out
    return (
        activations[None],
        input_grads[None],
        g_gains[None],
        g_biases[None],
        g_qkv.reshape(48, WIDTH).T[None],
        g_proj.reshape(16, WIDTH).T[None],
        g_fc.reshape(64, WIDTH).T[None],
        g_out.T[None],
    )


def solution(mesh):
    weight = P("section", None, "dp")
    rows = P("section", "dp", None)
    return jax.shard_map(
        local,
        mesh=mesh,
        in_specs=(P("dp", None), P("dp")) + (weight,) * 6 + (P("dp", None),),
        out_specs=(rows, rows) + (weight,) * 6,
        check_vma=False,
    )
```

```python
import jax
import jax.numpy as jnp
from jax import lax
from jax.experimental import pallas as pl
from jax.experimental.pallas import tpu as pltpu
from jax.sharding import PartitionSpec as P

MESH = pl.DeviceIdType.MESH
F32 = jnp.float32
BF16 = jnp.bfloat16
EPS = 1e-05
ROWS = 128
WIDTH = 1024
HEAD = 64
GC = 0.7978845608028654
NT = (((1,), (1,)), ((), ()))

PARTS = {"B": (0, 4), "C": (4, 4), "A1": (8, 2), "A2": (10, 2)}
INNER_IS_Y = {"B": False, "C": True, "A1": True, "A2": False}


def remote(src, dst, ssem, rsem, target):
    return pltpu.make_async_remote_copy(
        src_ref=src, dst_ref=dst, send_sem=ssem, recv_sem=rsem, device_id=target, device_id_type=MESH
    )


class Ring:
    def __init__(self, view, pos, left, right, ssem, rsem):
        self.view, self.pos, self.left, self.right = view, pos, left, right
        self.ssem, self.rsem = ssem, rsem

    def at(self, off):
        return lax.rem(self.pos + off, 4)

    def cp(self, off, half, slot, target):
        ref = self.view(self.at(off), half)
        return remote(ref, ref, self.ssem(slot), self.rsem(slot), target)

    def start(self):
        self.cp(0, None, 0, self.right).start()
        self.cp(0, None, 1, self.left).start()

    def mid(self):
        self.cp(3, None, 0, self.right).wait_recv()
        self.cp(3, 0, 2, self.right).start()
        self.cp(1, None, 1, self.left).wait_recv()
        self.cp(1, 1, 3, self.left).start()

    def end(self):
        self.cp(2, 0, 2, self.right).wait_recv()
        self.cp(2, 1, 3, self.left).wait_recv()

    def sent(self):
        self.cp(0, None, 0, self.right).wait_send()
        self.cp(0, None, 1, self.left).wait_send()
        self.cp(3, 0, 2, self.right).wait_send()
        self.cp(1, 1, 3, self.left).wait_send()


class SumRing:
    def __init__(self, view, pos, left, right, bufs, ssem, rsem, add):
        self.view, self.pos, self.left, self.right = view, pos, left, right
        self.half_l, self.half_r, self.full_l, self.full_r = bufs
        self.ssem, self.rsem, self.add = ssem, rsem, add

    def at(self, off):
        return lax.rem(self.pos + off, 4)

    def cp(self, k):
        off, half, buf, target = (
            (2, 0, self.half_l, self.right),
            (2, 1, self.half_r, self.left),
            (1, None, self.full_l, self.right),
            (3, None, self.full_r, self.left),
        )[k]
        return remote(self.view(self.at(off), half), buf, self.ssem(k), self.rsem(k), target)

    def start(self):
        self.cp(0).start()
        self.cp(1).start()

    def mid(self):
        self.cp(0).wait_recv()
        self.add(self.view(self.at(1), 0), (self.half_l,))
        self.cp(2).start()
        self.cp(1).wait_recv()
        self.add(self.view(self.at(3), 1), (self.half_r,))
        self.cp(3).start()

    def end(self):
        self.cp(2).wait_recv()
        self.cp(3).wait_recv()
        self.add(self.view(self.pos, None), (self.full_l, self.full_r))

    def sent(self):
        for k in range(4):
            self.cp(k).wait_send()


def add_into(view, terms):
    lead = view.shape[:-2]
    count = 1
    for size in lead:
        count *= size

    def body(step, carry):
        index, rest = [], step
        for size in reversed(lead):
            index.append(lax.rem(rest, size))
            rest = lax.div(rest, size)
        index = tuple(reversed(index))
        total = view[index].astype(F32)
        for term in terms:
            total = total + term[index].astype(F32)
        view[index] = total.astype(BF16)
        return carry

    lax.fori_loop(0, count, body, 0)


def kernel(
    tok_ref, seg_ref, gains_ref, bias_ref, qkv_ref, proj_ref, fc_ref, wout_ref, cot_ref,
    act_out, grad_out, ggain_out, gbias_out, gqkv_out, gproj_out, gfc_out, gwout_out,
    w, rb_outer, rb_half, rb_inner, rb_ihalf, rb_x, ra_x, ra_outer, ra_half, ra_inner, ra_ihalf,
    xin, x1, x2, x3, x4, qkv, probs, xh1, xh2, rs1, rs2, dgel, gf, dpre, dbr, datt, dmix, dmid, mask, qbias,
    bf, sgb, sb_y, sb_c, sb_x, sbw, sr, sr_c, sr_x, sr_z, sr_y,
    s_out, s_fc, s_proj, s_qkv, t_out, t_fc, t_proj, t_qkv, hb,
    loc_sem, ag_s, ag_r, agx_s, agx_r, sib_s, sib_r, rs_s, rs_r, rsx_s, rsx_r, ex_s, ex_r, sm_s, sm_r, sec_s, sec_r,
):
    sec = lax.axis_index("section")
    dp = lax.axis_index("dp")
    c = lax.rem(dp, 2)
    y = lax.rem(lax.div(dp, 2), 4)
    z = lax.rem(lax.div(dp, 8), 4)
    x = lax.div(dp, 32)
    ox, oc = 1 - x, 1 - c

    def at(px, pz, py, pc):
        return (sec, ((px * 4 + pz) * 4 + py) * 2 + pc)

    ys = [at(x, z, lax.rem(y + k, 4), c) for k in range(4)]
    zs = [at(x, lax.rem(z + k, 4), y, c) for k in range(4)]
    xp = at(ox, z, y, c)
    sib = at(x, z, y, oc)
    other_section = (1 - sec, dp)

    own = w.at[x, z, y, c]
    local = [
        pltpu.make_async_copy(qkv_ref, own.at[pl.ds(0, 3)], loc_sem.at[0]),
        pltpu.make_async_copy(proj_ref, own.at[pl.ds(3, 1)], loc_sem.at[1]),
        pltpu.make_async_copy(fc_ref, own.at[pl.ds(4, 4)], loc_sem.at[2]),
    ] + [
        pltpu.make_async_copy(wout_ref.at[:, pl.ds(1024 * j, 1024)], own.at[8 + j], loc_sem.at[3 + j]) for j in range(4)
    ]
    for cp in local:
        cp.start()
    barrier = pltpu.get_barrier_semaphore()
    partners = ys[1:] + zs[1:] + [xp, sib, other_section]
    for target in partners:
        pl.semaphore_signal(barrier, 1, device_id=target, device_id_type=MESH)
    pl.semaphore_wait(barrier, len(partners))
    for cp in local:
        cp.wait()

    def line(part, xx, o, half=None, core=None):
        base, size = PARTS[part]
        core = c if core is None else core
        inner = slice(None) if half is None else pl.ds(2 * half, 2)
        if INNER_IS_Y[part]:
            return w.at[xx, o, inner, core, pl.ds(base, size)]
        return w.at[xx, inner, o, core, pl.ds(base, size)]

    def single(part, xx, i, half=None):
        base, size = PARTS[part]
        if half is not None:
            size = size // 2
            base = base + half * size
        if INNER_IS_Y[part]:
            return w.at[xx, z, i, c, pl.ds(base, size)]
        return w.at[xx, i, y, c, pl.ds(base, size)]

    def axes(part):
        yy, zz = (y, ys[3], ys[1]), (z, zs[3], zs[1])
        return (yy, zz) if INNER_IS_Y[part] else (zz, yy)

    names = ("B", "C", "A1", "A2")

    def xside(other):
        return ox if other else x

    def gather_rings(part, other):
        inner, outer = axes(part)
        slot = names.index(part) * 2 + other
        xx = xside(other)
        first = Ring(lambda i, h: single(part, xx, i, h), *inner,
                     lambda k: ag_s.at[slot, 0, k], lambda k: ag_r.at[slot, 0, k])
        second = Ring(lambda o, h: line(part, xx, o, h), *outer,
                      lambda k: ag_s.at[slot, 1, k], lambda k: ag_r.at[slot, 1, k])
        return first, second

    rings = {(part, other): gather_rings(part, other) for part in ("B", "C") for other in (0, 1)}
    rings.update({(part, 0): gather_rings(part, 0) for part in ("A1", "A2")})

    def outer_pos(part):
        return z if INNER_IS_Y[part] else y

    def to_sibling(part, other, off, core=None):
        o = lax.rem(outer_pos(part) + off, 4)
        ref = line(part, xside(other), o, None, core)
        k = names.index(part)
        return remote(ref, ref, sib_s.at[k, other, off], sib_r.at[k, other, off], sib)

    def x_line(part, other, off):
        o = lax.rem(outer_pos(part) + off, 4)
        ref = line(part, xside(other), o)
        k = names.index(part) - 2
        return remote(ref, ref, agx_s.at[2 + k * 4 + off], agx_r.at[2 + k * 4 + off], xp)

    def x_single(part, other):
        k = names.index(part)
        ref = single(part, xside(other), z if not INNER_IS_Y[part] else y)
        return remote(ref, ref, agx_s.at[k], agx_r.at[k], xp)

    ring_a1, ring_a2 = rings["A1", 0], rings["A2", 0]
    x_single("B", 0).start()
    x_single("C", 0).start()
    ring_a1[0].start()
    ring_a2[0].start()
    rings["B", 0][0].start()
    rings["C", 0][0].start()

    sgb[...] = jnp.zeros_like(sgb)
    sgb[0:2, :] = gains_ref[...].astype(F32)
    sgb[2:12, :] = bias_ref[...].astype(F32)
    spread = (
        lax.broadcasted_iota(jnp.int32, (16, 128), 1)
        == lax.broadcasted_iota(jnp.int32, (16, 128), 0) + 16 * (y * 2 + c)
    ).astype(F32)
    sb_y[0] = jnp.dot(sgb[...].astype(BF16), spread.astype(BF16), preferred_element_type=F32)

    def small(slot, src, dst, target):
        return remote(src, dst, sm_s.at[slot], sm_r.at[slot], target)

    small_y = [small(k - 1, sb_y.at[0], sb_y.at[k], ys[k]) for k in (1, 2, 3)]
    for cp in small_y:
        cp.start()

    ring_a1[0].mid()
    ring_a2[0].mid()
    rings["B", 0][0].mid()
    rings["C", 0][0].mid()
    ring_a1[0].end()
    ring_a1[1].start()
    x_line("A1", 0, 0).start()
    ring_a2[0].end()
    ring_a2[1].start()
    x_line("A2", 0, 0).start()
    to_sibling("A1", 0, 0).start()
    to_sibling("A2", 0, 0).start()
    x_single("B", 1).wait_recv()
    rings["B", 1][0].start()
    x_single("C", 1).wait_recv()
    rings["C", 1][0].start()

    for cp in small_y:
        cp.wait_recv()
    sb_c[0] = sb_y[0] + sb_y[1] + sb_y[2] + sb_y[3]
    small_c = small(3, sb_c.at[0], sb_c.at[1], sib)
    small_c.start()

    for part in ("B", "C"):
        rings[part, 0][0].end()
        rings[part, 0][1].start()
        to_sibling(part, 0, 0).start()

    seg_col = jnp.broadcast_to(seg_ref[...].astype(F32), (ROWS, ROWS))
    qi = lax.broadcasted_iota(jnp.int32, (ROWS, ROWS), 0)
    ki = lax.broadcasted_iota(jnp.int32, (ROWS, ROWS), 1)
    allowed = (seg_col == seg_col.T) & (ki <= qi) & (lax.div(qi, 64) == lax.div(ki, 64))
    mask[...] = allowed.astype(F32)

    small_c.wait_recv()
    sb_x[x, z] = sb_c[0] + sb_c[1]
    small_z = [small(3 + k, sb_x.at[x, z], sb_x.at[x, z], zs[k]) for k in (1, 2, 3)]
    for cp in small_z:
        cp.start()

    def a_mid(part, ring):
        ring[1].mid()
        for off in (3, 1):
            x_line(part, 0, off).start()
            to_sibling(part, 0, off).start()

    a_mid("A1", ring_a1)
    a_mid("A2", ring_a2)
    rings["B", 1][0].mid()
    rings["C", 1][0].mid()
    for part in ("B", "C"):
        rings[part, 1][0].end()
        rings[part, 1][1].start()
        to_sibling(part, 1, 0).start()
    for part, ring in (("A1", ring_a1), ("A2", ring_a2)):
        ring[1].end()
        x_line(part, 0, 2).start()
        to_sibling(part, 0, 2).start()

    for k in (1, 2, 3):
        from_z = lax.rem(z + 4 - k, 4)
        small(3 + k, sb_x.at[x, from_z], sb_x.at[x, from_z], zs[k]).wait_recv()
    small_x = small(7, sb_x.at[x], sb_x.at[x], xp)
    small_x.start()

    def bulk_mid(part, other):
        rings[part, other][1].mid()
        for off in (3, 1):
            to_sibling(part, other, off).start()

    def bulk_end(part, other):
        rings[part, other][1].end()
        to_sibling(part, other, 2).start()

    bulk_mid("B", 0)
    bulk_mid("C", 0)
    small(7, sb_x.at[ox], sb_x.at[ox], xp).wait_recv()
    for g in range(8):
        bf[:, g * 128 : (g + 1) * 128] = sb_x[g // 4, g % 4]
    qbias[:, 0:WIDTH] = bf[3:4, :]
    qbias[:, WIDTH : 2 * WIDTH] = jnp.zeros((1, WIDTH), F32)
    qbias[:, 2 * WIDTH :] = bf[4:5, :]

    def row(k):
        return bf[k : k + 1, :]

    bulk_end("B", 0)
    bulk_mid("B", 1)
    bulk_end("C", 0)
    bulk_mid("C", 1)

    def a_pass_on(off):
        for part in ("A1", "A2"):
            x_line(part, 1, off).wait_recv()
            to_sibling(part, 1, off).start()

    a_pass_on(0)
    bulk_end("B", 1)
    bulk_end("C", 1)

    def from_sibling(part):
        for other in (0, 1):
            for off in (0, 3, 1, 2):
                to_sibling(part, other, off, oc).wait_recv()

    handed_on = remote(act_out, hb, sec_s, sec_r, other_section)
    handed_back = remote(grad_out, hb, sec_s, sec_r, other_section)

    @pl.when(sec == 0)
    def _():
        xin[...] = tok_ref[...].astype(F32)

    @pl.when(sec == 1)
    def _():
        handed_on.wait_recv()
        xin[...] = hb[...].astype(F32)

    def norm(values, gain, shift):
        centre = values - jnp.mean(values, axis=-1, keepdims=True)
        rs = lax.rsqrt(jnp.mean(centre * centre, axis=-1, keepdims=True) + EPS)
        hat = centre * rs
        return hat, rs, (hat * gain + shift).astype(BF16)

    def exchange(slot, src, dst):
        return remote(src, dst, ex_s.at[slot], ex_r.at[slot], sib)

    xh1[...], rs1[...], x1[0] = norm(xin[...], row(0), row(2))
    ex_first = exchange(0, x1.at[0], x1.at[1])
    ex_first.start()
    from_sibling("B")

    def qkv_weights(k):
        return w[k, :, :, :, 0:3].reshape(1536, WIDTH)

    for k in range(2):
        cols = slice(1536 * k, 1536 * (k + 1))
        mixed = lax.dot_general(x1[0], qkv_weights(k), NT, preferred_element_type=F32)
        qkv[:, cols] = (mixed + qbias[:, cols]).astype(BF16)

    low_lanes = lax.broadcasted_iota(jnp.int32, (ROWS, 128), 1) < HEAD
    zero = jnp.zeros((ROWS, 128), BF16)

    def pair(base, hp):
        return slice(base + hp * 128, base + hp * 128 + 128)

    def lanes_of(e):
        return low_lanes if e == 0 else ~low_lanes

    raw = []
    for hp in range(8):
        q, k = qkv[:, pair(0, hp)], qkv[:, pair(WIDTH, hp)]
        for e in range(2):
            raw.append(lax.dot_general(jnp.where(lanes_of(e), q, zero), k, NT, preferred_element_type=F32))
    seen = mask[...] > 0.5
    soft = []
    for scores in raw:
        scores = jnp.where(seen, scores * 0.125, -1e30)
        ex = jnp.exp(scores - jnp.max(scores, axis=-1, keepdims=True))
        soft.append(ex * (1.0 / jnp.sum(ex, axis=-1, keepdims=True)))
    for hp in range(8):
        v = qkv[:, pair(2 * WIDTH, hp)]
        parts = []
        for e in range(2):
            probs[2 * hp + e] = soft[2 * hp + e]
            parts.append(jnp.dot(soft[2 * hp + e].astype(BF16), v, preferred_element_type=F32))
        x2[0, :, pair(0, hp)] = jnp.where(low_lanes, parts[0], parts[1]).astype(BF16)
    ex_att = exchange(1, x2.at[0], x2.at[1])
    ex_att.start()

    a_pass_on(3)
    proj_w = w[:, :, :, :, 3].reshape(WIDTH, WIDTH)
    xin[...] = xin[...] + (lax.dot_general(x2[0], proj_w, NT, preferred_element_type=F32) + row(5))
    xh2[...], rs2[...], x3[0] = norm(xin[...], row(1), row(6))
    ex_second = exchange(2, x3.at[0], x3.at[1])
    ex_second.start()
    from_sibling("C")
    a_pass_on(1)

    def fc_weights(j):
        return w[j // 2, 2 * (j % 2) : 2 * (j % 2) + 2, :, :, 4:8].reshape(WIDTH, WIDTH)

    for j in range(4):
        pre = lax.dot_general(x3[0], fc_weights(j), NT, preferred_element_type=F32) + row(7 + j)
        square = pre * pre
        t = jnp.tanh(GC * (pre + 0.044715 * (square * pre)))
        half = 0.5 * (1.0 + t)
        x4[0, j] = (pre * half).astype(BF16)
        dgel[j] = half + (0.5 * GC) * pre * (1.0 - t * t) * (1.0 + 0.134145 * square)
    ex_act = exchange(3, x4.at[0], x4.at[1])
    ex_act.start()
    a_pass_on(2)
    from_sibling("A1")
    from_sibling("A2")

    def wout_weights(j):
        return w[:, :, :, :, 8 + j].reshape(WIDTH, WIDTH)

    result = xin[...] + row(11)
    for j in range(4):
        result = result + lax.dot_general(x4[0, j], wout_weights(j), NT, preferred_element_type=F32)
    act_out[...] = result.astype(BF16)

    @pl.when(sec == 0)
    def _():
        handed_on.start()

    for key in rings:
        rings[key][0].sent()
        rings[key][1].sent()
    for part in ("B", "C"):
        x_single(part, 0).wait_send()
    for part in names:
        for other in (0, 1):
            for off in range(4):
                to_sibling(part, other, off).wait_send()
                if part in ("A1", "A2") and other == 0:
                    x_line(part, 0, off).wait_send()
    for cp in small_y + [small_c] + small_z + [small_x]:
        cp.wait_send()

    sbw[...] = jnp.zeros_like(sbw)

    @pl.when(sec == 0)
    def _():
        handed_back.wait_recv()
        gf[...] = hb[...]

    @pl.when(sec == 1)
    def _():
        gf[...] = cot_ref[...]

    def column_sum(values):
        return jnp.sum(values.astype(F32), axis=0, keepdims=True)

    sbw[11:12, :] = column_sum(gf[...])
    s_out[...] = gf[...].T.reshape(2, 4, 4, 2, 1, 16, ROWS)

    def swap(slot, src, dst):
        return exchange(slot, src.at[:, :, :, oc], dst)

    ex_gf = swap(4, s_out, t_out)
    ex_gf.start()

    for j in range(4):
        d_act = jnp.dot(gf[...], wout_weights(j), preferred_element_type=F32)
        d_pre = (dgel[j] * d_act).astype(BF16)
        dpre[j] = d_pre
        sbw[7 + j : 8 + j, :] = column_sum(d_pre)
        s_fc[j // 2, 2 * (j % 2) : 2 * (j % 2) + 2] = d_pre.T.reshape(2, 4, 2, 4, 16, ROWS)
    ex_dpre = swap(5, s_fc, t_fc)
    ex_dpre.start()

    def lhs(mine, theirs, rows):
        return jnp.concatenate([mine.reshape(rows, ROWS), theirs.reshape(rows, ROWS)], axis=1)

    def sum_rings(part, other):
        inner, outer = axes(part)
        slot = names.index(part) * 2 + other
        xx = xside(other)
        if part in ("B", "C"):
            k = names.index(part) * 2 + other
            ibufs = (rb_ihalf.at[k, 0], rb_ihalf.at[k, 1], rb_inner.at[k, 0], rb_inner.at[k, 1])
            obufs = (rb_half.at[k, 0], rb_half.at[k, 1], rb_outer.at[k, 0], rb_outer.at[k, 1])
        else:
            k = names.index(part) - 2
            ibufs = (ra_ihalf.at[k, 0], ra_ihalf.at[k, 1], ra_inner.at[k, 0], ra_inner.at[k, 1])
            obufs = (ra_half.at[k, 0], ra_half.at[k, 1], ra_outer.at[k, 0], ra_outer.at[k, 1])
        first = SumRing(lambda o, h: line(part, xx, o, h), *outer, obufs,
                        lambda k: rs_s.at[slot, 0, k], lambda k: rs_r.at[slot, 0, k], add_into)
        second = SumRing(lambda i, h: single(part, xx, i, h), *inner, ibufs,
                         lambda k: rs_s.at[slot, 1, k], lambda k: rs_r.at[slot, 1, k], add_into)
        return first, second

    sums = {(part, other): sum_rings(part, other) for part in ("B", "C") for other in (0, 1)}
    sums.update({(part, 0): sum_rings(part, 0) for part in ("A1", "A2")})

    def x_sum(part, off):
        k = names.index(part) - 2
        o = lax.rem(outer_pos(part) + off, 4)
        return remote(line(part, ox, o), ra_x.at[k, off], rsx_s.at[2 + k * 4 + off], rsx_r.at[2 + k * 4 + off], xp)

    def x_last(part):
        k = names.index(part)
        return remote(single(part, ox, y if INNER_IS_Y[part] else z), rb_x.at[k], rsx_s.at[k], rsx_r.at[k], xp)

    def grads_out():
        ex_gf.wait_recv()
        ex_act.wait_recv()
        for other in (1, 0):
            xx = xside(other)
            left = lhs(s_out[xx, :, :, c], t_out[xx], 256)

            for j in range(4):
                right = x4[:, j].reshape(2 * ROWS, WIDTH)
                w[xx, :, :, c, 8 + j] = (
                    jnp.dot(left, right, preferred_element_type=F32).astype(BF16).reshape(4, 4, 16, WIDTH)
                )
            if other:
                for off in (2, 1, 3, 0):
                    for part in ("A1", "A2"):
                        x_sum(part, off).start()

    def grads_fc():
        ex_dpre.wait_recv()
        ex_second.wait_recv()
        right = x3[...].reshape(2 * ROWS, WIDTH)
        for other in (1, 0):
            xx = xside(other)

            for k in range(2):
                zz = slice(2 * k, 2 * k + 2)
                left = lhs(s_fc[xx, zz, :, c], t_fc[xx, zz], 512)
                w[xx, zz, :, c, 4:8] = (
                    jnp.dot(left, right, preferred_element_type=F32).astype(BF16).reshape(2, 4, 4, 16, WIDTH)
                )
            sums["C", other][0].start()

    @pl.when(sec == 0)
    def _():
        grads_out()

    d_second = jnp.zeros((ROWS, WIDTH), F32)
    for j in range(4):
        d_second = d_second + jnp.dot(dpre[j], fc_weights(j), preferred_element_type=F32)

    def norm_back(d_out, hat, rs, gain):
        d_hat = d_out * gain
        mean_one = jnp.mean(d_hat, axis=-1, keepdims=True)
        mean_two = jnp.mean(d_hat * hat, axis=-1, keepdims=True)
        return rs * (d_hat - mean_one - hat * mean_two)

    sbw[1:2, :] = column_sum(d_second * xh2[...])
    sbw[6:7, :] = column_sum(d_second)
    dmid[...] = gf[...].astype(F32) + norm_back(d_second, xh2[...], rs2[...], row(1))
    dbr[...] = dmid[...].astype(BF16)
    sbw[5:6, :] = column_sum(dbr[...])
    s_proj[...] = dbr[...].T.reshape(2, 4, 4, 2, 1, 16, ROWS)
    ex_dbr = swap(6, s_proj, t_proj)
    ex_dbr.start()

    @pl.when(sec == 0)
    def _():
        grads_fc()

    datt[...] = jnp.dot(dbr[...], proj_back(w), preferred_element_type=F32).astype(BF16)

    d_probs, masked_da = [], []
    for hp in range(8):
        da, v = datt[:, pair(0, hp)], qkv[:, pair(2 * WIDTH, hp)]
        for e in range(2):
            masked_da.append(jnp.where(lanes_of(e), da, zero))
            d_probs.append(lax.dot_general(masked_da[-1], v, NT, preferred_element_type=F32))
    d_scores = []
    for h in range(16):
        p, dp_ = probs[h], d_probs[h]
        d_scores.append((p * (dp_ - jnp.sum(dp_ * p, axis=-1, keepdims=True))).astype(BF16))
    for hp in range(8):
        q, k = qkv[:, pair(0, hp)], qkv[:, pair(WIDTH, hp)]
        dq, dk, dv = [], [], []
        for e in range(2):
            h = 2 * hp + e
            dv.append(jnp.dot(probs[h].astype(BF16).T, masked_da[h], preferred_element_type=F32))
            dq.append(jnp.dot(d_scores[h], k, preferred_element_type=F32))
            dk.append(jnp.dot(d_scores[h].T, jnp.where(lanes_of(e), q, zero), preferred_element_type=F32))
        dmix[:, pair(0, hp)] = (jnp.where(low_lanes, dq[0], dq[1]) * 0.125).astype(BF16)
        dmix[:, pair(WIDTH, hp)] = ((dk[0] + dk[1]) * 0.125).astype(BF16)
        dmix[:, pair(2 * WIDTH, hp)] = (dv[0] + dv[1]).astype(BF16)
    for k in range(2):
        s_qkv[k] = dmix[:, 1536 * k : 1536 * (k + 1)].T.reshape(4, 4, 2, 3, 16, ROWS)
    ex_dmix = swap(7, s_qkv, t_qkv)
    ex_dmix.start()
    sbw[3:4, :] = column_sum(dmix[:, 0:WIDTH])
    sbw[4:5, :] = column_sum(dmix[:, 2 * WIDTH :])
    d_first = jnp.dot(dmix[:, 0:1536], qkv_weights(0), preferred_element_type=F32)
    d_first = d_first + jnp.dot(dmix[:, 1536:], qkv_weights(1), preferred_element_type=F32)
    sbw[0:1, :] = column_sum(d_first * xh1[...])
    sbw[2:3, :] = column_sum(d_first)
    grad_out[...] = (dmid[...] + norm_back(d_first, xh1[...], rs1[...], row(0))).astype(BF16)

    @pl.when(sec == 1)
    def _():
        handed_back.start()
        grads_out()
        grads_fc()

    ex_first.wait_recv()
    ex_att.wait_recv()
    ex_dbr.wait_recv()
    ex_dmix.wait_recv()
    first_rows = x1[...].reshape(2 * ROWS, WIDTH)
    att_rows = x2[...].reshape(2 * ROWS, WIDTH)
    for other in (1, 0):
        xx = xside(other)
        left = lhs(s_proj[xx, :, :, c], t_proj[xx], 256)
        w[xx, :, :, c, 3] = jnp.dot(left, att_rows, preferred_element_type=F32).astype(BF16).reshape(4, 4, 16, WIDTH)

        for k in range(2):
            zz = slice(2 * k, 2 * k + 2)
            left = lhs(s_qkv[xx, zz, :, c], t_qkv[xx, zz], 384)
            w[xx, zz, :, c, 0:3] = (
                jnp.dot(left, first_rows, preferred_element_type=F32).astype(BF16).reshape(2, 4, 3, 16, WIDTH)
            )
        sums["B", other][0].start()

    for g in range(8):
        sr[g // 4, g % 4] = sbw[:, g * 128 : (g + 1) * 128]
    sm_core = small(8, sr, sr_c, sib)
    sm_core.start()

    def a_arrive(off):
        for part in ("A1", "A2"):
            x_sum(part, off).wait_recv()
            k = names.index(part) - 2
            add_into(line(part, x, lax.rem(outer_pos(part) + off, 4)), (ra_x.at[k, off],))

    sums["C", 1][0].mid()
    sums["C", 0][0].mid()
    a_arrive(2)
    sums["A1", 0][0].start()
    sums["A2", 0][0].start()
    sm_core.wait_recv()
    sm_core.wait_send()
    sr[...] = sr[...] + sr_c[...]
    sm_xs = small(9, sr.at[ox], sr_x, xp)
    sm_xs.start()
    sums["B", 1][0].mid()
    sums["B", 0][0].mid()
    a_arrive(1)
    a_arrive(3)
    sums["A1", 0][0].mid()
    sums["A2", 0][0].mid()
    sums["C", 1][0].end()
    sums["C", 1][1].start()
    sums["C", 0][0].end()
    sums["C", 0][1].start()
    sm_xs.wait_recv()
    sr[x] = sr[x] + sr_x[...]
    sm_zs = [small(9 + k, sr.at[x, lax.rem(z + k, 4)], sr_z.at[k - 1], zs[k]) for k in (1, 2, 3)]
    for cp in sm_zs:
        cp.start()
    sums["C", 1][1].mid()
    sums["C", 0][1].mid()
    sums["C", 1][1].end()
    x_last("C").start()
    sums["C", 0][1].end()
    for cp in sm_zs:
        cp.wait_recv()
    sr_y[0] = sr[x, z] + sr_z[0] + sr_z[1] + sr_z[2]
    sm_ys = [small(12 + k, sr_y.at[0], sr_y.at[k], ys[k]) for k in (1, 2, 3)]
    for cp in sm_ys:
        cp.start()
    sums["B", 1][0].end()
    sums["B", 1][1].start()
    sums["B", 0][0].end()
    sums["B", 0][1].start()
    a_arrive(0)
    sums["A1", 0][0].end()
    sums["A1", 0][1].start()
    sums["A2", 0][0].end()
    sums["A2", 0][1].start()
    sums["B", 1][1].mid()
    sums["B", 0][1].mid()
    sums["A1", 0][1].mid()
    sums["A2", 0][1].mid()
    sums["B", 1][1].end()
    x_last("B").start()
    sums["B", 0][1].end()
    for cp in sm_ys:
        cp.wait_recv()
    total = sr_y[0] + sr_y[1] + sr_y[2] + sr_y[3]
    picked = lax.dot_general(total, spread, NT, preferred_element_type=F32, precision=lax.Precision.HIGHEST)
    ggain_out[...] = picked[0:2, :]
    gbias_out[...] = picked[2:12, :]
    sums["A1", 0][1].end()
    sums["A2", 0][1].end()
    mine = w.at[x, z, y, c]
    for j in range(4):
        gwout_out[:, 1024 * j : 1024 * (j + 1)] = mine[8 + j].astype(F32)
    x_last("C").wait_recv()
    gfc_out[...] = mine[4:8].astype(F32) + rb_x[1].astype(F32)
    x_last("B").wait_recv()
    gqkv_out[...] = mine[0:3].astype(F32) + rb_x[0, 0:3].astype(F32)
    gproj_out[...] = mine[3:4].astype(F32) + rb_x[0, 3:4].astype(F32)

    for key in sums:
        sums[key][0].sent()
        sums[key][1].sent()
    for part in ("A1", "A2"):
        for off in range(4):
            x_sum(part, off).wait_send()
    for part in ("B", "C"):
        x_last(part).wait_send()
    for cp in [ex_first, ex_att, ex_second, ex_act, ex_gf, ex_dpre, ex_dbr, ex_dmix, sm_xs] + sm_zs + sm_ys:
        cp.wait_send()

    @pl.when(sec == 0)
    def _():
        handed_on.wait_send()

    @pl.when(sec == 1)
    def _():
        handed_back.wait_send()


def proj_back(w):
    return w[:, :, :, :, 3].reshape(WIDTH, WIDTH)


def local(tokens, segment_ids, gains, biases, w_qkv, w_proj, w_fc, w_out, cotangent):
    vmem = pl.BlockSpec(memory_space=pltpu.VMEM)
    hbm = pl.BlockSpec(memory_space=pl.ANY)

    def shape(*dims, dtype=F32):
        return jax.ShapeDtypeStruct(dims, dtype)

    def v(*dims, dtype=BF16):
        return pltpu.VMEM(dims, dtype)

    def dma(*dims):
        return pltpu.SemaphoreType.DMA(dims)

    scratch = [
        v(2, 4, 4, 2, 12, 16, WIDTH),
        v(4, 2, 4, 4, 16, WIDTH), v(4, 2, 2, 4, 16, WIDTH), v(4, 2, 4, 16, WIDTH), v(4, 2, 2, 16, WIDTH),
        v(2, 4, 16, WIDTH),
        v(2, 4, 4, 2, 16, WIDTH), v(2, 2, 4, 2, 16, WIDTH), v(2, 2, 2, 2, 16, WIDTH), v(2, 2, 2, 16, WIDTH),
        v(2, 2, 1, 16, WIDTH),
        v(ROWS, WIDTH, dtype=F32), v(2, ROWS, WIDTH), v(2, ROWS, WIDTH), v(2, ROWS, WIDTH), v(2, 4, ROWS, WIDTH),
        v(ROWS, 3 * WIDTH), v(16, ROWS, ROWS, dtype=F32), v(ROWS, WIDTH, dtype=F32), v(ROWS, WIDTH, dtype=F32),
        v(ROWS, 1, dtype=F32), v(ROWS, 1, dtype=F32), v(4, ROWS, WIDTH, dtype=F32), v(ROWS, WIDTH),
        v(4, ROWS, WIDTH), v(ROWS, WIDTH), v(ROWS, WIDTH), v(ROWS, 3 * WIDTH), v(ROWS, WIDTH, dtype=F32),
        v(ROWS, ROWS, dtype=F32), v(1, 3 * WIDTH, dtype=F32),
        v(16, WIDTH, dtype=F32), v(16, 16, dtype=F32), v(4, 16, 128, dtype=F32), v(2, 16, 128, dtype=F32),
        v(2, 4, 16, 128, dtype=F32), v(16, WIDTH, dtype=F32), v(2, 4, 16, 128, dtype=F32),
        v(2, 4, 16, 128, dtype=F32), v(4, 16, 128, dtype=F32), v(3, 16, 128, dtype=F32), v(4, 16, 128, dtype=F32),
        v(2, 4, 4, 2, 1, 16, ROWS), v(2, 4, 4, 2, 4, 16, ROWS), v(2, 4, 4, 2, 1, 16, ROWS), v(2, 4, 4, 2, 3, 16, ROWS),
        v(2, 4, 4, 1, 16, ROWS), v(2, 4, 4, 4, 16, ROWS), v(2, 4, 4, 1, 16, ROWS), v(2, 4, 4, 3, 16, ROWS),
        v(ROWS, WIDTH),
        dma(7), dma(8, 2, 4), dma(8, 2, 4), dma(10), dma(10), dma(4, 2, 4), dma(4, 2, 4),
        dma(8, 2, 4), dma(8, 2, 4), dma(10), dma(10), dma(8), dma(8), dma(16), dma(16),
        pltpu.SemaphoreType.DMA, pltpu.SemaphoreType.DMA,
    ]
    out = pl.pallas_call(
        kernel,
        out_shape=(
            shape(ROWS, WIDTH, dtype=BF16), shape(ROWS, WIDTH, dtype=BF16), shape(2, 16), shape(10, 16),
            shape(3, 16, WIDTH), shape(1, 16, WIDTH), shape(4, 16, WIDTH), shape(16, 4 * WIDTH),
        ),
        in_specs=[vmem, vmem, vmem, vmem, hbm, hbm, hbm, hbm, vmem],
        out_specs=(vmem,) * 8,
        scratch_shapes=scratch,
        compiler_params=pltpu.CompilerParams(
            collective_id=0, has_side_effects=True, vmem_limit_bytes=63 * 2**20
        ),
        name="relay",
    )(
        tokens,
        segment_ids.reshape(ROWS, 1),
        gains[0],
        biases[0],
        w_qkv[0].T.reshape(3, 16, WIDTH),
        w_proj[0].T.reshape(1, 16, WIDTH),
        w_fc[0].T.reshape(4, 16, WIDTH),
        w_out[0].T,
        cotangent,
    )
    activations, input_grads, g_gains, g_biases, g_qkv, g_proj, g_fc, g_out = out
    return (
        activations[None],
        input_grads[None],
        g_gains[None],
        g_biases[None],
        g_qkv.reshape(48, WIDTH).T[None],
        g_proj.reshape(16, WIDTH).T[None],
        g_fc.reshape(64, WIDTH).T[None],
        g_out.T[None],
    )


def solution(mesh):
    weight = P("section", None, "dp")
    rows = P("section", "dp", None)
    return jax.shard_map(
        local,
        mesh=mesh,
        in_specs=(P("dp", None), P("dp")) + (weight,) * 6 + (P("dp", None),),
        out_specs=(rows, rows) + (weight,) * 6,
        check_vma=False,
    )
```

```python
import jax
import jax.numpy as jnp
from jax import lax
from jax.experimental import pallas as pl
from jax.experimental.pallas import tpu as pltpu
from jax.sharding import PartitionSpec as P

MESH = pl.DeviceIdType.MESH
F32 = jnp.float32
BF16 = jnp.bfloat16
EPS = 1e-05
ROWS = 128
WIDTH = 1024
HEAD = 64
GC = 0.7978845608028654
NT = (((1,), (1,)), ((), ()))

PARTS = ("Be", "Ce", "A1", "A2", "Bl", "Cl")
FIRST = {"Be": 0, "Ce": 2, "A1": 4, "A2": 6, "Bl": 8, "Cl": 10}
INNER_IS_Y = {"Be": False, "Ce": True, "A1": True, "A2": False, "Bl": False, "Cl": True}
X_FIRST = {"Be": True, "Ce": True, "A1": False, "A2": False, "Bl": True, "Cl": True}
GROUPS = ((0, (0,)), (1, (0,)), (0, (1, 3)), (0, (2,)), (1, (1, 3)), (1, (2,)))
STAGES = ((0,), (1, 3), (2,))
SUM_AT = {"Be": (0, 4), "Ce": (0, 6), "A1": (0, 8), "A2": (0, 10), "Bl": (1, 8), "Cl": (1, 10)}

GATHER_ONE = [
    "Be.x.s", "A2.in0.start", "Ce.x.s", "A1.in0.start", "A1.g0.start", "Bl.in0.start", "Ce.in0.start", "Cl.in0.start",
    "A1.X.0.0", "A2.in0.mid", "Be.x.r", "A1.in0.mid", "A2.g0.start", "Ce.g0.start", "small.1", "Bl.x.s", "Ce.x.r",
    "A2.X.2.0", "Be.g0.start", "Cl.x.s", "A2.X.0.0", "A2.g2.start", "Ce.in0.mid", "A1.X.2.0", "Be.in0.start",
    "A1.in0.end", "A1.g0.mid", "A1.g3.start", "Bl.in0.mid", "Cl.g0.start", "Be.in0.mid", "A1.X.3.0", "Be.g2.start",
    "Cl.x.r", "Cl.in0.mid", "Cl.g2.start", "A2.in0.end", "A2.X.3.0", "Be.in1.start", "A2.g3.start", "Ce.in1.start",
    "Cl.in1.start", "A1.X.0.1", "Bl.in0.end", "A2.g2.mid", "Cl.g0.mid", "A1.sib.0.0", "A1.g3.mid", "Ce.g1.start",
    "Bl.x.r", "Bl.in1.start", "A2.g0.mid", "Be.g2.mid", "Cl.in0.end", "Cl.sib.0.0", "Be.in1.mid", "A2.X.2.1",
    "Ce.in0.end", "Be.in0.end", "Be.g3.start", "small.2", "A1.g2.start", "A2.g3.mid", "A2.X.3.1", "Ce.g2.start",
    "Be.g0.mid", "A2.X.0.1", "Be.g1.start", "A2.g2.end", "A2.g0.end", "Ce.sib.0.0", "Cl.g3.start", "A2.sib.0.1",
    "Ce.in1.mid", "Be.g4.start", "A2.g3.end", "Cl.g2.mid", "Bl.g0.start", "A2.sib.0.2", "Be.g3.mid", "Bl.in1.mid",
    "A2.sib.0.0", "Be.in1.end", "Bl.sib.0.0", "A2.XR.0", "Ce.g2.mid", "Cl.in1.mid", "A1.X.3.1", "Be.sib.0.1",
    "Be.sib.0.0", "A2.X.2.2", "small.3", "Ce.g3.start", "A1.g2.mid", "Ce.in1.end", "Ce.g0.mid", "A2.sib.1.0",
    "Ce.g5.start", "Cl.g3.mid", "A1.sib.0.1", "Cl.sib.0.1", "A1.X.2.1", "A2.X.3.2", "Be.g4.mid", "A2.XR.1",
    "A1.g3.end", "Be.g5.start", "Ce.g1.mid", "Bl.in1.end", "Bl.g5.start", "Ce.g3.mid", "Cl.g2.end", "Bl.g1.start",
    "A1.XR.0", "Ce.sib.1.0", "Cl.g0.end", "Ce.g4.start", "Be.g4.end", "A1.X.3.2", "Be.sib.1.0", "Be.g2.end",
    "Bl.g0.mid", "small.4", "A1.g0.end", "Cl.in1.end", "A2.sib.1.1", "A2.X.0.2", "Bl.g2.start", "Ce.g2.end",
    "Be.g0.end", "Be.g5.mid", "A1.X.0.2", "A1.g2.end", "Be.g1.mid", "Ce.sib.0.1", "Ce.g5.mid", "Cl.g5.start",
    "Cl.sib.1.0", "Bl.sib.1.0", "Ce.g3.end", "Be.sib.1.1", "A1.sib.0.2", "Be.g3.end", "Ce.g0.end", "Cl.g3.end",
    "Ce.sib.0.2", "Bl.g3.start", "Cl.sib.0.2", "Ce.g4.mid", "Ce.sib.1.1", "Bl.g4.start", "A1.XR.1", "Ce.g5.end",
    "small.5", "Cl.g4.start", "Be.g5.end", "A1.X.2.2", "Ce.g1.end", "Bl.g2.mid", "Bl.g1.mid", "Be.g1.end",
    "Bl.g0.end", "A1.sib.1.1", "Be.sib.0.2", "A1.sib.1.0", "Ce.g4.end", "Ce.sib.1.2", "Bl.g3.mid", "Cl.g1.start",
    "Bl.g5.mid", "Be.sib.1.2", "A2.XR.2", "A2.sib.1.2", "Cl.g4.mid", "Bl.sib.0.1", "Bl.g4.mid", "Bl.sib.1.1",
    "Cl.g5.mid", "Bl.g2.end", "Cl.g1.mid", "Bl.g1.end", "Cl.sib.1.1", "A1.XR.2", "A1.sib.1.2", "small.6",
]

GATHER_TWO = [
    "Cl.g4.end", "Bl.g3.end", "Cl.g1.end", "Cl.g5.end", "Cl.sib.1.2", "Bl.g5.end", "Bl.g4.end", "Bl.sib.1.2",
    "Bl.sib.0.2",
]

SUM_ONE = [
    "comp.gout1", "Cl.g5.start", "Bl.g1.start", "comp.gout0", "Bl.g5.start", "Cl.g2.start", "Bl.g4.start",
    "comp.gfc1", "A2.X.2", "Cl.g4.start", "Bl.g2.start", "Bl.g5.mid", "Bl.g3.start", "Cl.g3.start", "A1.X.2",
    "Cl.g1.start", "Bl.g1.mid", "Bl.g4.mid", "Cl.g0.start", "Cl.g2.mid",
]

SUM_TWO = [
    "Bl.g0.start", "Cl.g0.mid", "Bl.g2.mid", "Cl.g3.mid", "Cl.g4.mid",
]

SUM_THREE = [
    "A2.X.1", "Bl.g3.mid", "Cl.g3.end", "Cl.g5.mid", "Bl.g1.end", "Cl.g2.end", "Bl.g0.mid", "Bl.g4.end",
    "Cl.in0.start", "Cl.g1.mid", "comp.gatt1", "Ce.g5.start", "comp.gatt0", "Be.g5.start", "Ce.g1.start",
    "Be.g1.start", "Bl.g5.end", "Be.g2.start", "Ce.g3.start", "Cl.g5.end", "Be.g3.start", "Ce.g4.start",
    "Be.g4.start", "Ce.g0.start", "Ce.g5.mid", "Be.g0.start", "comp.gfc0", "Ce.g1.mid", "Bl.g2.end", "A2.XR.2",
    "A1.X.1", "A2.X.0", "Be.g5.mid", "Be.g3.mid", "Ce.g3.mid", "Be.g4.mid", "Cl.g4.end", "Be.g1.mid", "Ce.g4.mid",
    "Ce.g2.start", "Bl.g3.end", "comp.first", "small.7", "A2.g3.start", "Ce.g5.end", "Ce.g3.end", "Cl.g0.end",
    "Bl.in1.start", "Bl.in0.start", "Ce.g0.mid", "Be.g5.end", "Cl.in1.start", "A2.g2.start", "A2.XR.1", "Cl.g1.end",
    "A1.XR.2", "Bl.g0.end", "Ce.in1.start", "small.8", "Ce.g4.end", "A2.g0.start", "A1.g0.start", "A1.g2.start",
    "Ce.g2.mid", "Be.g2.mid", "Ce.in1.mid", "Be.g4.end", "A2.g3.mid", "Be.g3.end", "Ce.in0.start", "Cl.in0.mid",
    "Be.in1.start", "Ce.g1.end", "Be.in0.start", "A1.XR.1", "small.9", "Bl.in0.mid", "A1.X.0", "Bl.in1.mid",
    "A1.g3.start", "Cl.in1.mid", "Be.g0.mid", "A1.g2.mid", "Be.g1.end", "Ce.g2.end", "A2.g2.mid", "Be.g2.end",
    "A1.g3.mid", "A2.XR.0", "Bl.in0.end", "Cl.in0.end", "Ce.in1.end", "small.10", "Ce.in0.mid", "Ce.g0.end",
    "A2.g3.end", "Cl.in1.end", "A2.in0.start", "Be.in1.mid", "Be.in0.mid", "Ce.x.s", "Cl.x.s", "A1.XR.0", "A1.g3.end",
    "A1.in0.start", "Bl.in1.end", "Bl.x.s", "A1.g0.mid", "A2.g0.mid", "small.11", "Be.in1.end", "A2.g2.end", "Be.x.s",
    "Be.g0.end", "A2.in0.mid", "A1.g2.end", "A1.in0.mid", "Cl.x.r", "A1.g0.end", "Be.in0.end", "A2.g0.end",
    "Ce.in0.end", "Ce.x.r", "Bl.x.r", "Be.x.r", "A2.in0.end", "A1.in0.end",
]


def remote(src, dst, ssem, rsem, target):
    return pltpu.make_async_remote_copy(
        src_ref=src, dst_ref=dst, send_sem=ssem, recv_sem=rsem, device_id=target, device_id_type=MESH
    )


def kernel(
    seg_ref, gains_ref, bias_ref, tok_ref, qkv_ref, proj_ref, fc_ref, wout_ref, cot_ref,
    act_hbm, grad_hbm, ggain_hbm, gbias_hbm, gqkv_hbm, gproj_hbm, gfc_hbm, gwout_hbm,
    w, rbuf, act_out, grad_out, gsum, ggain_out, gbias_out, tokv, cotv,
    xin, x1, x2, x3, x4, qkv, probs, xh1, xh2, rs1, rs2, dgel, gf, dpre, dbr, datt, dmix, dmid, mask, qbias,
    bf, sgb, sb_y, sb_c, sb_x, sbw, sr, sr_c, sr_x, sr_z, sr_y,
    s_out, s_fc, s_proj, s_qkv, t_out, t_fc, t_proj, t_qkv, hb, sems,
):
    sec = lax.axis_index("section")
    dp = lax.axis_index("dp")
    c = lax.rem(dp, 2)
    y = lax.rem(lax.div(dp, 2), 4)
    z = lax.rem(lax.div(dp, 8), 4)
    x = lax.div(dp, 32)
    ox, oc = 1 - x, 1 - c
    yp = [lax.rem(y + k, 4) for k in range(4)]
    zp = [lax.rem(z + k, 4) for k in range(4)]

    def at(px, pz, py, pc):
        return (sec, ((px * 4 + pz) * 4 + py) * 2 + pc)

    ys = [at(x, z, yp[k], c) for k in range(4)]
    zs = [at(x, zp[k], y, c) for k in range(4)]
    xp = at(ox, z, y, c)
    sib = at(x, z, y, oc)
    other_section = (1 - sec, dp)

    taken = [0, 0]

    def sem():
        taken[0] += 1
        return sems.at[taken[0] - 1]

    def arrivals(pieces):
        taken[1] += pieces
        return taken[1] - pieces

    own = w.at[x, z, y, c]
    own_sem, tok_sem, cot_sem = sem(), sem(), sem()
    pltpu.make_async_copy(qkv_ref, own.at[pl.ds(0, 3)], own_sem).start()
    pltpu.make_async_copy(proj_ref, own.at[pl.ds(3, 1)], own_sem).start()
    pltpu.make_async_copy(fc_ref, own.at[pl.ds(4, 4)], own_sem).start()
    for j in range(4):
        pltpu.make_async_copy(wout_ref.at[:, pl.ds(1024 * j, 1024)], own.at[8 + j], own_sem).start()
    tok_in = pltpu.make_async_copy(tok_ref, tokv, tok_sem)
    cot_in = pltpu.make_async_copy(cot_ref, cotv, cot_sem)
    tok_in.start()
    cot_in.start()
    barrier = pltpu.get_barrier_semaphore()
    partners = ys[1:] + zs[1:] + [xp, sib, other_section]
    for target in partners:
        pl.semaphore_signal(barrier, 1, device_id=target, device_id_type=MESH)
    pl.semaphore_wait(barrier, len(partners))
    pltpu.make_async_copy(own, own, own_sem).wait()

    def slab(part, xx, i, o, half=None, summing=False):
        core, base = c, FIRST[part]
        if summing:
            core, base = (oc if SUM_AT[part][0] else c), SUM_AT[part][1]
        pieces = pl.ds(base, 2) if half is None else pl.ds(base + half, 1)
        pz, py = (o, i) if INNER_IS_Y[part] else (i, o)
        return w.at[xx, pz, py, core, pieces]

    def bytes_of(count):
        two = pl.ds(0, 2)
        return {
            1: w.at[0, 0, 0, 0, two],
            2: w.at[0, 0, two, 0, two],
            4: w.at[0, 0, :, 0, two],
            8: w.at[0, two, :, 0, two],
            15: w.at[0, 0, pl.ds(0, 3), 0, pl.ds(0, 10)],
            16: w.at[0, :, :, 0, two],
            30: w.at[0, two, pl.ds(0, 3), 0, pl.ds(0, 10)],
            32: w.at[:, :, :, 0, two],
        }[count]

    def await_arrival(which, count):
        ref = bytes_of(count)
        remote(ref, ref, which, which, sib).wait_recv()

    def await_sent(which, count):
        ref = bytes_of(count)
        remote(ref, ref, which, which, sib).wait_send()

    def axes(part):
        return (yp, zp, ys, zs) if INNER_IS_Y[part] else (zp, yp, zs, ys)

    def rings_of(part, summing):
        ip, op, idev, odev = axes(part)
        found = {}

        def along_inner(xx):
            return lambda j, half=None: slab(part, xx, ip[j], op[0], half, summing)

        def along_outer(xx, i):
            return lambda j, half=None: slab(part, xx, ip[i], op[j], half, summing)

        for other in (0, 1) if X_FIRST[part] else (0,):
            found[f"in{other}"] = ([along_inner(ox if other else x)], idev[3], idev[1])
        for g, (other, offsets) in enumerate(GROUPS):
            if X_FIRST[part] or not other:
                found[f"g{g}"] = ([along_outer(ox if other else x, i) for i in offsets], odev[3], odev[1])
        return found

    def small(src, dst, sems_of, target):
        return remote(src, dst, sems_of[0], sems_of[1], target)

    ag_rings = {part: rings_of(part, False) for part in PARTS}
    ag_sem = {(part, name): (sem(), sem()) for part in PARTS for name in ag_rings[part]}
    ag_sent = {part: (sem(), sem(), sem()) for part in PARTS}
    ag_x = {part: (sem(),) if X_FIRST[part] else (sem(), sem(), sem()) for part in PARTS}
    ag_sib = {part: sem() for part in PARTS}

    def line(part, xx, o):
        core, base = c, FIRST[part]
        if INNER_IS_Y[part]:
            return w.at[xx, o, :, core, pl.ds(base, 2)]
        return w.at[xx, :, o, core, pl.ds(base, 2)]

    def gather(step):
        part, name, *rest = step.split(".")
        if part == "small":
            small_steps[int(name)]()
            return
        ip, op, _, _ = axes(part)
        if name == "x" and rest[0] == "s":
            ref = slab(part, x, ip[0], op[0])
            remote(ref, ref, ag_sent[part][1], ag_x[part][0], xp).start()
        elif name == "x":
            await_arrival(ag_x[part][0], 1)
        elif name == "X":
            for i in GROUPS[int(rest[0])][1]:
                for o in STAGES[int(rest[1])]:
                    ref = slab(part, x, ip[i], op[o])
                    remote(ref, ref, ag_sent[part][1], ag_x[part][int(rest[1])], xp).start()
        elif name == "XR":
            await_arrival(ag_x[part][int(rest[0])], 4 * len(STAGES[int(rest[0])]))
        elif name == "sib":
            for o in STAGES[int(rest[1])]:
                ref = line(part, ox if int(rest[0]) else x, op[o])
                remote(ref, ref, ag_sent[part][2], ag_sib[part], sib).start()
        else:
            views, left, right = ag_rings[part][name]
            full, half = ag_sem[part, name]
            sent = ag_sent[part][0]
            if rest[0] == "start":
                for view in views:
                    remote(view(0), view(0), sent, full, right).start()
                    remote(view(0), view(0), sent, full, left).start()
            elif rest[0] == "mid":
                await_arrival(full, 2 * len(views))
                for view in views:
                    remote(view(3, 0), view(3, 0), sent, half, right).start()
                    remote(view(1, 1), view(1, 1), sent, half, left).start()
            else:
                await_arrival(half, len(views))

    spread = (
        lax.broadcasted_iota(jnp.int32, (16, 128), 1)
        == lax.broadcasted_iota(jnp.int32, (16, 128), 0) + 16 * (y * 2 + c)
    ).astype(F32)
    sm_y, sm_c, sm_z, sm_x = [(sem(), sem()) for _ in range(4)]

    def small_one():
        sgb[...] = jnp.zeros_like(sgb)
        sgb[0:2, :] = gains_ref[...].astype(F32)
        sgb[2:12, :] = bias_ref[...].astype(F32)
        sb_y[0] = jnp.dot(sgb[...].astype(BF16), spread.astype(BF16), preferred_element_type=F32)
        for k in (1, 2, 3):
            small(sb_y.at[0], sb_y.at[k], sm_y, ys[k]).start()

    def small_two():
        rows = sb_y.at[pl.ds(1, 3)]
        small(rows, rows, sm_y, sib).wait_recv()
        sb_c[0] = sb_y[0] + sb_y[1] + sb_y[2] + sb_y[3]
        small(sb_c.at[0], sb_c.at[1], sm_c, sib).start()

    def small_three():
        small(sb_c.at[0], sb_c.at[1], sm_c, sib).wait_recv()
        sb_x[x, z] = sb_c[0] + sb_c[1]
        for k in (1, 2, 3):
            small(sb_x.at[x, z], sb_x.at[x, z], sm_z, zs[k]).start()

    def small_four():
        rows = sb_x.at[0, pl.ds(0, 3)]
        small(rows, rows, sm_z, sib).wait_recv()
        small(sb_x.at[x], sb_x.at[x], sm_x, xp).start()

    def small_five():
        small(sb_x.at[ox], sb_x.at[ox], sm_x, xp).wait_recv()
        for g in range(8):
            bf[:, g * 128 : (g + 1) * 128] = sb_x[g // 4, g % 4]
        qbias[:, 0:WIDTH] = bf[3:4, :]
        qbias[:, WIDTH : 2 * WIDTH] = jnp.zeros((1, WIDTH), F32)
        qbias[:, 2 * WIDTH :] = bf[4:5, :]

    def row(k):
        return bf[k : k + 1, :]

    def small_six():
        seg = jnp.broadcast_to(seg_ref[...].astype(F32), (ROWS, ROWS))
        qi = lax.broadcasted_iota(jnp.int32, (ROWS, ROWS), 0)
        ki = lax.broadcasted_iota(jnp.int32, (ROWS, ROWS), 1)
        allowed = (seg == seg.T) & (ki <= qi) & (lax.div(qi, 64) == lax.div(ki, 64))
        mask[...] = allowed.astype(F32)

    small_steps = {1: small_one, 2: small_two, 3: small_three, 4: small_four, 5: small_five, 6: small_six}

    for step in GATHER_ONE:
        gather(step)

    handed = (sem(), sem())
    handed_on = remote(act_out, hb, *handed, other_section)
    handed_back = remote(grad_out, hb, *handed, other_section)
    tok_in.wait()
    cot_in.wait()

    @pl.when(sec == 0)
    def _():
        xin[...] = tokv[...].astype(F32)

    @pl.when(sec == 1)
    def _():
        for step in GATHER_TWO:
            gather(step)
        handed_on.wait_recv()
        xin[...] = hb[...].astype(F32)

    def norm(values, gain, shift):
        centre = values - jnp.mean(values, axis=-1, keepdims=True)
        rs = lax.rsqrt(jnp.mean(centre * centre, axis=-1, keepdims=True) + EPS)
        hat = centre * rs
        return hat, rs, (hat * gain + shift).astype(BF16)

    ex_sems = [(sem(), sem()) for _ in range(8)]

    def exchange(slot, src, dst):
        return remote(src, dst, *ex_sems[slot], sib)

    def from_sibling(part):
        await_arrival(ag_sib[part], 32)

    xh1[...], rs1[...], x1[0] = norm(xin[...], row(0), row(2))
    ex_first = exchange(0, x1.at[0], x1.at[1])
    ex_first.start()
    from_sibling("Be")
    from_sibling("Ce")

    def qkv_weights(k):
        return w[k, :, :, :, 0:3].reshape(1536, WIDTH)

    for k in range(2):
        cols = slice(1536 * k, 1536 * (k + 1))
        mixed = lax.dot_general(x1[0], qkv_weights(k), NT, preferred_element_type=F32)
        qkv[:, cols] = (mixed + qbias[:, cols]).astype(BF16)

    low_lanes = lax.broadcasted_iota(jnp.int32, (ROWS, 128), 1) < HEAD
    zero = jnp.zeros((ROWS, 128), BF16)

    def pair(base, hp):
        return slice(base + hp * 128, base + hp * 128 + 128)

    def lanes_of(e):
        return low_lanes if e == 0 else ~low_lanes

    raw = []
    for hp in range(8):
        q, k = qkv[:, pair(0, hp)], qkv[:, pair(WIDTH, hp)]
        for e in range(2):
            raw.append(lax.dot_general(jnp.where(lanes_of(e), q, zero), k, NT, preferred_element_type=F32))
    seen = mask[...] > 0.5
    soft = []
    for scores in raw:
        scores = jnp.where(seen, scores * 0.125, -1e30)
        ex = jnp.exp(scores - jnp.max(scores, axis=-1, keepdims=True))
        soft.append(ex * (1.0 / jnp.sum(ex, axis=-1, keepdims=True)))
    for hp in range(8):
        v = qkv[:, pair(2 * WIDTH, hp)]
        parts = []
        for e in range(2):
            probs[2 * hp + e] = soft[2 * hp + e]
            parts.append(jnp.dot(soft[2 * hp + e].astype(BF16), v, preferred_element_type=F32))
        x2[0, :, pair(0, hp)] = jnp.where(low_lanes, parts[0], parts[1]).astype(BF16)
    ex_att = exchange(1, x2.at[0], x2.at[1])
    ex_att.start()

    def proj_weights():
        return w[:, :, :, :, 3].reshape(WIDTH, WIDTH)

    xin[...] = xin[...] + (lax.dot_general(x2[0], proj_weights(), NT, preferred_element_type=F32) + row(5))
    xh2[...], rs2[...], x3[0] = norm(xin[...], row(1), row(6))
    ex_second = exchange(2, x3.at[0], x3.at[1])
    ex_second.start()

    @pl.when(sec == 0)
    def _():
        for step in GATHER_TWO:
            gather(step)

    from_sibling("A1")
    from_sibling("A2")

    def fc_weights(j):
        return w[j // 2, 2 * (j % 2) : 2 * (j % 2) + 2, :, :, 4:8].reshape(WIDTH, WIDTH)

    for j in range(4):
        pre = lax.dot_general(x3[0], fc_weights(j), NT, preferred_element_type=F32) + row(7 + j)
        square = pre * pre
        t = jnp.tanh(GC * (pre + 0.044715 * (square * pre)))
        half = 0.5 * (1.0 + t)
        x4[0, j] = (pre * half).astype(BF16)
        dgel[j] = half + (0.5 * GC) * pre * (1.0 - t * t) * (1.0 + 0.134145 * square)
    ex_act = exchange(3, x4.at[0], x4.at[1])
    ex_act.start()
    from_sibling("Bl")
    from_sibling("Cl")

    def wout_weights(j):
        return w[:, :, :, :, 8 + j].reshape(WIDTH, WIDTH)

    result = xin[...] + row(11)
    for j in range(4):
        result = result + lax.dot_general(x4[0, j], wout_weights(j), NT, preferred_element_type=F32)
    act_out[...] = result.astype(BF16)

    @pl.when(sec == 0)
    def _():
        handed_on.start()

    act_done = pltpu.make_async_copy(act_out, act_hbm, tok_sem)
    act_done.start()

    for part in PARTS:
        await_sent(ag_sent[part][0], 30 if X_FIRST[part] else 15)
        await_sent(ag_sent[part][1], 1 if X_FIRST[part] else 16)
        await_sent(ag_sent[part][2], 32)
    rows = sb_y.at[pl.ds(1, 3)]
    small(rows, rows, sm_y, sib).wait_send()
    small(sb_c.at[0], sb_c.at[1], sm_c, sib).wait_send()
    small(rows, rows, sm_z, sib).wait_send()
    small(sb_x.at[x], sb_x.at[x], sm_x, xp).wait_send()

    @pl.when(sec == 0)
    def _():
        handed_back.wait_recv()
        gf[...] = hb[...]

    @pl.when(sec == 1)
    def _():
        gf[...] = cotv[...]

    def column_sum(values):
        return jnp.sum(values.astype(F32), axis=0, keepdims=True)

    sbw[...] = jnp.zeros_like(sbw)
    sbw[11:12, :] = column_sum(gf[...])
    s_out[...] = gf[...].T.reshape(2, 4, 4, 2, 1, 16, ROWS)

    def swap(slot, src, dst):
        return exchange(slot, src.at[:, :, :, oc], dst)

    ex_gf = swap(4, s_out, t_out)
    ex_gf.start()
    for j in range(4):
        d_act = jnp.dot(gf[...], wout_weights(j), preferred_element_type=F32)
        d_pre = (dgel[j] * d_act).astype(BF16)
        dpre[j] = d_pre
        sbw[7 + j : 8 + j, :] = column_sum(d_pre)
        s_fc[j // 2, 2 * (j % 2) : 2 * (j % 2) + 2] = d_pre.T.reshape(2, 4, 2, 4, 16, ROWS)
    ex_dpre = swap(5, s_fc, t_fc)
    ex_dpre.start()
    ex_dbr = swap(6, s_proj, t_proj)
    ex_dmix = swap(7, s_qkv, t_qkv)

    def lhs(mine, theirs, rows):
        return jnp.concatenate([mine.reshape(rows, ROWS), theirs.reshape(rows, ROWS)], axis=1)

    def product(left, right):
        return jnp.dot(left, right, preferred_element_type=F32).astype(BF16)

    def grads_out(xx):
        left = lhs(s_out[xx, :, :, c], t_out[xx], 256)
        for j in range(4):
            w[xx, :, :, oc, 8 + j] = product(left, x4[:, j].reshape(2 * ROWS, WIDTH)).reshape(4, 4, 16, WIDTH)

    def grads_fc(xx):
        for k in range(2):
            zz = slice(2 * k, 2 * k + 2)
            left = lhs(s_fc[xx, zz, :, c], t_fc[xx, zz], 512)
            w[xx, zz, :, c, 8:12] = product(left, x3[...].reshape(2 * ROWS, WIDTH)).reshape(2, 4, 4, 16, WIDTH)

    def grads_att(xx):
        left = lhs(s_proj[xx, :, :, c], t_proj[xx], 256)
        w[xx, :, :, c, 7] = product(left, x2[...].reshape(2 * ROWS, WIDTH)).reshape(4, 4, 16, WIDTH)
        for k in range(2):
            zz = slice(2 * k, 2 * k + 2)
            left = lhs(s_qkv[xx, zz, :, c], t_qkv[xx, zz], 384)
            w[xx, zz, :, c, 4:7] = product(left, x1[...].reshape(2 * ROWS, WIDTH)).reshape(2, 4, 3, 16, WIDTH)

    def compute(name):
        if name == "gout1":
            ex_gf.wait_recv()
            ex_act.wait_recv()
            grads_out(ox)
        elif name == "gout0":
            grads_out(x)
        elif name == "gfc1":
            ex_dpre.wait_recv()
            ex_second.wait_recv()
            grads_fc(ox)
        elif name == "gfc0":
            grads_fc(x)
        elif name == "gatt1":
            ex_first.wait_recv()
            ex_att.wait_recv()
            ex_dbr.wait_recv()
            ex_dmix.wait_recv()
            grads_att(ox)
        elif name == "gatt0":
            grads_att(x)
        elif name == "first":
            pl.when(sec == 0)(back_first)

    rs_rings = {part: rings_of(part, True) for part in PARTS}
    rs_sem = {(part, name): (sem(), sem()) for part in PARTS for name in rs_rings[part]}
    rs_sent = {part: (sem(), sem()) for part in PARTS}
    rs_x = {part: (sem(),) if X_FIRST[part] else (sem(), sem(), sem()) for part in PARTS}
    rs_at = {(part, name): arrivals(6 * len(rs_rings[part][name][0])) for part in PARTS for name in rs_rings[part]}
    rs_x_at = {part: arrivals(2 if X_FIRST[part] else 32) for part in PARTS}

    def add(view, *terms, out=None):
        total = view[...].astype(F32)
        for term in terms:
            total = total + term[...].astype(F32)
        if out is None:
            view[...] = total.astype(BF16)
        else:
            out[...] = total

    def own_sum(part):
        return gsum.at[pl.ds(FIRST[part], 2)]

    def summing(step):
        part, name, *rest = step.split(".")
        if part == "small":
            small_steps[int(name)]()
            return
        if part == "comp":
            compute(name)
            return
        ip, op, _, _ = axes(part)
        if name == "x" and rest[0] == "s":
            buf = rbuf.at[pl.ds(rs_x_at[part], 2)]
            remote(slab(part, ox, ip[0], op[0], None, True), buf, rs_sent[part][1], rs_x[part][0], xp).start()
        elif name == "x":
            await_arrival(rs_x[part][0], 1)
            add(slab(part, x, ip[0], op[0], None, True), rbuf.at[pl.ds(rs_x_at[part], 2)], out=own_sum(part))
        elif name in ("X", "XR"):
            stage = int(rest[0])
            if name == "XR":
                await_arrival(rs_x[part][stage], 4 * len(STAGES[stage]))
            for o in STAGES[stage]:
                for i in range(4):
                    buf = rbuf.at[pl.ds(rs_x_at[part] + (o * 4 + i) * 2, 2)]
                    if name == "X":
                        ref = slab(part, ox, ip[i], op[o], None, True)
                        remote(ref, buf, rs_sent[part][1], rs_x[part][stage], xp).start()
                    else:
                        add(slab(part, x, ip[i], op[o], None, True), buf)
        else:
            views, left, right = rs_rings[part][name]
            half, full = rs_sem[part, name]
            sent = rs_sent[part][0]

            def buf(k, offset, size):
                return rbuf.at[pl.ds(rs_at[part, name] + 6 * k + offset, size)]

            if rest[0] == "start":
                for k, view in enumerate(views):
                    remote(view(2, 0), buf(k, 0, 1), sent, half, right).start()
                    remote(view(2, 1), buf(k, 1, 1), sent, half, left).start()
            elif rest[0] == "mid":
                await_arrival(half, len(views))
                for k, view in enumerate(views):
                    add(view(1, 0), buf(k, 0, 1))
                    remote(view(1), buf(k, 2, 2), sent, full, right).start()
                    add(view(3, 1), buf(k, 1, 1))
                    remote(view(3), buf(k, 4, 2), sent, full, left).start()
            else:
                await_arrival(full, 2 * len(views))
                last = name == "in0" and not X_FIRST[part]
                for k, view in enumerate(views):
                    add(view(0), buf(k, 2, 2), buf(k, 4, 2), out=own_sum(part) if last else None)

    sm_core, sm_xs, sm_zs, sm_ys = [(sem(), sem()) for _ in range(4)]

    def small_seven():
        for g in range(8):
            sr[g // 4, g % 4] = sbw[:, g * 128 : (g + 1) * 128]
        small(sr, sr_c, sm_core, sib).start()

    def small_eight():
        small(sr, sr_c, sm_core, sib).wait()
        sr[...] = sr[...] + sr_c[...]
        small(sr.at[ox], sr_x, sm_xs, xp).start()

    def small_nine():
        small(sr.at[ox], sr_x, sm_xs, xp).wait_recv()
        sr[x] = sr[x] + sr_x[...]
        for k in (1, 2, 3):
            small(sr.at[x, zp[k]], sr_z.at[k - 1], sm_zs, zs[k]).start()

    def small_ten():
        small(sr_z, sr_z, sm_zs, sib).wait_recv()
        sr_y[0] = sr[x, z] + sr_z[0] + sr_z[1] + sr_z[2]
        for k in (1, 2, 3):
            small(sr_y.at[0], sr_y.at[k], sm_ys, ys[k]).start()

    def small_eleven():
        rows = sr_y.at[pl.ds(1, 3)]
        small(rows, rows, sm_ys, sib).wait_recv()
        total = sr_y[0] + sr_y[1] + sr_y[2] + sr_y[3]
        picked = lax.dot_general(total, spread, NT, preferred_element_type=F32, precision=lax.Precision.HIGHEST)
        ggain_out[...] = picked[0:2, :]
        for k in range(10):
            gbias_out[k] = picked[2 + k : 3 + k, :]

    small_steps.update({7: small_seven, 8: small_eight, 9: small_nine, 10: small_ten, 11: small_eleven})

    @pl.when(sec == 0)
    def _():
        for step in SUM_ONE:
            summing(step)

    d_second = jnp.zeros((ROWS, WIDTH), F32)
    for j in range(4):
        d_second = d_second + jnp.dot(dpre[j], fc_weights(j), preferred_element_type=F32)

    def norm_back(d_out, hat, rs, gain):
        d_hat = d_out * gain
        mean_one = jnp.mean(d_hat, axis=-1, keepdims=True)
        mean_two = jnp.mean(d_hat * hat, axis=-1, keepdims=True)
        return rs * (d_hat - mean_one - hat * mean_two)

    sbw[1:2, :] = column_sum(d_second * xh2[...])
    sbw[6:7, :] = column_sum(d_second)
    dmid[...] = gf[...].astype(F32) + norm_back(d_second, xh2[...], rs2[...], row(1))
    dbr[...] = dmid[...].astype(BF16)
    sbw[5:6, :] = column_sum(dbr[...])
    s_proj[...] = dbr[...].T.reshape(2, 4, 4, 2, 1, 16, ROWS)
    ex_dbr.start()

    @pl.when(sec == 0)
    def _():
        for step in SUM_TWO:
            summing(step)

    datt[...] = jnp.dot(dbr[...], proj_weights(), preferred_element_type=F32).astype(BF16)
    d_probs, masked_da = [], []
    for hp in range(8):
        da, v = datt[:, pair(0, hp)], qkv[:, pair(2 * WIDTH, hp)]
        for e in range(2):
            masked_da.append(jnp.where(lanes_of(e), da, zero))
            d_probs.append(lax.dot_general(masked_da[-1], v, NT, preferred_element_type=F32))
    d_scores = []
    for h in range(16):
        p, dp_ = probs[h], d_probs[h]
        d_scores.append((p * (dp_ - jnp.sum(dp_ * p, axis=-1, keepdims=True))).astype(BF16))
    for hp in range(8):
        q, k = qkv[:, pair(0, hp)], qkv[:, pair(WIDTH, hp)]
        dq, dk, dv = [], [], []
        for e in range(2):
            h = 2 * hp + e
            dv.append(jnp.dot(probs[h].astype(BF16).T, masked_da[h], preferred_element_type=F32))
            dq.append(jnp.dot(d_scores[h], k, preferred_element_type=F32))
            dk.append(jnp.dot(d_scores[h].T, jnp.where(lanes_of(e), q, zero), preferred_element_type=F32))
        dmix[:, pair(0, hp)] = (jnp.where(low_lanes, dq[0], dq[1]) * 0.125).astype(BF16)
        dmix[:, pair(WIDTH, hp)] = ((dk[0] + dk[1]) * 0.125).astype(BF16)
        dmix[:, pair(2 * WIDTH, hp)] = (dv[0] + dv[1]).astype(BF16)
    for k in range(2):
        s_qkv[k] = dmix[:, 1536 * k : 1536 * (k + 1)].T.reshape(4, 4, 2, 3, 16, ROWS)
    ex_dmix.start()
    sbw[3:4, :] = column_sum(dmix[:, 0:WIDTH])
    sbw[4:5, :] = column_sum(dmix[:, 2 * WIDTH :])

    def back_first():
        d_first = jnp.dot(dmix[:, 0:1536], qkv_weights(0), preferred_element_type=F32)
        d_first = d_first + jnp.dot(dmix[:, 1536:], qkv_weights(1), preferred_element_type=F32)
        sbw[0:1, :] = column_sum(d_first * xh1[...])
        sbw[2:3, :] = column_sum(d_first)
        grad_out[...] = (dmid[...] + norm_back(d_first, xh1[...], rs1[...], row(0))).astype(BF16)
        pltpu.make_async_copy(grad_out, grad_hbm, cot_sem).start()

    @pl.when(sec == 1)
    def _():
        back_first()
        handed_back.start()
        for step in SUM_ONE + SUM_TWO:
            summing(step)

    for step in SUM_THREE:
        summing(step)

    done = [
        pltpu.make_async_copy(gsum.at[pl.ds(0, 3)], gqkv_hbm, own_sem),
        pltpu.make_async_copy(gsum.at[pl.ds(3, 1)], gproj_hbm, own_sem),
        pltpu.make_async_copy(gsum.at[pl.ds(4, 4)], gfc_hbm, own_sem),
    ] + [
        pltpu.make_async_copy(gsum.at[8 + j], gwout_hbm.at[:, pl.ds(1024 * j, 1024)], own_sem) for j in range(4)
    ]
    for cp in done:
        cp.start()
    small_done = [
        pltpu.make_async_copy(ggain_out, ggain_hbm, sem()),
        pltpu.make_async_copy(gbias_out, gbias_hbm, sem()),
    ]
    for cp in small_done:
        cp.start()

    for part in PARTS:
        await_sent(rs_sent[part][0], 30 if X_FIRST[part] else 15)
        await_sent(rs_sent[part][1], 1 if X_FIRST[part] else 16)
    for cp in (ex_first, ex_att, ex_second, ex_act, ex_gf, ex_dpre, ex_dbr, ex_dmix):
        cp.wait_send()
    small(sr.at[ox], sr_x, sm_xs, xp).wait_send()
    small(sr_z, sr_z, sm_zs, sib).wait_send()
    rows = sr_y.at[pl.ds(1, 3)]
    small(rows, rows, sm_ys, sib).wait_send()

    @pl.when(sec == 0)
    def _():
        handed_on.wait_send()

    @pl.when(sec == 1)
    def _():
        handed_back.wait_send()

    act_done.wait()
    pltpu.make_async_copy(grad_out, grad_hbm, cot_sem).wait()
    pltpu.make_async_copy(gsum, gsum, own_sem).wait()
    for cp in small_done:
        cp.wait()
    if (taken[0], taken[1]) != (SEMAPHORES, ARRIVALS):
        raise ValueError(taken)


SEMAPHORES = 255
ARRIVALS = 372


def move(*refs):
    count = len(refs) // 3
    sems = refs[-1]
    into = [pltpu.make_async_copy(refs[k], refs[2 * count + k], sems.at[0, k]) for k in range(count)]
    out = [pltpu.make_async_copy(refs[2 * count + k], refs[count + k], sems.at[1, k]) for k in range(count)]
    for cp in into:
        cp.start()
    for k in range(count):
        into[k].wait()
        out[k].start()
    for cp in out:
        cp.wait()


def local(tokens, segment_ids, gains, biases, w_qkv, w_proj, w_fc, w_out, cotangent):
    vmem = pl.BlockSpec(memory_space=pltpu.VMEM)
    hbm = pl.BlockSpec(memory_space=pl.ANY)

    def shape(*dims, dtype=F32):
        return jax.ShapeDtypeStruct(dims, dtype)

    def v(*dims, dtype=BF16):
        return pltpu.VMEM(dims, dtype)

    scratch = [
        v(2, 4, 4, 2, 12, 16, WIDTH), v(ARRIVALS, 16, WIDTH),
        v(ROWS, WIDTH), v(ROWS, WIDTH), v(12, 16, WIDTH, dtype=F32), v(2, 16, dtype=F32), v(10, 1, 16, dtype=F32),
        v(ROWS, WIDTH), v(ROWS, WIDTH),
        v(ROWS, WIDTH, dtype=F32), v(2, ROWS, WIDTH), v(2, ROWS, WIDTH), v(2, ROWS, WIDTH), v(2, 4, ROWS, WIDTH),
        v(ROWS, 3 * WIDTH), v(16, ROWS, ROWS, dtype=F32), v(ROWS, WIDTH, dtype=F32), v(ROWS, WIDTH, dtype=F32),
        v(ROWS, 1, dtype=F32), v(ROWS, 1, dtype=F32), v(4, ROWS, WIDTH, dtype=F32), v(ROWS, WIDTH),
        v(4, ROWS, WIDTH), v(ROWS, WIDTH), v(ROWS, WIDTH), v(ROWS, 3 * WIDTH), v(ROWS, WIDTH, dtype=F32),
        v(ROWS, ROWS, dtype=F32), v(1, 3 * WIDTH, dtype=F32),
        v(16, WIDTH, dtype=F32), v(16, 16, dtype=F32), v(4, 16, 128, dtype=F32), v(2, 16, 128, dtype=F32),
        v(2, 4, 16, 128, dtype=F32), v(16, WIDTH, dtype=F32), v(2, 4, 16, 128, dtype=F32),
        v(2, 4, 16, 128, dtype=F32), v(4, 16, 128, dtype=F32), v(3, 16, 128, dtype=F32), v(4, 16, 128, dtype=F32),
        v(2, 4, 4, 2, 1, 16, ROWS), v(2, 4, 4, 2, 4, 16, ROWS), v(2, 4, 4, 2, 1, 16, ROWS), v(2, 4, 4, 2, 3, 16, ROWS),
        v(2, 4, 4, 1, 16, ROWS), v(2, 4, 4, 4, 16, ROWS), v(2, 4, 4, 1, 16, ROWS), v(2, 4, 4, 3, 16, ROWS),
        v(ROWS, WIDTH),
        pltpu.SemaphoreType.DMA((SEMAPHORES,)),
    ]
    results = (
        shape(ROWS, WIDTH, dtype=BF16), shape(ROWS, WIDTH, dtype=BF16), shape(2, 16), shape(10, 1, 16),
        shape(3, 16, WIDTH), shape(1, 16, WIDTH), shape(4, 16, WIDTH), shape(16, 4 * WIDTH),
    )
    out = pl.pallas_call(
        kernel,
        out_shape=results,
        in_specs=[vmem, vmem, vmem] + [hbm] * 6,
        out_specs=(hbm,) * 8,
        scratch_shapes=scratch,
        compiler_params=pltpu.CompilerParams(
            collective_id=0, has_side_effects=True, vmem_limit_bytes=63 * 2**20
        ),
        name="relay",
    )(
        segment_ids.reshape(1, ROWS),
        gains[0],
        biases[0],
        tokens,
        w_qkv[0].T.reshape(3, 16, WIDTH),
        w_proj[0].T.reshape(1, 16, WIDTH),
        w_fc[0].T.reshape(4, 16, WIDTH),
        w_out[0].T,
        cotangent,
    )
    out = pl.pallas_call(
        move,
        out_shape=results,
        in_specs=[hbm] * 8,
        out_specs=(hbm,) * 8,
        scratch_shapes=[pltpu.VMEM(r.shape, r.dtype) for r in results] + [pltpu.SemaphoreType.DMA((2, 8))],
        name="move",
    )(*out)
    activations, input_grads, g_gains, g_biases, g_qkv, g_proj, g_fc, g_out = out
    return (
        activations[None],
        input_grads[None],
        g_gains[None],
        g_biases.transpose(1, 0, 2),
        g_qkv.reshape(48, WIDTH).T[None],
        g_proj.reshape(16, WIDTH).T[None],
        g_fc.reshape(64, WIDTH).T[None],
        g_out.T[None],
    )


def solution(mesh):
    weight = P("section", None, "dp")
    rows = P("section", "dp", None)
    return jax.shard_map(
        local,
        mesh=mesh,
        in_specs=(P("dp", None), P("dp")) + (weight,) * 6 + (P("dp", None),),
        out_specs=(rows, rows) + (weight,) * 6,
        check_vma=False,
    )
```

```python
import jax
import jax.numpy as jnp
from jax import lax
from jax.experimental import pallas as pl
from jax.experimental.pallas import tpu as pltpu
from jax.sharding import PartitionSpec as P

MESH = pl.DeviceIdType.MESH
F32 = jnp.float32
BF16 = jnp.bfloat16
EPS = 1e-05
ROWS = 128
WIDTH = 1024
HEAD = 64
GC = 0.7978845608028654
NT = (((1,), (1,)), ((), ()))

PARTS = ("Be", "Ce", "A1", "A2", "Bl", "Cl")
FIRST = {"Be": 0, "Ce": 2, "A1": 4, "A2": 6, "Bl": 8, "Cl": 10}
INNER_IS_Y = {"Be": False, "Ce": True, "A1": True, "A2": False, "Bl": False, "Cl": True}
X_FIRST = {"Be": True, "Ce": True, "A1": False, "A2": False, "Bl": True, "Cl": True}
GROUPS = {
    "g0": (0, (0,)), "g1": (1, (0,)), "g2": (0, (1, 3)), "g3": (0, (2,)), "g4": (1, (1, 3)), "g5": (1, (2,)),
    "gA": (0, (0, 1, 2, 3)), "gB": (1, (0, 1, 2, 3)),
}
FINE = ("g0", "g1", "g2", "g3", "g4", "g5")
COARSE = ("gA", "gB")
GATHER_GROUPS = {"Be": COARSE, "Ce": COARSE, "A1": FINE, "A2": FINE, "Bl": COARSE, "Cl": COARSE}
SUM_GROUPS = {"Be": COARSE, "Ce": COARSE, "A1": COARSE, "A2": COARSE, "Bl": COARSE, "Cl": COARSE}
STAGES = ((0,), (1, 3), (2,))
SUM_AT = {"Be": (0, 4), "Ce": (0, 6), "A1": (0, 8), "A2": (0, 10), "Bl": (1, 8), "Cl": (1, 10)}

GATHER_ONE = [
    "Ce.x.s", "A2.in0.start", "A1.in0.start", "A2.g0.start", "A2.X.g0.0", "Be.in0.start", "Bl.in0.start",
    "Ce.in0.start", "A1.g0.start", "Cl.x.s", "Cl.in0.start", "A1.in0.mid", "Ce.x.r", "Bl.x.s", "small.1", "Be.x.s",
    "A2.g0.mid", "Be.in0.mid", "A2.in0.mid", "A1.g2.start", "A2.X.g2.0", "Ce.in1.start", "A2.g2.start", "A2.X.g0.1",
    "A1.in0.end", "Be.in0.end", "Bl.x.r", "Ce.in0.mid", "A1.sib.0.0", "Be.x.r", "Be.in1.start", "A1.g3.start",
    "Bl.in1.start", "Ce.in1.mid", "A1.X.g2.0", "Cl.x.r", "Bl.in0.mid", "Be.gA.start", "Ce.in0.end", "A1.g0.mid",
    "Be.in1.mid", "A1.X.g3.0", "small.2", "A1.g3.mid", "A2.in0.end", "A2.X.g3.0", "A2.g3.start", "Ce.in1.end",
    "Ce.gA.start", "A1.g0.end", "A1.X.g0.0", "A2.sib.0.0", "Bl.in1.mid", "Cl.in1.start", "Be.in1.end", "Cl.in0.mid",
    "Be.gB.start", "A1.g2.mid", "A1.g3.end", "A1.X.g2.1", "A1.X.g0.1", "Ce.gB.start", "A2.g3.mid", "small.3",
    "A1.XR.0", "Be.sib.1.0", "A2.XR.0", "Be.gA.mid", "Be.sib.0.0", "A1.X.g3.1", "A2.g2.mid", "Ce.sib.0.0",
    "A1.X.g3.2", "Cl.in0.end", "Bl.in0.end", "A2.X.g3.1", "A2.sib.0.1", "Bl.sib.0.0", "A1.sib.1.0", "Cl.in1.mid",
    "Be.gB.mid", "Ce.gA.mid", "Be.sib.0.1", "A1.sib.0.1", "Ce.gB.mid", "small.4", "A2.X.g2.1", "A2.g2.end",
    "A1.X.g0.2", "Bl.in1.end", "Ce.sib.1.0", "Be.sib.1.1", "Ce.sib.1.1", "Ce.sib.0.1", "Cl.gA.start", "A2.g3.end",
    "Bl.gA.start", "A1.XR.1", "Ce.gA.end", "Ce.gB.end", "A1.g2.end", "Be.gA.end", "Be.gB.end", "A1.X.g2.2",
    "A2.X.g2.2", "Ce.sib.0.2", "small.5", "Bl.gB.start", "Cl.in1.end", "Cl.sib.1.0", "A2.g0.end", "Be.sib.1.2",
    "Cl.gB.start", "Ce.sib.1.2", "Cl.sib.0.0", "A2.X.g3.2", "Be.sib.0.2", "A2.sib.1.0", "A2.X.g0.2", "A1.sib.1.1",
    "A2.XR.1", "Cl.gA.mid", "Bl.gA.mid", "Bl.sib.0.1", "A2.sib.0.2", "Bl.sib.1.0", "Cl.sib.0.1", "A2.sib.1.1",
    "small.6",
]

GATHER_TWO = [
    "Cl.gB.mid", "A1.sib.0.2", "Cl.sib.1.1", "Bl.gB.mid", "A1.XR.2", "A1.sib.1.2", "A2.XR.2", "Bl.gA.end",
    "A2.sib.1.2", "Cl.gA.end", "Cl.sib.0.2", "Bl.sib.1.1", "Cl.gB.end", "Cl.sib.1.2", "Bl.sib.0.2", "Bl.gB.end",
    "Bl.sib.1.2",
]

SUM_ONE = [
    "comp.gout1", "comp.gout0", "Cl.gA.start", "Bl.gB.start", "Cl.gB.start", "Bl.gA.start", "comp.gfc1", "A1.X.2",
    "A2.X.2",
]

SUM_TWO = [
    "Bl.gB.mid", "Cl.gA.mid", "comp.gfc0", "Cl.gB.mid", "Bl.gA.mid",
]

SUM_THREE = [
    "A2.X.1", "Bl.gB.end", "comp.gatt1", "A1.X.1", "Ce.gB.start", "comp.gatt0", "Be.gB.start", "Ce.gA.start",
    "Be.gA.start", "Cl.gB.end", "Ce.gB.mid", "Be.gB.mid", "Cl.in1.start", "Bl.gA.end", "A2.XR.2", "Bl.in1.start",
    "A1.XR.2", "A1.gA.start", "A1.X.0", "Bl.in0.start", "Be.gA.mid", "Be.gB.end", "Be.in1.start", "Ce.gB.end",
    "Ce.in1.start", "A2.gA.start", "Cl.gA.end", "A2.XR.1", "Bl.in1.mid", "A2.X.0", "Cl.in1.mid", "Cl.in0.start",
    "Ce.gA.mid", "Be.gA.end", "A1.XR.1", "A1.gA.mid", "Ce.in1.mid", "comp.first", "small.7", "A2.gA.mid",
    "Be.in0.start", "Be.in1.mid", "A1.XR.0", "Ce.in1.end", "Ce.x.s", "small.8", "Bl.in0.mid", "Ce.gA.end",
    "Bl.in1.end", "Cl.in1.end", "Ce.in0.start", "A1.gA.end", "A1.in0.start", "small.9", "Cl.in0.mid", "Bl.x.s",
    "Cl.x.s", "A2.XR.0", "A2.gA.end", "A2.in0.start", "Be.in1.end", "small.10", "Ce.in0.mid", "Be.x.s", "Be.in0.mid",
    "A1.in0.mid", "A2.in0.mid", "Bl.in0.end", "Cl.in0.end", "small.11", "Be.in0.end", "Ce.in0.end", "Be.x.r",
    "Bl.x.r", "Cl.x.r", "A1.in0.end", "Ce.x.r", "A2.in0.end",
]


def remote(src, dst, ssem, rsem, target):
    return pltpu.make_async_remote_copy(
        src_ref=src, dst_ref=dst, send_sem=ssem, recv_sem=rsem, device_id=target, device_id_type=MESH
    )


def kernel(
    seg_ref, gains_ref, bias_ref, tok_ref, qkv_ref, proj_ref, fc_ref, wout_ref, cot_ref,
    act_hbm, grad_hbm, ggain_hbm, gbias_hbm, gqkv_hbm, gproj_hbm, gfc_hbm, gwout_hbm,
    w, rbuf, act_out, grad_out, gsum, ggain_out, gbias_out, tokv, cotv, segs,
    xin, x1, x2, x3, x4, qkv, probs, xh1, xh2, rs1, rs2, dgel, gf, dpre, dbr, datt, dmix, dmid, mask, qbias,
    bf, sgb, sb_y, sb_c, sb_x, sbw, sr, sr_c, sr_x, sr_z, sr_y,
    s_out, s_fc, s_proj, s_qkv, t_out, t_fc, t_proj, t_qkv, hb, sems,
):
    sec = lax.axis_index("section")
    dp = lax.axis_index("dp")
    c = lax.rem(dp, 2)
    y = lax.rem(lax.div(dp, 2), 4)
    z = lax.rem(lax.div(dp, 8), 4)
    x = lax.div(dp, 32)
    ox, oc = 1 - x, 1 - c
    yp = [lax.rem(y + k, 4) for k in range(4)]
    zp = [lax.rem(z + k, 4) for k in range(4)]

    def at(px, pz, py, pc):
        return (sec, ((px * 4 + pz) * 4 + py) * 2 + pc)

    ys = [at(x, z, yp[k], c) for k in range(4)]
    zs = [at(x, zp[k], y, c) for k in range(4)]
    xp = at(ox, z, y, c)
    sib = at(x, z, y, oc)
    other_section = (1 - sec, ((lax.rem(x + c, 2) * 4 + z) * 4 + y) * 2 + c)
    crossed = (sec == 1) & (c == 1)
    rows_at = sec * c

    taken = [0, 0]

    def sem():
        taken[0] += 1
        return sems.at[taken[0] - 1]

    def arrivals(slabs):
        taken[1] += slabs
        return taken[1] - slabs

    own = w.at[x, z, y, c]
    own_sem, tok_sem, cot_sem = sem(), sem(), sem()
    pltpu.make_async_copy(qkv_ref, own.at[pl.ds(0, 3)], own_sem).start()
    pltpu.make_async_copy(proj_ref, own.at[pl.ds(3, 1)], own_sem).start()
    pltpu.make_async_copy(fc_ref, own.at[pl.ds(4, 4)], own_sem).start()
    for j in range(4):
        pltpu.make_async_copy(wout_ref.at[:, pl.ds(1024 * j, 1024)], own.at[8 + j], own_sem).start()
    tok_in = pltpu.make_async_copy(tok_ref, tokv, tok_sem)
    cot_in = pltpu.make_async_copy(cot_ref, cotv.at[0], cot_sem)
    tok_in.start()
    cot_in.start()
    barrier = pltpu.get_barrier_semaphore()
    partners = ys[1:] + zs[1:] + [xp, sib, other_section]
    for target in partners:
        pl.semaphore_signal(barrier, 1, device_id=target, device_id_type=MESH)
    pl.semaphore_wait(barrier, len(partners))
    pltpu.make_async_copy(own, own, own_sem).wait()

    def slab(part, xx, i, o, half=None, summing=False):
        core, base = c, FIRST[part]
        if summing:
            core, base = (oc if SUM_AT[part][0] else c), SUM_AT[part][1]
        pieces = pl.ds(base, 2) if half is None else pl.ds(base + half, 1)
        pz, py = (o, i) if INNER_IS_Y[part] else (i, o)
        return w.at[xx, pz, py, core, pieces]

    def bytes_of(count):
        two = pl.ds(0, 2)
        return {
            1: w.at[0, 0, 0, 0, two],
            2: w.at[0, 0, two, 0, two],
            4: w.at[0, 0, :, 0, two],
            8: w.at[0, two, :, 0, two],
            15: w.at[0, 0, pl.ds(0, 3), 0, pl.ds(0, 10)],
            16: w.at[0, :, :, 0, two],
            30: w.at[0, two, pl.ds(0, 3), 0, pl.ds(0, 10)],
            32: w.at[:, :, :, 0, two],
        }[count]

    def await_arrival(which, count):
        ref = bytes_of(count)
        remote(ref, ref, which, which, sib).wait_recv()

    def await_sent(which, count):
        ref = bytes_of(count)
        remote(ref, ref, which, which, sib).wait_send()

    def axes(part):
        return (yp, zp, ys, zs) if INNER_IS_Y[part] else (zp, yp, zs, ys)

    def line(part, xx, o, half=None, summing=False):
        core, base = c, FIRST[part]
        if summing:
            core, base = (oc if SUM_AT[part][0] else c), SUM_AT[part][1]
        inner = slice(None) if half is None else pl.ds(2 * half, 2)
        pz, py = (o, inner) if INNER_IS_Y[part] else (inner, o)
        return w.at[xx, pz, py, core, pl.ds(base, 2)]

    def rings_of(part, summing):
        ip, op, idev, odev = axes(part)
        found = {}

        def along_inner(xx):
            return lambda j, half=None: slab(part, xx, ip[j], op[0], half, summing)

        def along_outer(xx, i):
            return lambda j, half=None: slab(part, xx, ip[i], op[j], half, summing)

        def along_line(xx):
            return lambda j, half=None: line(part, xx, op[j], half, summing)

        for other in (0, 1) if X_FIRST[part] else (0,):
            found[f"in{other}"] = ([along_inner(ox if other else x)], 1, idev[3], idev[1])
        for g in (SUM_GROUPS if summing else GATHER_GROUPS)[part]:
            other, offsets = GROUPS[g]
            if X_FIRST[part] or not other:
                xx = ox if other else x
                if len(offsets) == 4:
                    found[g] = ([along_line(xx)], 4, odev[3], odev[1])
                else:
                    found[g] = ([along_outer(xx, i) for i in offsets], 1, odev[3], odev[1])
        return found

    def small(src, dst, sems_of, target):
        return remote(src, dst, sems_of[0], sems_of[1], target)

    ag_rings = {part: rings_of(part, False) for part in PARTS}
    ag_sem = {(part, name): (sem(), sem()) for part in PARTS for name in ag_rings[part]}
    ag_sent = {part: (sem(), sem(), sem()) for part in PARTS}
    ag_x = {part: (sem(),) if X_FIRST[part] else (sem(), sem(), sem()) for part in PARTS}
    ag_sib = {part: sem() for part in PARTS}

    def gather(step):
        part, name, *rest = step.split(".")
        if part == "small":
            small_steps[int(name)]()
            return
        ip, op, _, _ = axes(part)
        if name == "x" and rest[0] == "s":
            ref = slab(part, x, ip[0], op[0])
            remote(ref, ref, ag_sent[part][1], ag_x[part][0], xp).start()
        elif name == "x":
            await_arrival(ag_x[part][0], 1)
        elif name == "X":
            offsets = GROUPS[rest[0]][1]
            for o in STAGES[int(rest[1])]:
                whole = len(offsets) == 4
                for ref in [line(part, x, op[o])] if whole else [slab(part, x, ip[i], op[o]) for i in offsets]:
                    remote(ref, ref, ag_sent[part][1], ag_x[part][int(rest[1])], xp).start()
        elif name == "XR":
            await_arrival(ag_x[part][int(rest[0])], 4 * len(STAGES[int(rest[0])]))
        elif name == "sib":
            for o in STAGES[int(rest[1])]:
                ref = line(part, ox if int(rest[0]) else x, op[o])
                remote(ref, ref, ag_sent[part][2], ag_sib[part], sib).start()
        else:
            views, size, left, right = ag_rings[part][name]
            count = size * len(views)
            full, half = ag_sem[part, name]
            sent = ag_sent[part][0]
            if rest[0] == "start":
                for view in views:
                    remote(view(0), view(0), sent, full, right).start()
                    remote(view(0), view(0), sent, full, left).start()
            elif rest[0] == "mid":
                await_arrival(full, 2 * count)
                for view in views:
                    remote(view(3, 0), view(3, 0), sent, half, right).start()
                    remote(view(1, 1), view(1, 1), sent, half, left).start()
            else:
                await_arrival(half, count)

    spread = (
        lax.broadcasted_iota(jnp.int32, (16, 128), 1)
        == lax.broadcasted_iota(jnp.int32, (16, 128), 0) + 16 * (y * 2 + c)
    ).astype(F32)
    sm_y, sm_c, sm_z, sm_x = [(sem(), sem()) for _ in range(4)]

    cross = [(sem(), sem()) for _ in range(4)]
    seg_cross = remote(segs.at[0], segs.at[1], *cross[0], xp)
    cot_cross = remote(cotv.at[0], cotv.at[1], *cross[1], xp)
    act_cross = remote(act_out, act_hbm, *cross[2], xp)
    grad_cross = remote(grad_out, grad_hbm, *cross[3], xp)

    def small_one():
        segs[0] = jnp.broadcast_to(seg_ref[...].astype(F32), (8, ROWS))

        @pl.when(crossed)
        def _():
            seg_cross.start()

        sgb[...] = jnp.zeros_like(sgb)
        sgb[0:2, :] = gains_ref[...].astype(F32)
        sgb[2:12, :] = bias_ref[...].astype(F32)
        sb_y[0] = jnp.dot(sgb[...].astype(BF16), spread.astype(BF16), preferred_element_type=F32)
        for k in (1, 2, 3):
            small(sb_y.at[0], sb_y.at[k], sm_y, ys[k]).start()

    def small_two():
        rows = sb_y.at[pl.ds(1, 3)]
        small(rows, rows, sm_y, sib).wait_recv()
        sb_c[0] = sb_y[0] + sb_y[1] + sb_y[2] + sb_y[3]
        small(sb_c.at[0], sb_c.at[1], sm_c, sib).start()

    def small_three():
        small(sb_c.at[0], sb_c.at[1], sm_c, sib).wait_recv()
        sb_x[x, z] = sb_c[0] + sb_c[1]
        for k in (1, 2, 3):
            small(sb_x.at[x, z], sb_x.at[x, z], sm_z, zs[k]).start()

    def small_four():
        rows = sb_x.at[0, pl.ds(0, 3)]
        small(rows, rows, sm_z, sib).wait_recv()
        small(sb_x.at[x], sb_x.at[x], sm_x, xp).start()

    def small_five():
        small(sb_x.at[ox], sb_x.at[ox], sm_x, xp).wait_recv()
        for g in range(8):
            bf[:, g * 128 : (g + 1) * 128] = sb_x[g // 4, g % 4]
        qbias[:, 0:WIDTH] = bf[3:4, :]
        qbias[:, WIDTH : 2 * WIDTH] = jnp.zeros((1, WIDTH), F32)
        qbias[:, 2 * WIDTH :] = bf[4:5, :]

    def row(k):
        return bf[k : k + 1, :]

    def small_six():
        @pl.when(crossed)
        def _():
            seg_cross.wait()

        seg = jnp.broadcast_to(segs[rows_at][0:1], (ROWS, ROWS))
        qi = lax.broadcasted_iota(jnp.int32, (ROWS, ROWS), 0)
        ki = lax.broadcasted_iota(jnp.int32, (ROWS, ROWS), 1)
        allowed = (seg == seg.T) & (ki <= qi) & (lax.div(qi, 64) == lax.div(ki, 64))
        mask[...] = allowed.astype(F32)

    small_steps = {1: small_one, 2: small_two, 3: small_three, 4: small_four, 5: small_five, 6: small_six}

    for step in GATHER_ONE:
        gather(step)

    halves = [pl.ds(0, 512), pl.ds(512, 512)]
    handed_on = [remote(act_out.at[:, k], hb.at[:, k], sem(), sem(), other_section) for k in halves]
    handed_back = remote(grad_out, hb, sem(), sem(), other_section)
    tok_in.wait()
    cot_in.wait()

    @pl.when(sec == 0)
    def _():
        xin[...] = tokv[...].astype(F32)

    @pl.when(sec == 1)
    def _():
        for step in GATHER_TWO:
            gather(step)

        @pl.when(crossed)
        def _():
            cot_cross.start()

        for cp in handed_on:
            cp.wait_recv()
        xin[...] = hb[...].astype(F32)

    def norm(values, gain, shift):
        centre = values - jnp.mean(values, axis=-1, keepdims=True)
        rs = lax.rsqrt(jnp.mean(centre * centre, axis=-1, keepdims=True) + EPS)
        hat = centre * rs
        return hat, rs, (hat * gain + shift).astype(BF16)

    ex_sems = [(sem(), sem()) for _ in range(8)]

    def exchange(slot, src, dst):
        return remote(src, dst, *ex_sems[slot], sib)

    def from_sibling(part):
        await_arrival(ag_sib[part], 32)

    xh1[...], rs1[...], x1[0] = norm(xin[...], row(0), row(2))
    ex_first = exchange(0, x1.at[0], x1.at[1])
    ex_first.start()
    from_sibling("Be")
    from_sibling("Ce")

    def qkv_weights(k):
        return w[k, :, :, :, 0:3].reshape(1536, WIDTH)

    for k in range(2):
        cols = slice(1536 * k, 1536 * (k + 1))
        mixed = lax.dot_general(x1[0], qkv_weights(k), NT, preferred_element_type=F32)
        qkv[:, cols] = (mixed + qbias[:, cols]).astype(BF16)

    low_lanes = lax.broadcasted_iota(jnp.int32, (ROWS, 128), 1) < HEAD
    zero = jnp.zeros((ROWS, 128), BF16)

    def pair(base, hp):
        return slice(base + hp * 128, base + hp * 128 + 128)

    def lanes_of(e):
        return low_lanes if e == 0 else ~low_lanes

    raw = []
    for hp in range(8):
        q, k = qkv[:, pair(0, hp)], qkv[:, pair(WIDTH, hp)]
        for e in range(2):
            raw.append(lax.dot_general(jnp.where(lanes_of(e), q, zero), k, NT, preferred_element_type=F32))
    seen = mask[...] > 0.5
    soft = []
    for scores in raw:
        scores = jnp.where(seen, scores * 0.125, -1e30)
        ex = jnp.exp(scores - jnp.max(scores, axis=-1, keepdims=True))
        soft.append(ex * (1.0 / jnp.sum(ex, axis=-1, keepdims=True)))
    for hp in range(8):
        v = qkv[:, pair(2 * WIDTH, hp)]
        parts = []
        for e in range(2):
            probs[2 * hp + e] = soft[2 * hp + e]
            parts.append(jnp.dot(soft[2 * hp + e].astype(BF16), v, preferred_element_type=F32))
        x2[0, :, pair(0, hp)] = jnp.where(low_lanes, parts[0], parts[1]).astype(BF16)
    ex_att = exchange(1, x2.at[0], x2.at[1])
    ex_att.start()

    def proj_weights():
        return w[:, :, :, :, 3].reshape(WIDTH, WIDTH)

    xin[...] = xin[...] + (lax.dot_general(x2[0], proj_weights(), NT, preferred_element_type=F32) + row(5))
    xh2[...], rs2[...], x3[0] = norm(xin[...], row(1), row(6))
    ex_second = exchange(2, x3.at[0], x3.at[1])
    ex_second.start()

    @pl.when(sec == 0)
    def _():
        for step in GATHER_TWO:
            gather(step)

    from_sibling("A1")
    from_sibling("A2")

    def fc_weights(j):
        return w[j // 2, 2 * (j % 2) : 2 * (j % 2) + 2, :, :, 4:8].reshape(WIDTH, WIDTH)

    for j in range(4):
        pre = lax.dot_general(x3[0], fc_weights(j), NT, preferred_element_type=F32) + row(7 + j)
        square = pre * pre
        t = jnp.tanh(GC * (pre + 0.044715 * (square * pre)))
        half = 0.5 * (1.0 + t)
        x4[0, j] = (pre * half).astype(BF16)
        dgel[j] = half + (0.5 * GC) * pre * (1.0 - t * t) * (1.0 + 0.134145 * square)
    ex_act = exchange(3, x4.at[0], x4.at[1])
    ex_act.start()
    from_sibling("Bl")
    from_sibling("Cl")

    def wout_weights(j):
        return w[:, :, :, :, 8 + j].reshape(WIDTH, WIDTH)

    def hand_on(n):
        @pl.when(sec == 0)
        def _():
            handed_on[n].start()

    for n in range(2):
        cols = slice(512 * n, 512 * (n + 1))
        result = xin[:, cols] + row(11)[:, cols]
        for j in range(4):
            half = w[n, :, :, :, 8 + j].reshape(512, WIDTH)
            result = result + lax.dot_general(x4[0, j], half, NT, preferred_element_type=F32)
        act_out[:, cols] = result.astype(BF16)
        hand_on(n)

    act_done = pltpu.make_async_copy(act_out, act_hbm, tok_sem)
    grad_done = pltpu.make_async_copy(grad_out, grad_hbm, cot_sem)

    @pl.when(crossed)
    def _():
        act_cross.start()

    @pl.when(~crossed)
    def _():
        act_done.start()

    for part in PARTS:
        await_sent(ag_sent[part][0], 30 if X_FIRST[part] else 15)
        await_sent(ag_sent[part][1], 1 if X_FIRST[part] else 16)
        await_sent(ag_sent[part][2], 32)
    rows = sb_y.at[pl.ds(1, 3)]
    small(rows, rows, sm_y, sib).wait_send()
    small(sb_c.at[0], sb_c.at[1], sm_c, sib).wait_send()
    small(rows, rows, sm_z, sib).wait_send()
    small(sb_x.at[x], sb_x.at[x], sm_x, xp).wait_send()

    @pl.when(sec == 0)
    def _():
        handed_back.wait_recv()
        gf[...] = hb[...]

    @pl.when(sec == 1)
    def _():
        @pl.when(crossed)
        def _():
            cot_cross.wait()

        gf[...] = cotv[rows_at]

    def column_sum(values):
        return jnp.sum(values.astype(F32), axis=0, keepdims=True)

    sbw[...] = jnp.zeros_like(sbw)
    sbw[11:12, :] = column_sum(gf[...])
    s_out[...] = gf[...].T.reshape(2, 4, 4, 2, 1, 16, ROWS)

    def swap(slot, src, dst):
        return exchange(slot, src.at[:, :, :, oc], dst)

    ex_gf = swap(4, s_out, t_out)
    ex_gf.start()
    for j in range(4):
        d_act = jnp.dot(gf[...], wout_weights(j), preferred_element_type=F32)
        d_pre = (dgel[j] * d_act).astype(BF16)
        dpre[j] = d_pre
        sbw[7 + j : 8 + j, :] = column_sum(d_pre)
        s_fc[j // 2, 2 * (j % 2) : 2 * (j % 2) + 2] = d_pre.T.reshape(2, 4, 2, 4, 16, ROWS)
    ex_dpre = swap(5, s_fc, t_fc)
    ex_dpre.start()
    ex_dbr = swap(6, s_proj, t_proj)
    ex_dmix = swap(7, s_qkv, t_qkv)

    def lhs(mine, theirs, rows):
        return jnp.concatenate([mine.reshape(rows, ROWS), theirs.reshape(rows, ROWS)], axis=1)

    def product(left, right):
        return jnp.dot(left, right, preferred_element_type=F32).astype(BF16)

    def grads_out(xx):
        left = lhs(s_out[xx, :, :, c], t_out[xx], 256)
        for j in range(4):
            w[xx, :, :, oc, 8 + j] = product(left, x4[:, j].reshape(2 * ROWS, WIDTH)).reshape(4, 4, 16, WIDTH)

    def grads_fc(xx):
        for k in range(2):
            zz = slice(2 * k, 2 * k + 2)
            left = lhs(s_fc[xx, zz, :, c], t_fc[xx, zz], 512)
            w[xx, zz, :, c, 8:12] = product(left, x3[...].reshape(2 * ROWS, WIDTH)).reshape(2, 4, 4, 16, WIDTH)

    def grads_att(xx):
        left = lhs(s_proj[xx, :, :, c], t_proj[xx], 256)
        w[xx, :, :, c, 7] = product(left, x2[...].reshape(2 * ROWS, WIDTH)).reshape(4, 4, 16, WIDTH)
        for k in range(2):
            zz = slice(2 * k, 2 * k + 2)
            left = lhs(s_qkv[xx, zz, :, c], t_qkv[xx, zz], 384)
            w[xx, zz, :, c, 4:7] = product(left, x1[...].reshape(2 * ROWS, WIDTH)).reshape(2, 4, 3, 16, WIDTH)

    def compute(name):
        if name == "gout1":
            ex_gf.wait_recv()
            ex_act.wait_recv()
            grads_out(ox)
        elif name == "gout0":
            grads_out(x)
        elif name == "gfc1":
            ex_dpre.wait_recv()
            ex_second.wait_recv()
            grads_fc(ox)
        elif name == "gfc0":
            grads_fc(x)
        elif name == "gatt1":
            ex_first.wait_recv()
            ex_att.wait_recv()
            ex_dbr.wait_recv()
            ex_dmix.wait_recv()
            grads_att(ox)
        elif name == "gatt0":
            grads_att(x)
        elif name == "first":
            pl.when(sec == 0)(back_first)

    rs_rings = {part: rings_of(part, True) for part in PARTS}
    rs_sem = {(part, name): (sem(), sem()) for part in PARTS for name in rs_rings[part]}
    rs_sent = {part: (sem(), sem()) for part in PARTS}
    rs_x = {part: (sem(),) if X_FIRST[part] else (sem(), sem(), sem()) for part in PARTS}
    rs_at = {
        (part, name): arrivals(3 * rs_rings[part][name][1] * len(rs_rings[part][name][0]))
        for part in PARTS
        for name in rs_rings[part]
    }
    rs_x_at = {part: arrivals(1 if X_FIRST[part] else 16) for part in PARTS}

    def add(view, *terms, out=None):
        if len(view.shape) > 3:
            for k in range(view.shape[0]):
                add(view.at[k], *(term.at[k] for term in terms))
            return
        total = view[...].astype(F32)
        for term in terms:
            total = total + term[...].astype(F32)
        if out is None:
            view[...] = total.astype(BF16)
        else:
            out[...] = total

    def own_sum(part):
        return gsum.at[pl.ds(FIRST[part], 2)]

    def summing(step):
        part, name, *rest = step.split(".")
        if part == "small":
            small_steps[int(name)]()
            return
        if part == "comp":
            compute(name)
            return
        ip, op, _, _ = axes(part)
        if name == "x" and rest[0] == "s":
            buf = rbuf.at[rs_x_at[part]]
            remote(slab(part, ox, ip[0], op[0], None, True), buf, rs_sent[part][1], rs_x[part][0], xp).start()
        elif name == "x":
            await_arrival(rs_x[part][0], 1)
            add(slab(part, x, ip[0], op[0], None, True), rbuf.at[rs_x_at[part]], out=own_sum(part))
        elif name in ("X", "XR"):
            stage = int(rest[0])
            if name == "XR":
                await_arrival(rs_x[part][stage], 4 * len(STAGES[stage]))
            for o in STAGES[stage]:
                buf = rbuf.at[pl.ds(rs_x_at[part] + 4 * o, 4)]
                if name == "X":
                    ref = line(part, ox, op[o], None, True)
                    remote(ref, buf, rs_sent[part][1], rs_x[part][stage], xp).start()
                else:
                    add(line(part, x, op[o], None, True), buf)
        else:
            views, size, left, right = rs_rings[part][name]
            count = size * len(views)
            half, full = rs_sem[part, name]
            sent = rs_sent[part][0]

            def arrived(k):
                base = rs_at[part, name] + 3 * size * k
                if size == 1:
                    halves = [rbuf.at[base, pl.ds(0, 1)], rbuf.at[base, pl.ds(1, 1)]]
                    return halves + [rbuf.at[base + 1], rbuf.at[base + 2]]
                return [rbuf.at[pl.ds(base, 2)], rbuf.at[pl.ds(base + 2, 2)], rbuf.at[pl.ds(base + 4, 4)], rbuf.at[pl.ds(base + 8, 4)]]

            if rest[0] == "start":
                for k, view in enumerate(views):
                    remote(view(2, 0), arrived(k)[0], sent, half, right).start()
                    remote(view(2, 1), arrived(k)[1], sent, half, left).start()
            elif rest[0] == "mid":
                await_arrival(half, count)
                for k, view in enumerate(views):
                    add(view(1, 0), arrived(k)[0])
                    remote(view(1), arrived(k)[2], sent, full, right).start()
                    add(view(3, 1), arrived(k)[1])
                    remote(view(3), arrived(k)[3], sent, full, left).start()
            else:
                await_arrival(full, 2 * count)
                last = name == "in0" and not X_FIRST[part]
                for k, view in enumerate(views):
                    add(view(0), arrived(k)[2], arrived(k)[3], out=own_sum(part) if last else None)

    sm_core, sm_xs, sm_zs, sm_ys = [(sem(), sem()) for _ in range(4)]

    def small_seven():
        for g in range(8):
            sr[g // 4, g % 4] = sbw[:, g * 128 : (g + 1) * 128]
        small(sr, sr_c, sm_core, sib).start()

    def small_eight():
        small(sr, sr_c, sm_core, sib).wait()
        sr[...] = sr[...] + sr_c[...]
        small(sr.at[ox], sr_x, sm_xs, xp).start()

    def small_nine():
        small(sr.at[ox], sr_x, sm_xs, xp).wait_recv()
        sr[x] = sr[x] + sr_x[...]
        for k in (1, 2, 3):
            small(sr.at[x, zp[k]], sr_z.at[k - 1], sm_zs, zs[k]).start()

    def small_ten():
        small(sr_z, sr_z, sm_zs, sib).wait_recv()
        sr_y[0] = sr[x, z] + sr_z[0] + sr_z[1] + sr_z[2]
        for k in (1, 2, 3):
            small(sr_y.at[0], sr_y.at[k], sm_ys, ys[k]).start()

    def small_eleven():
        rows = sr_y.at[pl.ds(1, 3)]
        small(rows, rows, sm_ys, sib).wait_recv()
        total = sr_y[0] + sr_y[1] + sr_y[2] + sr_y[3]
        picked = lax.dot_general(total, spread, NT, preferred_element_type=F32, precision=lax.Precision.HIGHEST)
        ggain_out[...] = picked[0:2, :]
        for k in range(10):
            gbias_out[k] = picked[2 + k : 3 + k, :]

    small_steps.update({7: small_seven, 8: small_eight, 9: small_nine, 10: small_ten, 11: small_eleven})

    @pl.when(sec == 0)
    def _():
        for step in SUM_ONE:
            summing(step)

    d_second = jnp.zeros((ROWS, WIDTH), F32)
    for j in range(4):
        d_second = d_second + jnp.dot(dpre[j], fc_weights(j), preferred_element_type=F32)

    def norm_back(d_out, hat, rs, gain):
        d_hat = d_out * gain
        mean_one = jnp.mean(d_hat, axis=-1, keepdims=True)
        mean_two = jnp.mean(d_hat * hat, axis=-1, keepdims=True)
        return rs * (d_hat - mean_one - hat * mean_two)

    sbw[1:2, :] = column_sum(d_second * xh2[...])
    sbw[6:7, :] = column_sum(d_second)
    dmid[...] = gf[...].astype(F32) + norm_back(d_second, xh2[...], rs2[...], row(1))
    dbr[...] = dmid[...].astype(BF16)
    sbw[5:6, :] = column_sum(dbr[...])
    s_proj[...] = dbr[...].T.reshape(2, 4, 4, 2, 1, 16, ROWS)
    ex_dbr.start()

    @pl.when(sec == 0)
    def _():
        for step in SUM_TWO:
            summing(step)

    datt[...] = jnp.dot(dbr[...], proj_weights(), preferred_element_type=F32).astype(BF16)
    d_probs, masked_da = [], []
    for hp in range(8):
        da, v = datt[:, pair(0, hp)], qkv[:, pair(2 * WIDTH, hp)]
        for e in range(2):
            masked_da.append(jnp.where(lanes_of(e), da, zero))
            d_probs.append(lax.dot_general(masked_da[-1], v, NT, preferred_element_type=F32))
    d_scores = []
    for h in range(16):
        p, dp_ = probs[h], d_probs[h]
        d_scores.append((p * (dp_ - jnp.sum(dp_ * p, axis=-1, keepdims=True))).astype(BF16))
    for hp in range(8):
        q, k = qkv[:, pair(0, hp)], qkv[:, pair(WIDTH, hp)]
        dq, dk, dv = [], [], []
        for e in range(2):
            h = 2 * hp + e
            dv.append(jnp.dot(probs[h].astype(BF16).T, masked_da[h], preferred_element_type=F32))
            dq.append(jnp.dot(d_scores[h], k, preferred_element_type=F32))
            dk.append(jnp.dot(d_scores[h].T, jnp.where(lanes_of(e), q, zero), preferred_element_type=F32))
        dmix[:, pair(0, hp)] = (jnp.where(low_lanes, dq[0], dq[1]) * 0.125).astype(BF16)
        dmix[:, pair(WIDTH, hp)] = ((dk[0] + dk[1]) * 0.125).astype(BF16)
        dmix[:, pair(2 * WIDTH, hp)] = (dv[0] + dv[1]).astype(BF16)
    for k in range(2):
        s_qkv[k] = dmix[:, 1536 * k : 1536 * (k + 1)].T.reshape(4, 4, 2, 3, 16, ROWS)
    ex_dmix.start()
    sbw[3:4, :] = column_sum(dmix[:, 0:WIDTH])
    sbw[4:5, :] = column_sum(dmix[:, 2 * WIDTH :])

    def back_first():
        d_first = jnp.dot(dmix[:, 0:1536], qkv_weights(0), preferred_element_type=F32)
        d_first = d_first + jnp.dot(dmix[:, 1536:], qkv_weights(1), preferred_element_type=F32)
        sbw[0:1, :] = column_sum(d_first * xh1[...])
        sbw[2:3, :] = column_sum(d_first)
        grad_out[...] = (dmid[...] + norm_back(d_first, xh1[...], rs1[...], row(0))).astype(BF16)

        @pl.when(crossed)
        def _():
            grad_cross.start()

        @pl.when(~crossed)
        def _():
            grad_done.start()

    @pl.when(sec == 1)
    def _():
        back_first()
        handed_back.start()
        for step in SUM_ONE + SUM_TWO:
            summing(step)

    for step in SUM_THREE:
        summing(step)

    done = [
        pltpu.make_async_copy(gsum.at[pl.ds(0, 3)], gqkv_hbm, own_sem),
        pltpu.make_async_copy(gsum.at[pl.ds(3, 1)], gproj_hbm, own_sem),
        pltpu.make_async_copy(gsum.at[pl.ds(4, 4)], gfc_hbm, own_sem),
    ] + [
        pltpu.make_async_copy(gsum.at[8 + j], gwout_hbm.at[:, pl.ds(1024 * j, 1024)], own_sem) for j in range(4)
    ]
    for cp in done:
        cp.start()
    small_done = [
        pltpu.make_async_copy(ggain_out, ggain_hbm, sem()),
        pltpu.make_async_copy(gbias_out, gbias_hbm, sem()),
    ]
    for cp in small_done:
        cp.start()

    for part in PARTS:
        await_sent(rs_sent[part][0], 30 if X_FIRST[part] else 15)
        await_sent(rs_sent[part][1], 1 if X_FIRST[part] else 16)
    for cp in (ex_first, ex_att, ex_second, ex_act, ex_gf, ex_dpre, ex_dbr, ex_dmix):
        cp.wait_send()
    small(sr.at[ox], sr_x, sm_xs, xp).wait_send()
    small(sr_z, sr_z, sm_zs, sib).wait_send()
    rows = sr_y.at[pl.ds(1, 3)]
    small(rows, rows, sm_ys, sib).wait_send()

    @pl.when(sec == 0)
    def _():
        for cp in handed_on:
            cp.wait_send()

    @pl.when(sec == 1)
    def _():
        handed_back.wait_send()

    @pl.when(crossed)
    def _():
        act_cross.wait()
        grad_cross.wait()

    @pl.when(~crossed)
    def _():
        act_done.wait()
        grad_done.wait()

    pltpu.make_async_copy(gsum, gsum, own_sem).wait()
    for cp in small_done:
        cp.wait()
    if (taken[0], taken[1]) != (SEMAPHORES, ARRIVALS):
        raise ValueError(taken)


SEMAPHORES = 195
ARRIVALS = 186


def move(*refs):
    count = len(refs) // 3
    sems = refs[-1]
    into = [pltpu.make_async_copy(refs[k], refs[2 * count + k], sems.at[0, k]) for k in range(count)]
    out = [pltpu.make_async_copy(refs[2 * count + k], refs[count + k], sems.at[1, k]) for k in range(count)]
    for cp in into:
        cp.start()
    for k in range(count):
        into[k].wait()
        out[k].start()
    for cp in out:
        cp.wait()


def local(tokens, segment_ids, gains, biases, w_qkv, w_proj, w_fc, w_out, cotangent):
    vmem = pl.BlockSpec(memory_space=pltpu.VMEM)
    hbm = pl.BlockSpec(memory_space=pl.ANY)

    def shape(*dims, dtype=F32):
        return jax.ShapeDtypeStruct(dims, dtype)

    def v(*dims, dtype=BF16):
        return pltpu.VMEM(dims, dtype)

    scratch = [
        v(2, 4, 4, 2, 12, 16, WIDTH), v(ARRIVALS, 2, 16, WIDTH),
        v(ROWS, WIDTH), v(ROWS, WIDTH), v(12, 16, WIDTH, dtype=F32), v(2, 16, dtype=F32), v(10, 1, 16, dtype=F32),
        v(ROWS, WIDTH), v(2, ROWS, WIDTH), v(2, 8, ROWS, dtype=F32),
        v(ROWS, WIDTH, dtype=F32), v(2, ROWS, WIDTH), v(2, ROWS, WIDTH), v(2, ROWS, WIDTH), v(2, 4, ROWS, WIDTH),
        v(ROWS, 3 * WIDTH), v(16, ROWS, ROWS, dtype=F32), v(ROWS, WIDTH, dtype=F32), v(ROWS, WIDTH, dtype=F32),
        v(ROWS, 1, dtype=F32), v(ROWS, 1, dtype=F32), v(4, ROWS, WIDTH, dtype=F32), v(ROWS, WIDTH),
        v(4, ROWS, WIDTH), v(ROWS, WIDTH), v(ROWS, WIDTH), v(ROWS, 3 * WIDTH), v(ROWS, WIDTH, dtype=F32),
        v(ROWS, ROWS, dtype=F32), v(1, 3 * WIDTH, dtype=F32),
        v(16, WIDTH, dtype=F32), v(16, 16, dtype=F32), v(4, 16, 128, dtype=F32), v(2, 16, 128, dtype=F32),
        v(2, 4, 16, 128, dtype=F32), v(16, WIDTH, dtype=F32), v(2, 4, 16, 128, dtype=F32),
        v(2, 4, 16, 128, dtype=F32), v(4, 16, 128, dtype=F32), v(3, 16, 128, dtype=F32), v(4, 16, 128, dtype=F32),
        v(2, 4, 4, 2, 1, 16, ROWS), v(2, 4, 4, 2, 4, 16, ROWS), v(2, 4, 4, 2, 1, 16, ROWS), v(2, 4, 4, 2, 3, 16, ROWS),
        v(2, 4, 4, 1, 16, ROWS), v(2, 4, 4, 4, 16, ROWS), v(2, 4, 4, 1, 16, ROWS), v(2, 4, 4, 3, 16, ROWS),
        v(ROWS, WIDTH),
        pltpu.SemaphoreType.DMA((SEMAPHORES,)),
    ]
    results = (
        shape(ROWS, WIDTH, dtype=BF16), shape(ROWS, WIDTH, dtype=BF16), shape(2, 16), shape(10, 1, 16),
        shape(3, 16, WIDTH), shape(1, 16, WIDTH), shape(4, 16, WIDTH), shape(16, 4 * WIDTH),
    )
    out = pl.pallas_call(
        kernel,
        out_shape=results,
        in_specs=[vmem, vmem, vmem] + [hbm] * 6,
        out_specs=(hbm,) * 8,
        scratch_shapes=scratch,
        compiler_params=pltpu.CompilerParams(
            collective_id=0, has_side_effects=True, vmem_limit_bytes=63 * 2**20
        ),
        name="relay",
    )(
        segment_ids.reshape(1, ROWS),
        gains[0],
        biases[0],
        tokens,
        w_qkv[0].T.reshape(3, 16, WIDTH),
        w_proj[0].T.reshape(1, 16, WIDTH),
        w_fc[0].T.reshape(4, 16, WIDTH),
        w_out[0].T,
        cotangent,
    )
    out = pl.pallas_call(
        move,
        out_shape=results,
        in_specs=[hbm] * 8,
        out_specs=(hbm,) * 8,
        scratch_shapes=[pltpu.VMEM(r.shape, r.dtype) for r in results] + [pltpu.SemaphoreType.DMA((2, 8))],
        name="move",
    )(*out)
    activations, input_grads, g_gains, g_biases, g_qkv, g_proj, g_fc, g_out = out
    return (
        activations[None],
        input_grads[None],
        g_gains[None],
        g_biases.transpose(1, 0, 2),
        g_qkv.reshape(48, WIDTH).T[None],
        g_proj.reshape(16, WIDTH).T[None],
        g_fc.reshape(64, WIDTH).T[None],
        g_out.T[None],
    )


def solution(mesh):
    weight = P("section", None, "dp")
    rows = P("section", "dp", None)
    return jax.shard_map(
        local,
        mesh=mesh,
        in_specs=(P("dp", None), P("dp")) + (weight,) * 6 + (P("dp", None),),
        out_specs=(rows, rows) + (weight,) * 6,
        check_vma=False,
    )
```

```python
import jax
import jax.numpy as jnp
from jax import lax
from jax.experimental import pallas as pl
from jax.experimental.pallas import tpu as pltpu
from jax.sharding import PartitionSpec as P

MESH = pl.DeviceIdType.MESH
F32 = jnp.float32
BF16 = jnp.bfloat16
EPS = 1e-05
ROWS = 128
WIDTH = 1024
HEAD = 64
GC = 0.7978845608028654
NT = (((1,), (1,)), ((), ()))

PARTS = ("Be", "Ce", "A1", "A2", "Bl", "Cl")
FIRST = {"Be": 0, "Ce": 2, "A1": 4, "A2": 6, "Bl": 8, "Cl": 10}
INNER_IS_Y = {"Be": False, "Ce": True, "A1": True, "A2": False, "Bl": False, "Cl": True}
X_FIRST = {"Be": True, "Ce": True, "A1": False, "A2": False, "Bl": True, "Cl": True}
GROUPS = {
    "g0": (0, (0,)), "g1": (1, (0,)), "g2": (0, (1, 3)), "g3": (0, (2,)), "g4": (1, (1, 3)), "g5": (1, (2,)),
    "gA": (0, (0, 1, 2, 3)), "gB": (1, (0, 1, 2, 3)),
}
FINE = ("g0", "g1", "g2", "g3", "g4", "g5")
COARSE = ("gA", "gB")
GATHER_GROUPS = {"Be": COARSE, "Ce": COARSE, "A1": FINE, "A2": FINE, "Bl": COARSE, "Cl": COARSE}
SUM_GROUPS = {"Be": COARSE, "Ce": COARSE, "A1": COARSE, "A2": COARSE, "Bl": COARSE, "Cl": COARSE}
STAGES = ((0,), (1, 3), (2,))
SUM_AT = {"Be": (0, 4), "Ce": (0, 6), "A1": (0, 8), "A2": (0, 10), "Bl": (1, 8), "Cl": (1, 10)}

GATHER_ONE = [
    "Ce.x.s", "A2.in0.start", "A1.in0.start", "A2.g0.start", "A2.X.g0.0", "Be.in0.start", "Bl.in0.start",
    "Ce.in0.start", "A1.g0.start", "Cl.x.s", "Cl.in0.start", "A1.in0.mid", "Ce.x.r", "Bl.x.s", "small.1", "Be.x.s",
    "A2.g0.mid", "Be.in0.mid", "A2.in0.mid", "A1.g2.start", "A2.X.g2.0", "Ce.in1.start", "A2.g2.start", "A2.X.g0.1",
    "A1.in0.end", "Be.in0.end", "Bl.x.r", "Ce.in0.mid", "A1.sib.0.0", "Be.x.r", "Be.in1.start", "A1.g3.start",
    "Bl.in1.start", "Ce.in1.mid", "A1.X.g2.0", "Cl.x.r", "Bl.in0.mid", "Be.gA.start", "Ce.in0.end", "A1.g0.mid",
    "Be.in1.mid", "A1.X.g3.0", "small.2", "A1.g3.mid", "A2.in0.end", "A2.X.g3.0", "A2.g3.start", "Ce.in1.end",
    "Ce.gA.start", "A1.g0.end", "A1.X.g0.0", "A2.sib.0.0", "Bl.in1.mid", "Cl.in1.start", "Be.in1.end", "Cl.in0.mid",
    "Be.gB.start", "A1.g2.mid", "A1.g3.end", "A1.X.g2.1", "A1.X.g0.1", "Ce.gB.start", "A2.g3.mid", "small.3",
    "A1.XR.0", "Be.sib.1.0", "A2.XR.0", "Be.gA.mid", "Be.sib.0.0", "A1.X.g3.1", "A2.g2.mid", "Ce.sib.0.0",
    "A1.X.g3.2", "Cl.in0.end", "Bl.in0.end", "A2.X.g3.1", "A2.sib.0.1", "Bl.sib.0.0", "A1.sib.1.0", "Cl.in1.mid",
    "Be.gB.mid", "Ce.gA.mid", "Be.sib.0.1", "A1.sib.0.1", "Ce.gB.mid", "small.4", "A2.X.g2.1", "A2.g2.end",
    "A1.X.g0.2", "Bl.in1.end", "Ce.sib.1.0", "Be.sib.1.1", "Ce.sib.1.1", "Ce.sib.0.1", "Cl.gA.start", "A2.g3.end",
    "Bl.gA.start", "A1.XR.1", "Ce.gA.end", "Ce.gB.end", "A1.g2.end", "Be.gA.end", "Be.gB.end", "A1.X.g2.2",
    "A2.X.g2.2", "Ce.sib.0.2", "small.5", "Bl.gB.start", "Cl.in1.end", "Cl.sib.1.0", "A2.g0.end", "Be.sib.1.2",
    "Cl.gB.start", "Ce.sib.1.2", "Cl.sib.0.0", "A2.X.g3.2", "Be.sib.0.2", "A2.sib.1.0", "A2.X.g0.2", "A1.sib.1.1",
    "A2.XR.1", "Cl.gA.mid", "Bl.gA.mid", "Bl.sib.0.1", "A2.sib.0.2", "Bl.sib.1.0", "Cl.sib.0.1", "A2.sib.1.1",
    "small.6",
]

GATHER_TWO = [
    "Cl.gB.mid", "A1.sib.0.2", "Cl.sib.1.1", "Bl.gB.mid", "A1.XR.2", "A1.sib.1.2", "A2.XR.2", "Bl.gA.end",
    "A2.sib.1.2", "Cl.gA.end", "Cl.sib.0.2", "Bl.sib.1.1", "Cl.gB.end", "Cl.sib.1.2", "Bl.sib.0.2", "Bl.gB.end",
    "Bl.sib.1.2",
]

SUM_ONE = [
    "comp.gout1", "comp.gout0", "Cl.gA.start", "Bl.gB.start", "Cl.gB.start", "Bl.gA.start", "comp.gfc1", "A1.X.2",
    "A2.X.2",
]

SUM_TWO = [
    "Bl.gB.mid", "Cl.gA.mid", "comp.gfc0", "Cl.gB.mid", "Bl.gA.mid",
]

SUM_THREE = [
    "A2.X.1", "Bl.gB.end", "comp.gatt1", "A1.X.1", "Ce.gB.start", "comp.gatt0", "Be.gB.start", "Ce.gA.start",
    "Be.gA.start", "Cl.gB.end", "Ce.gB.mid", "Be.gB.mid", "Cl.in1.start", "Bl.gA.end", "A2.XR.2", "Bl.in1.start",
    "A1.XR.2", "A1.gA.start", "A1.X.0", "Bl.in0.start", "Be.gA.mid", "Be.gB.end", "Be.in1.start", "Ce.gB.end",
    "Ce.in1.start", "A2.gA.start", "Cl.gA.end", "A2.XR.1", "Bl.in1.mid", "A2.X.0", "Cl.in1.mid", "Cl.in0.start",
    "Ce.gA.mid", "Be.gA.end", "A1.XR.1", "A1.gA.mid", "Ce.in1.mid", "comp.first", "small.7", "A2.gA.mid",
    "Be.in0.start", "Be.in1.mid", "A1.XR.0", "Ce.in1.end", "Ce.x.s", "small.8", "Bl.in0.mid", "Ce.gA.end",
    "Bl.in1.end", "Cl.in1.end", "Ce.in0.start", "A1.gA.end", "A1.in0.start", "small.9", "Cl.in0.mid", "Bl.x.s",
    "Cl.x.s", "A2.XR.0", "A2.gA.end", "A2.in0.start", "Be.in1.end", "small.10", "Ce.in0.mid", "Be.x.s", "Be.in0.mid",
    "A1.in0.mid", "A2.in0.mid", "Bl.in0.end", "Cl.in0.end", "small.11", "Be.in0.end", "Ce.in0.end", "Be.x.r",
    "Bl.x.r", "Cl.x.r", "A1.in0.end", "Ce.x.r", "A2.in0.end",
]


def remote(src, dst, ssem, rsem, target):
    return pltpu.make_async_remote_copy(
        src_ref=src, dst_ref=dst, send_sem=ssem, recv_sem=rsem, device_id=target, device_id_type=MESH
    )


def kernel(
    seg_ref, gains_ref, bias_ref, tok_ref, qkv_ref, proj_ref, fc_ref, wout_ref, cot_ref,
    act_hbm, grad_hbm, ggain_hbm, gbias_hbm, gqkv_hbm, gproj_hbm, gfc_hbm, gwout_hbm,
    w, rbuf, act_out, grad_out, gsum, ggain_out, gbias_out, tokv, cotv, segs,
    xin, x1, x2, x3, x4, qkv, probs, xh1, xh2, rs1, rs2, dgel, gf, dpre, dbr, datt, dmix, dmid, mask, qbias,
    bf, sgb, sb_y, sb_c, sb_x, sbw, sr, sr_c, sr_x, sr_z, sr_y,
    s_out, s_fc, s_proj, s_qkv, t_out, t_fc, t_proj, t_qkv, hb, turned, room, sems,
):
    sec = lax.axis_index("section")
    dp = lax.axis_index("dp")
    c = lax.rem(dp, 2)
    y = lax.rem(lax.div(dp, 2), 4)
    z = lax.rem(lax.div(dp, 8), 4)
    x = lax.div(dp, 32)
    ox, oc = 1 - x, 1 - c
    yp = [lax.rem(y + k, 4) for k in range(4)]
    zp = [lax.rem(z + k, 4) for k in range(4)]

    def at(px, pz, py, pc):
        return (sec, ((px * 4 + pz) * 4 + py) * 2 + pc)

    ys = [at(x, z, yp[k], c) for k in range(4)]
    zs = [at(x, zp[k], y, c) for k in range(4)]
    xp = at(ox, z, y, c)
    sib = at(x, z, y, oc)
    other_section = (1 - sec, ((lax.rem(x + c, 2) * 4 + z) * 4 + y) * 2 + c)
    crossed = (sec == 1) & (c == 1)
    rows_at = sec * c

    taken = [0, 0]

    def sem():
        taken[0] += 1
        return sems.at[taken[0] - 1]

    def arrivals(slabs):
        taken[1] += slabs
        return taken[1] - slabs

    barrier = pltpu.get_barrier_semaphore()
    partners = ys[1:] + zs[1:] + [xp, sib, other_section]
    for target in partners:
        pl.semaphore_signal(barrier, 1, device_id=target, device_id_type=MESH)
    own = w.at[x, z, y, c]
    own_sem, tok_sem, cot_sem = sem(), sem(), sem()
    pltpu.make_async_copy(qkv_ref, own.at[pl.ds(0, 3)], own_sem).start()
    pltpu.make_async_copy(proj_ref, own.at[pl.ds(3, 1)], own_sem).start()
    pltpu.make_async_copy(fc_ref, own.at[pl.ds(4, 4)], own_sem).start()
    for j in range(4):
        pltpu.make_async_copy(wout_ref.at[:, pl.ds(1024 * j, 1024)], own.at[8 + j], own_sem).start()
    tok_in = pltpu.make_async_copy(tok_ref, tokv, tok_sem)
    cot_in = pltpu.make_async_copy(cot_ref, cotv.at[0], cot_sem)
    tok_in.start()
    cot_in.start()
    pl.semaphore_wait(barrier, len(partners))
    pltpu.make_async_copy(own, own, own_sem).wait()

    def slab(part, xx, i, o, half=None, summing=False):
        core, base = c, FIRST[part]
        if summing:
            core, base = (oc if SUM_AT[part][0] else c), SUM_AT[part][1]
        pieces = pl.ds(base, 2) if half is None else pl.ds(base + half, 1)
        pz, py = (o, i) if INNER_IS_Y[part] else (i, o)
        return w.at[xx, pz, py, core, pieces]

    def bytes_of(count):
        two = pl.ds(0, 2)
        return {
            1: w.at[0, 0, 0, 0, two],
            2: w.at[0, 0, two, 0, two],
            4: w.at[0, 0, :, 0, two],
            8: w.at[0, two, :, 0, two],
            15: w.at[0, 0, pl.ds(0, 3), 0, pl.ds(0, 10)],
            16: w.at[0, :, :, 0, two],
            30: w.at[0, two, pl.ds(0, 3), 0, pl.ds(0, 10)],
            32: w.at[:, :, :, 0, two],
        }[count]

    def await_arrival(which, count):
        ref = bytes_of(count)
        remote(ref, ref, which, which, sib).wait_recv()

    def await_sent(which, count):
        ref = bytes_of(count)
        remote(ref, ref, which, which, sib).wait_send()

    def axes(part):
        return (yp, zp, ys, zs) if INNER_IS_Y[part] else (zp, yp, zs, ys)

    def line(part, xx, o, half=None, summing=False):
        core, base = c, FIRST[part]
        if summing:
            core, base = (oc if SUM_AT[part][0] else c), SUM_AT[part][1]
        inner = slice(None) if half is None else pl.ds(2 * half, 2)
        pz, py = (o, inner) if INNER_IS_Y[part] else (inner, o)
        return w.at[xx, pz, py, core, pl.ds(base, 2)]

    def rings_of(part, summing):
        ip, op, idev, odev = axes(part)
        found = {}

        def along_inner(xx):
            return lambda j, half=None: slab(part, xx, ip[j], op[0], half, summing)

        def along_outer(xx, i):
            return lambda j, half=None: slab(part, xx, ip[i], op[j], half, summing)

        def along_line(xx):
            return lambda j, half=None: line(part, xx, op[j], half, summing)

        for other in (0, 1) if X_FIRST[part] else (0,):
            found[f"in{other}"] = ([along_inner(ox if other else x)], 1, idev[3], idev[1])
        for g in (SUM_GROUPS if summing else GATHER_GROUPS)[part]:
            other, offsets = GROUPS[g]
            if X_FIRST[part] or not other:
                xx = ox if other else x
                if len(offsets) == 4:
                    found[g] = ([along_line(xx)], 4, odev[3], odev[1])
                else:
                    found[g] = ([along_outer(xx, i) for i in offsets], 1, odev[3], odev[1])
        return found

    def small(src, dst, sems_of, target):
        return remote(src, dst, sems_of[0], sems_of[1], target)

    ag_rings = {part: rings_of(part, False) for part in PARTS}
    ag_sem = {(part, name): (sem(), sem()) for part in PARTS for name in ag_rings[part]}
    ag_sent = {part: (sem(), sem(), sem()) for part in PARTS}
    ag_x = {part: (sem(),) if X_FIRST[part] else (sem(), sem(), sem()) for part in PARTS}
    ag_sib = {part: sem() for part in PARTS}

    def gather(step):
        part, name, *rest = step.split(".")
        if part == "small":
            small_steps[int(name)]()
            return
        ip, op, _, _ = axes(part)
        if name == "x" and rest[0] == "s":
            ref = slab(part, x, ip[0], op[0])
            remote(ref, ref, ag_sent[part][1], ag_x[part][0], xp).start()
        elif name == "x":
            await_arrival(ag_x[part][0], 1)
        elif name == "X":
            offsets = GROUPS[rest[0]][1]
            for o in STAGES[int(rest[1])]:
                whole = len(offsets) == 4
                for ref in [line(part, x, op[o])] if whole else [slab(part, x, ip[i], op[o]) for i in offsets]:
                    remote(ref, ref, ag_sent[part][1], ag_x[part][int(rest[1])], xp).start()
        elif name == "XR":
            await_arrival(ag_x[part][int(rest[0])], 4 * len(STAGES[int(rest[0])]))
        elif name == "sib":
            for o in STAGES[int(rest[1])]:
                ref = line(part, ox if int(rest[0]) else x, op[o])
                remote(ref, ref, ag_sent[part][2], ag_sib[part], sib).start()
        else:
            views, size, left, right = ag_rings[part][name]
            count = size * len(views)
            full, half = ag_sem[part, name]
            sent = ag_sent[part][0]
            if rest[0] == "start":
                for view in views:
                    remote(view(0), view(0), sent, full, right).start()
                    remote(view(0), view(0), sent, full, left).start()
            elif rest[0] == "mid":
                await_arrival(full, 2 * count)
                for view in views:
                    remote(view(3, 0), view(3, 0), sent, half, right).start()
                    remote(view(1, 1), view(1, 1), sent, half, left).start()
            else:
                await_arrival(half, count)

    spread = (
        lax.broadcasted_iota(jnp.int32, (16, 128), 1)
        == lax.broadcasted_iota(jnp.int32, (16, 128), 0) + 16 * (y * 2 + c)
    ).astype(F32)
    sm_y, sm_c, sm_z, sm_x = [(sem(), sem()) for _ in range(4)]

    cross = [(sem(), sem()) for _ in range(4)]
    seg_cross = remote(segs.at[0], segs.at[1], *cross[0], xp)
    cot_cross = remote(cotv.at[0], cotv.at[1], *cross[1], xp)
    act_cross = remote(act_out, act_hbm, *cross[2], xp)
    grad_cross = remote(grad_out, grad_hbm, *cross[3], xp)

    def small_one():
        segs[0] = jnp.broadcast_to(seg_ref[...].astype(F32), (8, ROWS))

        @pl.when(crossed)
        def _():
            seg_cross.start()

        sgb[...] = jnp.zeros_like(sgb)
        sgb[0:2, :] = gains_ref[...].astype(F32)
        sgb[2:12, :] = bias_ref[...].astype(F32)
        sb_y[0] = jnp.dot(sgb[...].astype(BF16), spread.astype(BF16), preferred_element_type=F32)
        for k in (1, 2, 3):
            small(sb_y.at[0], sb_y.at[k], sm_y, ys[k]).start()

    def small_two():
        rows = sb_y.at[pl.ds(1, 3)]
        small(rows, rows, sm_y, sib).wait_recv()
        sb_c[0] = sb_y[0] + sb_y[1] + sb_y[2] + sb_y[3]
        small(sb_c.at[0], sb_c.at[1], sm_c, sib).start()

    def small_three():
        small(sb_c.at[0], sb_c.at[1], sm_c, sib).wait_recv()
        sb_x[x, z] = sb_c[0] + sb_c[1]
        for k in (1, 2, 3):
            small(sb_x.at[x, z], sb_x.at[x, z], sm_z, zs[k]).start()

    def small_four():
        rows = sb_x.at[0, pl.ds(0, 3)]
        small(rows, rows, sm_z, sib).wait_recv()
        small(sb_x.at[x], sb_x.at[x], sm_x, xp).start()

    def small_five():
        small(sb_x.at[ox], sb_x.at[ox], sm_x, xp).wait_recv()
        for g in range(8):
            bf[:, g * 128 : (g + 1) * 128] = sb_x[g // 4, g % 4]
        qbias[:, 0:WIDTH] = bf[3:4, :]
        qbias[:, WIDTH : 2 * WIDTH] = jnp.zeros((1, WIDTH), F32)
        qbias[:, 2 * WIDTH :] = bf[4:5, :]

    def row(k):
        return bf[k : k + 1, :]

    def small_six():
        @pl.when(crossed)
        def _():
            seg_cross.wait()

        seg = jnp.broadcast_to(segs[rows_at][0:1], (ROWS, ROWS))
        qi = lax.broadcasted_iota(jnp.int32, (ROWS, ROWS), 0)
        ki = lax.broadcasted_iota(jnp.int32, (ROWS, ROWS), 1)
        allowed = (seg == seg.T) & (ki <= qi) & (lax.div(qi, 64) == lax.div(ki, 64))
        mask[...] = allowed.astype(F32)

    small_steps = {1: small_one, 2: small_two, 3: small_three, 4: small_four, 5: small_five, 6: small_six}

    for step in GATHER_ONE:
        gather(step)

    def from_sibling(part):
        await_arrival(ag_sib[part], 32)

    def fc_weights(j):
        return w[j // 2, 2 * (j % 2) : 2 * (j % 2) + 2, :, :, 4:8].reshape(WIDTH, WIDTH)

    def wout_weights(j):
        return w[:, :, :, :, 8 + j].reshape(WIDTH, WIDTH)

    halves = [pl.ds(0, 512), pl.ds(512, 512)]
    handed_on = [remote(act_out.at[:, k], hb.at[:, k], sem(), sem(), other_section) for k in halves]
    handed_back = remote(grad_out, hb, sem(), sem(), other_section)
    tok_in.wait()
    cot_in.wait()

    @pl.when(sec == 0)
    def _():
        xin[...] = tokv[...].astype(F32)

    @pl.when(sec == 1)
    def _():
        for step in GATHER_TWO:
            gather(step)

        @pl.when(crossed)
        def _():
            cot_cross.start()

        for part in PARTS:
            from_sibling(part)
        for j in range(4):
            rbuf[32 * j : 32 * j + 32] = wout_weights(j).T.reshape(32, 2, 16, WIDTH)
        rbuf[128:160] = fc_weights(0).T.reshape(32, 2, 16, WIDTH)
        for j in range(1, 4):
            turned[j - 1] = fc_weights(j).T
        for cp in handed_on:
            cp.wait_recv()
        xin[...] = hb[...].astype(F32)

    def norm(values, gain, shift):
        centre = values - jnp.mean(values, axis=-1, keepdims=True)
        rs = lax.rsqrt(jnp.mean(centre * centre, axis=-1, keepdims=True) + EPS)
        hat = centre * rs
        return hat, rs, (hat * gain + shift).astype(BF16)

    ex_sems = [(sem(), sem()) for _ in range(8)]

    def exchange(slot, src, dst):
        return remote(src, dst, *ex_sems[slot], sib)

    xh1[...], rs1[...], x1[0] = norm(xin[...], row(0), row(2))
    ex_first = exchange(0, x1.at[0], x1.at[1])
    ex_first.start()

    @pl.when(sec == 0)
    def _():
        from_sibling("Be")
        from_sibling("Ce")

    def qkv_weights(k):
        return w[k, :, :, :, 0:3].reshape(1536, WIDTH)

    for k in range(2):
        cols = slice(1536 * k, 1536 * (k + 1))
        mixed = lax.dot_general(x1[0], qkv_weights(k), NT, preferred_element_type=F32)
        qkv[:, cols] = (mixed + qbias[:, cols]).astype(BF16)

    low_lanes = lax.broadcasted_iota(jnp.int32, (ROWS, 128), 1) < HEAD
    zero = jnp.zeros((ROWS, 128), BF16)

    def pair(base, hp):
        return slice(base + hp * 128, base + hp * 128 + 128)

    def lanes_of(e):
        return low_lanes if e == 0 else ~low_lanes

    raw = []
    for hp in range(8):
        q, k = qkv[:, pair(0, hp)], qkv[:, pair(WIDTH, hp)]
        for e in range(2):
            raw.append(lax.dot_general(jnp.where(lanes_of(e), q, zero), k, NT, preferred_element_type=F32))
    seen = mask[...] > 0.5
    soft = []
    for scores in raw:
        scores = jnp.where(seen, scores * 0.125, -1e30)
        ex = jnp.exp(scores - jnp.max(scores, axis=-1, keepdims=True))
        soft.append(ex * (1.0 / jnp.sum(ex, axis=-1, keepdims=True)))
    for hp in range(8):
        v = qkv[:, pair(2 * WIDTH, hp)]
        parts = []
        for e in range(2):
            probs[2 * hp + e] = soft[2 * hp + e]
            parts.append(jnp.dot(soft[2 * hp + e].astype(BF16), v, preferred_element_type=F32))
        x2[0, :, pair(0, hp)] = jnp.where(low_lanes, parts[0], parts[1]).astype(BF16)
    ex_att = exchange(1, x2.at[0], x2.at[1])
    ex_att.start()

    def proj_weights():
        return w[:, :, :, :, 3].reshape(WIDTH, WIDTH)

    xin[...] = xin[...] + (lax.dot_general(x2[0], proj_weights(), NT, preferred_element_type=F32) + row(5))
    xh2[...], rs2[...], x3[0] = norm(xin[...], row(1), row(6))
    ex_second = exchange(2, x3.at[0], x3.at[1])
    ex_second.start()

    def up(j, pre):
        pre = pre + row(7 + j)
        square = pre * pre
        t = jnp.tanh(GC * (pre + 0.044715 * (square * pre)))
        half = 0.5 * (1.0 + t)
        x4[0, j] = (pre * half).astype(BF16)
        dgel[j] = half + (0.5 * GC) * pre * (1.0 - t * t) * (1.0 + 0.134145 * square)

    ex_act = exchange(3, x4.at[0], x4.at[1])

    @pl.when(sec == 0)
    def _():
        for step in GATHER_TWO:
            gather(step)
        from_sibling("A1")
        from_sibling("A2")
        for j in range(4):
            up(j, lax.dot_general(x3[0], fc_weights(j), NT, preferred_element_type=F32))
        ex_act.start()
        from_sibling("Bl")
        from_sibling("Cl")
        for n in range(2):
            cols = slice(512 * n, 512 * (n + 1))
            result = xin[:, cols] + row(11)[:, cols]
            for j in range(4):
                half = w[n, :, :, :, 8 + j].reshape(512, WIDTH)
                result = result + lax.dot_general(x4[0, j], half, NT, preferred_element_type=F32)
            act_out[:, cols] = result.astype(BF16)
            handed_on[n].start()

    @pl.when(sec == 1)
    def _():
        for j in range(4):
            right = rbuf[128:160].reshape(WIDTH, WIDTH) if j == 0 else turned[j - 1]
            up(j, jnp.dot(x3[0], right, preferred_element_type=F32))
        ex_act.start()
        result = xin[...] + row(11)
        for j in range(4):
            right = rbuf[32 * j : 32 * j + 32].reshape(WIDTH, WIDTH)
            result = result + jnp.dot(x4[0, j], right, preferred_element_type=F32)
        act_out[...] = result.astype(BF16)

    for target in (ys[1], ys[3], zs[1], zs[3], xp):
        pl.semaphore_signal(room, 1, device_id=target, device_id_type=MESH)

    act_done = pltpu.make_async_copy(act_out, act_hbm, tok_sem)
    grad_done = pltpu.make_async_copy(grad_out, grad_hbm, cot_sem)

    @pl.when(crossed)
    def _():
        act_cross.start()

    @pl.when(~crossed)
    def _():
        act_done.start()

    for part in PARTS:
        await_sent(ag_sent[part][0], 30 if X_FIRST[part] else 15)
        await_sent(ag_sent[part][1], 1 if X_FIRST[part] else 16)
        await_sent(ag_sent[part][2], 32)
    rows = sb_y.at[pl.ds(1, 3)]
    small(rows, rows, sm_y, sib).wait_send()
    small(sb_c.at[0], sb_c.at[1], sm_c, sib).wait_send()
    small(rows, rows, sm_z, sib).wait_send()
    small(sb_x.at[x], sb_x.at[x], sm_x, xp).wait_send()

    @pl.when(sec == 0)
    def _():
        handed_back.wait_recv()
        gf[...] = hb[...]

    @pl.when(sec == 1)
    def _():
        @pl.when(crossed)
        def _():
            cot_cross.wait()

        gf[...] = cotv[rows_at]

    def column_sum(values):
        return jnp.sum(values.astype(F32), axis=0, keepdims=True)

    sbw[...] = jnp.zeros_like(sbw)
    sbw[11:12, :] = column_sum(gf[...])
    s_out[...] = gf[...].T.reshape(2, 4, 4, 2, 1, 16, ROWS)

    def swap(slot, src, dst):
        return exchange(slot, src.at[:, :, :, oc], dst)

    ex_gf = swap(4, s_out, t_out)
    ex_gf.start()
    for j in range(4):
        d_act = jnp.dot(gf[...], wout_weights(j), preferred_element_type=F32)
        d_pre = (dgel[j] * d_act).astype(BF16)
        dpre[j] = d_pre
        sbw[7 + j : 8 + j, :] = column_sum(d_pre)
        s_fc[j // 2, 2 * (j % 2) : 2 * (j % 2) + 2] = d_pre.T.reshape(2, 4, 2, 4, 16, ROWS)
    ex_dpre = swap(5, s_fc, t_fc)
    ex_dpre.start()
    ex_dbr = swap(6, s_proj, t_proj)
    ex_dmix = swap(7, s_qkv, t_qkv)

    def lhs(mine, theirs, rows):
        return jnp.concatenate([mine.reshape(rows, ROWS), theirs.reshape(rows, ROWS)], axis=1)

    def product(left, right):
        return jnp.dot(left, right, preferred_element_type=F32).astype(BF16)

    def grads_out(xx):
        left = lhs(s_out[xx, :, :, c], t_out[xx], 256)
        for j in range(4):
            w[xx, :, :, oc, 8 + j] = product(left, x4[:, j].reshape(2 * ROWS, WIDTH)).reshape(4, 4, 16, WIDTH)

    def grads_fc(xx):
        for k in range(2):
            zz = slice(2 * k, 2 * k + 2)
            left = lhs(s_fc[xx, zz, :, c], t_fc[xx, zz], 512)
            w[xx, zz, :, c, 8:12] = product(left, x3[...].reshape(2 * ROWS, WIDTH)).reshape(2, 4, 4, 16, WIDTH)

    def grads_att(xx):
        left = lhs(s_proj[xx, :, :, c], t_proj[xx], 256)
        w[xx, :, :, c, 7] = product(left, x2[...].reshape(2 * ROWS, WIDTH)).reshape(4, 4, 16, WIDTH)
        for k in range(2):
            zz = slice(2 * k, 2 * k + 2)
            left = lhs(s_qkv[xx, zz, :, c], t_qkv[xx, zz], 384)
            w[xx, zz, :, c, 4:7] = product(left, x1[...].reshape(2 * ROWS, WIDTH)).reshape(2, 4, 3, 16, WIDTH)

    def compute(name):
        if name == "gout1":
            ex_gf.wait_recv()
            ex_act.wait_recv()
            grads_out(ox)
        elif name == "gout0":
            grads_out(x)
        elif name == "gfc1":
            ex_dpre.wait_recv()
            ex_second.wait_recv()
            grads_fc(ox)
        elif name == "gfc0":
            grads_fc(x)
        elif name == "gatt1":
            ex_first.wait_recv()
            ex_att.wait_recv()
            ex_dbr.wait_recv()
            ex_dmix.wait_recv()
            grads_att(ox)
        elif name == "gatt0":
            grads_att(x)
        elif name == "first":
            pl.when(sec == 0)(back_first)

    rs_rings = {part: rings_of(part, True) for part in PARTS}
    rs_sem = {(part, name): (sem(), sem()) for part in PARTS for name in rs_rings[part]}
    rs_sent = {part: (sem(), sem()) for part in PARTS}
    rs_x = {part: (sem(),) if X_FIRST[part] else (sem(), sem(), sem()) for part in PARTS}
    rs_at = {
        (part, name): arrivals(3 * rs_rings[part][name][1] * len(rs_rings[part][name][0]))
        for part in PARTS
        for name in rs_rings[part]
    }
    rs_x_at = {part: arrivals(1 if X_FIRST[part] else 16) for part in PARTS}

    def add(view, *terms, out=None):
        if len(view.shape) > 3:
            for k in range(view.shape[0]):
                add(view.at[k], *(term.at[k] for term in terms))
            return
        total = view[...].astype(F32)
        for term in terms:
            total = total + term[...].astype(F32)
        if out is None:
            view[...] = total.astype(BF16)
        else:
            out[...] = total

    def leave(part):
        first = FIRST[part]
        for piece in (first, first + 1):
            if piece < 3:
                target = gqkv_hbm.at[piece]
            elif piece == 3:
                target = gproj_hbm.at[0]
            elif piece < 8:
                target = gfc_hbm.at[piece - 4]
            else:
                target = gwout_hbm.at[:, pl.ds(1024 * (piece - 8), 1024)]
            pltpu.make_async_copy(gsum.at[piece], target, own_sem).start()

    def own_sum(part):
        return gsum.at[pl.ds(FIRST[part], 2)]

    def summing(step):
        part, name, *rest = step.split(".")
        if part == "small":
            small_steps[int(name)]()
            return
        if part == "comp":
            compute(name)
            return
        ip, op, _, _ = axes(part)
        if name == "x" and rest[0] == "s":
            buf = rbuf.at[rs_x_at[part]]
            remote(slab(part, ox, ip[0], op[0], None, True), buf, rs_sent[part][1], rs_x[part][0], xp).start()
        elif name == "x":
            await_arrival(rs_x[part][0], 1)
            add(slab(part, x, ip[0], op[0], None, True), rbuf.at[rs_x_at[part]], out=own_sum(part))
            leave(part)
        elif name in ("X", "XR"):
            stage = int(rest[0])
            if name == "XR":
                await_arrival(rs_x[part][stage], 4 * len(STAGES[stage]))
            for o in STAGES[stage]:
                buf = rbuf.at[pl.ds(rs_x_at[part] + 4 * o, 4)]
                if name == "X":
                    ref = line(part, ox, op[o], None, True)
                    remote(ref, buf, rs_sent[part][1], rs_x[part][stage], xp).start()
                else:
                    add(line(part, x, op[o], None, True), buf)
        else:
            views, size, left, right = rs_rings[part][name]
            count = size * len(views)
            half, full = rs_sem[part, name]
            sent = rs_sent[part][0]

            def arrived(k):
                base = rs_at[part, name] + 3 * size * k
                if size == 1:
                    halves = [rbuf.at[base, pl.ds(0, 1)], rbuf.at[base, pl.ds(1, 1)]]
                    return halves + [rbuf.at[base + 1], rbuf.at[base + 2]]
                return [rbuf.at[pl.ds(base, 2)], rbuf.at[pl.ds(base + 2, 2)], rbuf.at[pl.ds(base + 4, 4)], rbuf.at[pl.ds(base + 8, 4)]]

            if rest[0] == "start":
                for k, view in enumerate(views):
                    remote(view(2, 0), arrived(k)[0], sent, half, right).start()
                    remote(view(2, 1), arrived(k)[1], sent, half, left).start()
            elif rest[0] == "mid":
                await_arrival(half, count)
                for k, view in enumerate(views):
                    add(view(1, 0), arrived(k)[0])
                    remote(view(1), arrived(k)[2], sent, full, right).start()
                    add(view(3, 1), arrived(k)[1])
                    remote(view(3), arrived(k)[3], sent, full, left).start()
            else:
                await_arrival(full, 2 * count)
                last = name == "in0" and not X_FIRST[part]
                for k, view in enumerate(views):
                    add(view(0), arrived(k)[2], arrived(k)[3], out=own_sum(part) if last else None)
                if last:
                    leave(part)

    sm_core, sm_xs, sm_zs, sm_ys = [(sem(), sem()) for _ in range(4)]

    def small_seven():
        for g in range(8):
            sr[g // 4, g % 4] = sbw[:, g * 128 : (g + 1) * 128]
        small(sr, sr_c, sm_core, sib).start()

    def small_eight():
        small(sr, sr_c, sm_core, sib).wait()
        sr[...] = sr[...] + sr_c[...]
        small(sr.at[ox], sr_x, sm_xs, xp).start()

    def small_nine():
        small(sr.at[ox], sr_x, sm_xs, xp).wait_recv()
        sr[x] = sr[x] + sr_x[...]
        for k in (1, 2, 3):
            small(sr.at[x, zp[k]], sr_z.at[k - 1], sm_zs, zs[k]).start()

    def small_ten():
        small(sr_z, sr_z, sm_zs, sib).wait_recv()
        sr_y[0] = sr[x, z] + sr_z[0] + sr_z[1] + sr_z[2]
        for k in (1, 2, 3):
            small(sr_y.at[0], sr_y.at[k], sm_ys, ys[k]).start()

    def small_eleven():
        rows = sr_y.at[pl.ds(1, 3)]
        small(rows, rows, sm_ys, sib).wait_recv()
        total = sr_y[0] + sr_y[1] + sr_y[2] + sr_y[3]
        picked = lax.dot_general(total, spread, NT, preferred_element_type=F32, precision=lax.Precision.HIGHEST)
        ggain_out[...] = picked[0:2, :]
        for k in range(10):
            gbias_out[k] = picked[2 + k : 3 + k, :]

    small_steps.update({7: small_seven, 8: small_eight, 9: small_nine, 10: small_ten, 11: small_eleven})

    pl.semaphore_wait(room, 5)

    @pl.when(sec == 0)
    def _():
        for step in SUM_ONE:
            summing(step)

    d_second = jnp.zeros((ROWS, WIDTH), F32)
    for j in range(4):
        d_second = d_second + jnp.dot(dpre[j], fc_weights(j), preferred_element_type=F32)

    def norm_back(d_out, hat, rs, gain):
        d_hat = d_out * gain
        mean_one = jnp.mean(d_hat, axis=-1, keepdims=True)
        mean_two = jnp.mean(d_hat * hat, axis=-1, keepdims=True)
        return rs * (d_hat - mean_one - hat * mean_two)

    sbw[1:2, :] = column_sum(d_second * xh2[...])
    sbw[6:7, :] = column_sum(d_second)
    dmid[...] = gf[...].astype(F32) + norm_back(d_second, xh2[...], rs2[...], row(1))
    dbr[...] = dmid[...].astype(BF16)
    sbw[5:6, :] = column_sum(dbr[...])
    s_proj[...] = dbr[...].T.reshape(2, 4, 4, 2, 1, 16, ROWS)
    ex_dbr.start()

    @pl.when(sec == 0)
    def _():
        for step in SUM_TWO:
            summing(step)

    datt[...] = jnp.dot(dbr[...], proj_weights(), preferred_element_type=F32).astype(BF16)
    d_probs, masked_da = [], []
    for hp in range(8):
        da, v = datt[:, pair(0, hp)], qkv[:, pair(2 * WIDTH, hp)]
        for e in range(2):
            masked_da.append(jnp.where(lanes_of(e), da, zero))
            d_probs.append(lax.dot_general(masked_da[-1], v, NT, preferred_element_type=F32))
    d_scores = []
    for h in range(16):
        p, dp_ = probs[h], d_probs[h]
        d_scores.append((p * (dp_ - jnp.sum(dp_ * p, axis=-1, keepdims=True))).astype(BF16))
    for hp in range(8):
        q, k = qkv[:, pair(0, hp)], qkv[:, pair(WIDTH, hp)]
        dq, dk, dv = [], [], []
        for e in range(2):
            h = 2 * hp + e
            dv.append(jnp.dot(probs[h].astype(BF16).T, masked_da[h], preferred_element_type=F32))
            dq.append(jnp.dot(d_scores[h], k, preferred_element_type=F32))
            dk.append(jnp.dot(d_scores[h].T, jnp.where(lanes_of(e), q, zero), preferred_element_type=F32))
        dmix[:, pair(0, hp)] = (jnp.where(low_lanes, dq[0], dq[1]) * 0.125).astype(BF16)
        dmix[:, pair(WIDTH, hp)] = ((dk[0] + dk[1]) * 0.125).astype(BF16)
        dmix[:, pair(2 * WIDTH, hp)] = (dv[0] + dv[1]).astype(BF16)
    for k in range(2):
        s_qkv[k] = dmix[:, 1536 * k : 1536 * (k + 1)].T.reshape(4, 4, 2, 3, 16, ROWS)
    ex_dmix.start()
    sbw[3:4, :] = column_sum(dmix[:, 0:WIDTH])
    sbw[4:5, :] = column_sum(dmix[:, 2 * WIDTH :])

    def back_first():
        d_first = jnp.dot(dmix[:, 0:1536], qkv_weights(0), preferred_element_type=F32)
        d_first = d_first + jnp.dot(dmix[:, 1536:], qkv_weights(1), preferred_element_type=F32)
        sbw[0:1, :] = column_sum(d_first * xh1[...])
        sbw[2:3, :] = column_sum(d_first)
        grad_out[...] = (dmid[...] + norm_back(d_first, xh1[...], rs1[...], row(0))).astype(BF16)

        @pl.when(crossed)
        def _():
            grad_cross.start()

        @pl.when(~crossed)
        def _():
            grad_done.start()

    @pl.when(sec == 1)
    def _():
        back_first()
        handed_back.start()
        for step in SUM_ONE + SUM_TWO:
            summing(step)

    for step in SUM_THREE:
        summing(step)

    small_done = [
        pltpu.make_async_copy(ggain_out, ggain_hbm, sem()),
        pltpu.make_async_copy(gbias_out, gbias_hbm, sem()),
    ]
    for cp in small_done:
        cp.start()

    for part in PARTS:
        await_sent(rs_sent[part][0], 30 if X_FIRST[part] else 15)
        await_sent(rs_sent[part][1], 1 if X_FIRST[part] else 16)
    for cp in (ex_first, ex_att, ex_second, ex_act, ex_gf, ex_dpre, ex_dbr, ex_dmix):
        cp.wait_send()
    small(sr.at[ox], sr_x, sm_xs, xp).wait_send()
    small(sr_z, sr_z, sm_zs, sib).wait_send()
    rows = sr_y.at[pl.ds(1, 3)]
    small(rows, rows, sm_ys, sib).wait_send()

    @pl.when(sec == 0)
    def _():
        for cp in handed_on:
            cp.wait_send()

    @pl.when(sec == 1)
    def _():
        handed_back.wait_send()

    @pl.when(crossed)
    def _():
        act_cross.wait()
        grad_cross.wait()

    @pl.when(~crossed)
    def _():
        act_done.wait()
        grad_done.wait()

    pltpu.make_async_copy(gsum, gsum, own_sem).wait()
    for cp in small_done:
        cp.wait()
    if (taken[0], taken[1]) != (SEMAPHORES, ARRIVALS):
        raise ValueError(taken)


SEMAPHORES = 195
ARRIVALS = 186


def move(*refs):
    count = len(refs) // 3
    sems = refs[-1]
    into = [pltpu.make_async_copy(refs[k], refs[2 * count + k], sems.at[0, k]) for k in range(count)]
    out = [pltpu.make_async_copy(refs[2 * count + k], refs[count + k], sems.at[1, k]) for k in range(count)]
    for cp in into:
        cp.start()
    for k in range(count):
        into[k].wait()
        out[k].start()
    for cp in out:
        cp.wait()


def local(tokens, segment_ids, gains, biases, w_qkv, w_proj, w_fc, w_out, cotangent):
    vmem = pl.BlockSpec(memory_space=pltpu.VMEM)
    hbm = pl.BlockSpec(memory_space=pl.ANY)

    def shape(*dims, dtype=F32):
        return jax.ShapeDtypeStruct(dims, dtype)

    def v(*dims, dtype=BF16):
        return pltpu.VMEM(dims, dtype)

    scratch = [
        v(2, 4, 4, 2, 12, 16, WIDTH), v(ARRIVALS, 2, 16, WIDTH),
        v(ROWS, WIDTH), v(ROWS, WIDTH), v(12, 16, WIDTH, dtype=F32), v(2, 16, dtype=F32), v(10, 1, 16, dtype=F32),
        v(ROWS, WIDTH), v(2, ROWS, WIDTH), v(2, 8, ROWS, dtype=F32),
        v(ROWS, WIDTH, dtype=F32), v(2, ROWS, WIDTH), v(2, ROWS, WIDTH), v(2, ROWS, WIDTH), v(2, 4, ROWS, WIDTH),
        v(ROWS, 3 * WIDTH), v(16, ROWS, ROWS, dtype=F32), v(ROWS, WIDTH, dtype=F32), v(ROWS, WIDTH, dtype=F32),
        v(ROWS, 1, dtype=F32), v(ROWS, 1, dtype=F32), v(4, ROWS, WIDTH, dtype=F32), v(ROWS, WIDTH),
        v(4, ROWS, WIDTH), v(ROWS, WIDTH), v(ROWS, WIDTH), v(ROWS, 3 * WIDTH), v(ROWS, WIDTH, dtype=F32),
        v(ROWS, ROWS, dtype=F32), v(1, 3 * WIDTH, dtype=F32),
        v(16, WIDTH, dtype=F32), v(16, 16, dtype=F32), v(4, 16, 128, dtype=F32), v(2, 16, 128, dtype=F32),
        v(2, 4, 16, 128, dtype=F32), v(16, WIDTH, dtype=F32), v(2, 4, 16, 128, dtype=F32),
        v(2, 4, 16, 128, dtype=F32), v(4, 16, 128, dtype=F32), v(3, 16, 128, dtype=F32), v(4, 16, 128, dtype=F32),
        v(2, 4, 4, 2, 1, 16, ROWS), v(2, 4, 4, 2, 4, 16, ROWS), v(2, 4, 4, 2, 1, 16, ROWS), v(2, 4, 4, 2, 3, 16, ROWS),
        v(2, 4, 4, 1, 16, ROWS), v(2, 4, 4, 4, 16, ROWS), v(2, 4, 4, 1, 16, ROWS), v(2, 4, 4, 3, 16, ROWS),
        v(ROWS, WIDTH), v(3, WIDTH, WIDTH),
        pltpu.SemaphoreType.REGULAR, pltpu.SemaphoreType.DMA((SEMAPHORES,)),
    ]
    results = (
        shape(ROWS, WIDTH, dtype=BF16), shape(ROWS, WIDTH, dtype=BF16), shape(2, 16), shape(10, 1, 16),
        shape(3, 16, WIDTH), shape(1, 16, WIDTH), shape(4, 16, WIDTH), shape(16, 4 * WIDTH),
    )
    out = pl.pallas_call(
        kernel,
        out_shape=results,
        in_specs=[vmem, vmem, vmem] + [hbm] * 6,
        out_specs=(hbm,) * 8,
        scratch_shapes=scratch,
        compiler_params=pltpu.CompilerParams(
            collective_id=0, has_side_effects=True, vmem_limit_bytes=63 * 2**20
        ),
        name="relay",
    )(
        segment_ids.reshape(1, ROWS),
        gains[0],
        biases[0],
        tokens,
        w_qkv[0].T.reshape(3, 16, WIDTH),
        w_proj[0].T.reshape(1, 16, WIDTH),
        w_fc[0].T.reshape(4, 16, WIDTH),
        w_out[0].T,
        cotangent,
    )
    out = pl.pallas_call(
        move,
        out_shape=results,
        in_specs=[hbm] * 8,
        out_specs=(hbm,) * 8,
        scratch_shapes=[pltpu.VMEM(r.shape, r.dtype) for r in results] + [pltpu.SemaphoreType.DMA((2, 8))],
        name="move",
    )(*out)
    activations, input_grads, g_gains, g_biases, g_qkv, g_proj, g_fc, g_out = out
    return (
        activations[None],
        input_grads[None],
        g_gains[None],
        g_biases.transpose(1, 0, 2),
        g_qkv.reshape(48, WIDTH).T[None],
        g_proj.reshape(16, WIDTH).T[None],
        g_fc.reshape(64, WIDTH).T[None],
        g_out.T[None],
    )


def solution(mesh):
    weight = P("section", None, "dp")
    rows = P("section", "dp", None)
    return jax.shard_map(
        local,
        mesh=mesh,
        in_specs=(P("dp", None), P("dp")) + (weight,) * 6 + (P("dp", None),),
        out_specs=(rows, rows) + (weight,) * 6,
        check_vma=False,
    )
```

```python
import jax
import jax.numpy as jnp
from jax import lax
from jax.experimental import pallas as pl
from jax.experimental.pallas import tpu as pltpu
from jax.sharding import PartitionSpec as P

MESH = pl.DeviceIdType.MESH
F32 = jnp.float32
BF16 = jnp.bfloat16
EPS = 1e-05
ROWS = 128
WIDTH = 1024
HEAD = 64
GC = 0.7978845608028654
NT = (((1,), (1,)), ((), ()))

PARTS = ("Be", "Ce", "A1", "Bm", "Cm", "A2", "Bl", "Cl")
FIRST = {"Be": 0, "Ce": 2, "A1": 4, "Bm": 6, "Cm": 7, "A2": 8, "Bl": 10, "Cl": 11}
SIZE = {"Be": 2, "Ce": 2, "A1": 2, "Bm": 1, "Cm": 1, "A2": 2, "Bl": 1, "Cl": 1}
INNER_IS_Y = {part: part[0] == "C" or part == "A1" for part in PARTS}
X_FIRST = {part: part[0] != "A" for part in PARTS}
GROUPS = {
    "g0": (0, (0,)), "g1": (1, (0,)), "g2": (0, (1, 3)), "g3": (0, (2,)), "g4": (1, (1, 3)), "g5": (1, (2,)),
    "gA": (0, (0, 1, 2, 3)), "gB": (1, (0, 1, 2, 3)),
}
FINE = ("g0", "g1", "g2", "g3", "g4", "g5")
COARSE = ("gA", "gB")
GATHER_GROUPS = {"Be": COARSE, "Ce": COARSE, "A1": FINE, "Bm": COARSE, "Cm": COARSE, "A2": FINE, "Bl": COARSE, "Cl": COARSE}
SUM_GROUPS = {"Be": COARSE, "Ce": COARSE, "A1": COARSE, "Bm": COARSE, "Cm": COARSE, "A2": COARSE, "Bl": COARSE, "Cl": COARSE}
STAGES = ((0,), (1, 3), (2,))
SUM_AT = {part: (0, FIRST[part] + 4) if FIRST[part] < 8 else (1, FIRST[part]) for part in PARTS}
BESIDE = {"Bm": 0, "Cm": 1, "Bl": 0, "Cl": 1}

GATHER_ONE = [
    "A2.in0.start", "A1.in0.start", "A2.X.g0.0", "Be.x.s", "Ce.in0.start", "A1.g0.start", "Be.in0.start",
    "Bl.in0.start", "Cm.x.s", "A2.g0.start", "Bl.x.s", "Cl.x.s", "A1.in0.mid", "Cm.in0.start", "small.1",
    "A2.in0.mid", "A2.g2.start", "A2.X.g2.0", "Be.x.r", "A1.g0.mid", "Be.in1.start", "A1.g2.start", "Ce.x.s",
    "Cm.x.r", "Cl.in0.start", "A2.g0.mid", "Bm.x.s", "A1.X.g0.1", "Cl.x.r", "Cm.in0.mid", "A1.X.g2.0", "A2.in0.end",
    "A2.g3.start", "Bm.in0.start", "Ce.in0.mid", "Be.in0.mid", "Bl.in0.mid", "Be.in1.mid", "Ce.x.r", "A2.g2.mid",
    "Ce.in1.start", "A1.in0.end", "A1.g2.mid", "A1.g3.start", "A2.g0.end", "Be.in0.end", "Be.sib.0.0", "A2.X.g0.1",
    "Cm.in0.end", "Cm.gA.start", "A1.X.g3.0", "A1.X.g0.0", "small.2", "Ce.in0.end", "Cl.in1.start", "Cm.in1.start",
    "Be.gA.start", "Cl.in0.mid", "Bl.x.r", "Bm.x.r", "Bm.in0.mid", "A2.sib.0.0", "Bm.in1.start", "Be.in1.end",
    "A2.X.g3.0", "Ce.gA.start", "A1.g3.mid", "A1.X.g2.1", "Cm.gA.mid", "A1.sib.0.1", "A1.sib.0.0", "Ce.in1.mid",
    "Cm.in1.mid", "Be.gB.start", "Ce.in1.end", "Be.gA.mid", "Bm.in1.mid", "Ce.sib.1.0", "small.3", "Bl.in0.end",
    "Bl.sib.0.0", "Be.sib.0.1", "A2.XR.0", "A1.X.g3.1", "A1.g2.end", "Ce.gB.start", "Ce.sib.0.0", "A2.g2.end",
    "Be.sib.1.0", "Bm.in0.end", "A2.g3.mid", "A1.XR.0", "Cl.in0.end", "Cm.sib.0.0", "A2.sib.0.1", "Cm.gA.end",
    "Ce.gA.mid", "Ce.sib.0.1", "A2.X.g2.1", "Bm.in1.end", "Be.gB.mid", "A1.g0.end", "A2.X.g3.1", "A1.g3.end",
    "Cm.sib.0.1", "small.4", "A2.sib.1.0", "Cl.in1.mid", "Cm.in1.end", "A2.X.g0.2", "Bm.gB.start", "A1.XR.1",
    "A1.sib.1.1", "Bm.gA.start", "Cl.sib.0.0", "Be.sib.1.1", "A1.sib.0.2", "A1.X.g2.2", "Bl.in1.start", "Ce.gB.mid",
    "A1.X.g0.2", "Cm.sib.1.0", "A2.g3.end", "Ce.sib.1.1", "Cl.in1.end", "Bl.gA.start", "Bl.in1.mid", "A2.sib.0.2",
    "Cm.gB.start", "Be.gB.end", "Be.sib.1.2", "small.5", "Cl.gA.start", "Ce.gA.end", "Ce.sib.0.2", "Be.gA.end",
    "Be.sib.0.2", "A1.X.g3.2", "A1.sib.1.0", "Ce.gB.end", "Bl.in1.end", "Bl.gB.start", "Ce.sib.1.2", "Cm.sib.0.2",
    "Bl.sib.1.0", "Bm.gB.mid", "A2.X.g2.2", "A2.XR.1", "Cl.sib.1.0", "Bm.sib.0.0", "A2.sib.1.1", "Cl.gB.start",
    "Bm.gA.mid", "Bm.sib.1.0", "Bm.sib.1.1", "Bm.sib.0.1", "Cm.gB.mid", "Cm.sib.1.1", "small.6",
]

GATHER_TWO = [
    "A1.XR.2", "A1.sib.1.2", "Cl.gA.mid", "Bl.gB.mid", "Bl.sib.1.1", "A2.X.g3.2", "Cl.sib.0.1", "Cl.gB.mid",
    "Bl.gA.mid", "Bl.sib.0.1", "Cm.gB.end", "Cm.sib.1.2", "Bm.gA.end", "Bm.gB.end", "Bm.sib.1.2", "Bm.sib.0.2",
    "Cl.sib.1.1", "Bl.gB.end", "A2.XR.2", "A2.sib.1.2", "Cl.gA.end", "Cl.sib.0.2", "Bl.sib.1.2", "Cl.gB.end",
    "Cl.sib.1.2", "Bl.gA.end", "Bl.sib.0.2",
]

GATHER_THREE = [

]

SUM_ONE = [
    "comp.gout1", "A2.X.2", "Bl.gB.start", "Cl.gB.start", "comp.gout0", "Cl.gA.start", "Bl.gA.start", "comp.gfc1",
    "Cm.gB.start", "Bm.gB.start", "Cl.gB.mid", "Bl.gB.mid", "A1.X.2",
]

SUM_TWO = [
    "Cl.gA.mid", "Bm.gB.mid",
]

SUM_THREE = [
    "Cm.gB.mid", "Cl.gB.end", "Cl.in1.start", "A2.XR.2", "A2.gA.start", "A2.X.1", "comp.gfc0", "Cm.gA.start",
    "Bm.gA.start", "comp.gatt1", "Ce.gB.start", "Cl.gA.end", "Cl.in1.mid", "Be.gB.start", "A1.X.1", "comp.gatt0",
    "Cm.gB.end", "comp.first", "small.7", "Bm.gB.end", "Ce.gA.start", "Be.gA.start", "Cl.in1.end", "Ce.gB.mid",
    "Be.gB.mid", "Bl.gA.mid", "A1.XR.2", "A1.X.0", "Ce.gA.mid", "A1.gA.start", "Ce.gB.end", "Bl.gB.end", "Be.gA.mid",
    "Be.gB.end", "small.8", "Bl.gA.end", "Cm.gA.mid", "Cm.in1.start", "Ce.in1.start", "Bm.in1.start", "A2.X.0",
    "Bm.gA.mid", "Bl.in1.start", "A1.XR.1", "A1.gA.mid", "Be.in1.start", "Be.gA.end", "Ce.gA.end", "A2.XR.1",
    "A2.gA.mid", "A1.XR.0", "Cl.x.s", "small.9", "Bl.in0.start", "Bm.gA.end", "Bm.in1.mid", "Bl.in1.mid",
    "Be.in0.start", "Cm.gA.end", "Cm.in0.start", "Ce.in0.start", "Cl.in0.start", "Cm.in1.mid", "A1.gA.end",
    "A1.in0.start", "Ce.in1.mid", "Be.in1.mid", "Bm.in0.start", "A2.XR.0", "small.10", "A2.gA.end", "A2.in0.start",
    "Bm.in1.end", "Bm.x.s", "Bl.in0.mid", "Bl.in1.end", "Ce.in0.mid", "Bl.x.s", "Cl.in0.mid", "Cm.in1.end", "Cm.x.s",
    "Be.in0.mid", "Be.in1.end", "Be.x.s", "Cm.in0.mid", "Bm.in0.mid", "A1.in0.mid", "small.11", "Ce.in1.end",
    "Ce.x.s", "A2.in0.mid", "Bl.in0.end", "Ce.in0.end", "Bl.x.r", "Bm.in0.end", "Cm.in0.end", "Be.in0.end", "Be.x.r",
    "Bm.x.r", "Cm.x.r", "Cl.in0.end", "Cl.x.r", "Ce.x.r", "A2.in0.end", "A1.in0.end",
]


def remote(src, dst, ssem, rsem, target):
    return pltpu.make_async_remote_copy(
        src_ref=src, dst_ref=dst, send_sem=ssem, recv_sem=rsem, device_id=target, device_id_type=MESH
    )


def kernel(
    seg_ref, gains_ref, bias_ref, tok_ref, qkv_ref, proj_ref, fc_ref, wout_ref, cot_ref,
    act_hbm, grad_hbm, ggain_hbm, gbias_hbm, gqkv_hbm, gproj_hbm, gfc_hbm, gwout_hbm,
    w, rbuf, act_out, grad_out, gsum, ggain_out, gbias_out, cotv, segs,
    xin, x1, x2, x3, x4, qkv, probs, xh1, xh2, rs1, rs2, dgel, gf, dpre, dbr, datt, dmix, dmid, mask, qbias,
    bf, sgb, sb_y, sb_c, sb_x, sbw, sr, sr_c, sr_x, sr_z, sr_y,
    s_out, s_fc, s_proj, s_qkv, t_out, t_fc, t_proj, t_qkv, hb, turned, room, sems,
):
    sec = lax.axis_index("section")
    dp = lax.axis_index("dp")
    c = lax.rem(dp, 2)
    y = lax.rem(lax.div(dp, 2), 4)
    z = lax.rem(lax.div(dp, 8), 4)
    x = lax.div(dp, 32)
    ox, oc = 1 - x, 1 - c
    yp = [lax.rem(y + k, 4) for k in range(4)]
    zp = [lax.rem(z + k, 4) for k in range(4)]

    def at(px, pz, py, pc):
        return (sec, ((px * 4 + pz) * 4 + py) * 2 + pc)

    ys = [at(x, z, yp[k], c) for k in range(4)]
    zs = [at(x, zp[k], y, c) for k in range(4)]
    xp = at(ox, z, y, c)
    sib = at(x, z, y, oc)
    other_section = (1 - sec, ((lax.rem(x + c, 2) * 4 + z) * 4 + y) * 2 + c)
    crossed = (sec == 1) & (c == 1)
    rows_at = sec * c

    taken = [0, 0]

    def sem():
        taken[0] += 1
        return sems.at[taken[0] - 1]

    def arrivals(slabs):
        taken[1] += slabs
        return taken[1] - slabs

    barrier = pltpu.get_barrier_semaphore()
    partners = ys[1:] + zs[1:] + [xp, sib, other_section]
    for target in partners:
        pl.semaphore_signal(barrier, 1, device_id=target, device_id_type=MESH)
    own = w.at[x, z, y, c]
    own_sem, tok_sem, cot_sem = sem(), sem(), sem()
    pltpu.make_async_copy(qkv_ref, own.at[pl.ds(0, 3)], own_sem).start()
    pltpu.make_async_copy(proj_ref, own.at[pl.ds(3, 1)], own_sem).start()
    pltpu.make_async_copy(fc_ref, own.at[pl.ds(4, 4)], own_sem).start()
    for j in range(4):
        pltpu.make_async_copy(wout_ref.at[:, pl.ds(1024 * j, 1024)], own.at[8 + j], own_sem).start()
    tok_in = pltpu.make_async_copy(tok_ref, datt, tok_sem)
    cot_in = pltpu.make_async_copy(cot_ref, cotv.at[0], cot_sem)
    tok_in.start()
    cot_in.start()
    pl.semaphore_wait(barrier, len(partners))
    pltpu.make_async_copy(own, own, own_sem).wait()

    def slab(part, xx, i, o, half=None, summing=False):
        core, base = c, FIRST[part]
        if summing:
            core, base = (oc if SUM_AT[part][0] else c), SUM_AT[part][1]
        pz, py = (o, i) if INNER_IS_Y[part] else (i, o)
        if half is None:
            return w.at[xx, pz, py, core, pl.ds(base, SIZE[part])]
        if SIZE[part] == 2:
            return w.at[xx, pz, py, core, pl.ds(base + half, 1)]
        return w.at[xx, pz, py, core, pl.ds(base, 1), :, pl.ds(512 * half, 512)]

    def bytes_of(pieces):
        for xs in (1, 2):
            for a in (1, 2, 3, 4):
                for b in (1, 2, 3, 4):
                    k = pieces // (xs * a * b)
                    if k <= 12 and xs * a * b * k == pieces:
                        return w.at[pl.ds(0, xs), pl.ds(0, a), pl.ds(0, b), 0, pl.ds(0, k)]

    def await_arrival(which, count):
        ref = bytes_of(count)
        remote(ref, ref, which, which, sib).wait_recv()

    def await_sent(which, count):
        ref = bytes_of(count)
        remote(ref, ref, which, which, sib).wait_send()

    def axes(part):
        return (yp, zp, ys, zs) if INNER_IS_Y[part] else (zp, yp, zs, ys)

    def line(part, xx, o, half=None, summing=False):
        core, base = c, FIRST[part]
        if summing:
            core, base = (oc if SUM_AT[part][0] else c), SUM_AT[part][1]
        inner = slice(None) if half is None else pl.ds(2 * half, 2)
        pz, py = (o, inner) if INNER_IS_Y[part] else (inner, o)
        return w.at[xx, pz, py, core, pl.ds(base, SIZE[part])]

    def rings_of(part, summing):
        ip, op, idev, odev = axes(part)
        found = {}

        def along_inner(xx):
            return lambda j, half=None: slab(part, xx, ip[j], op[0], half, summing)

        def along_outer(xx, i):
            return lambda j, half=None: slab(part, xx, ip[i], op[j], half, summing)

        def along_line(xx):
            return lambda j, half=None: line(part, xx, op[j], half, summing)

        for other in (0, 1) if X_FIRST[part] else (0,):
            found[f"in{other}"] = ([along_inner(ox if other else x)], 1, idev[3], idev[1])
        for g in (SUM_GROUPS if summing else GATHER_GROUPS)[part]:
            other, offsets = GROUPS[g]
            if X_FIRST[part] or not other:
                xx = ox if other else x
                if len(offsets) == 4:
                    found[g] = ([along_line(xx)], 4, odev[3], odev[1])
                else:
                    found[g] = ([along_outer(xx, i) for i in offsets], 1, odev[3], odev[1])
        return found

    def small(src, dst, sems_of, target):
        return remote(src, dst, sems_of[0], sems_of[1], target)

    ag_rings = {part: rings_of(part, False) for part in PARTS}
    ag_sem = {(part, name): (sem(), sem()) for part in PARTS for name in ag_rings[part]}
    ag_sent = {part: (sem(), sem(), sem()) for part in PARTS}
    ag_x = {part: (sem(),) if X_FIRST[part] else (sem(), sem(), sem()) for part in PARTS}
    ag_sib = {part: sem() for part in PARTS}

    def gather(step):
        part, name, *rest = step.split(".")
        if part == "small":
            small_steps[int(name)]()
            return
        ip, op, _, _ = axes(part)
        if name == "x" and rest[0] == "s":
            ref = slab(part, x, ip[0], op[0])
            remote(ref, ref, ag_sent[part][1], ag_x[part][0], xp).start()
        elif name == "x":
            await_arrival(ag_x[part][0], SIZE[part])
        elif name == "X":
            offsets = GROUPS[rest[0]][1]
            for o in STAGES[int(rest[1])]:
                whole = len(offsets) == 4
                for ref in [line(part, x, op[o])] if whole else [slab(part, x, ip[i], op[o]) for i in offsets]:
                    remote(ref, ref, ag_sent[part][1], ag_x[part][int(rest[1])], xp).start()
        elif name == "XR":
            await_arrival(ag_x[part][int(rest[0])], 4 * SIZE[part] * len(STAGES[int(rest[0])]))
        elif name == "sib":
            for o in STAGES[int(rest[1])]:
                ref = line(part, ox if int(rest[0]) else x, op[o])
                remote(ref, ref, ag_sent[part][2], ag_sib[part], sib).start()
        else:
            views, size, left, right = ag_rings[part][name]
            count = size * len(views) * SIZE[part]
            full, half = ag_sem[part, name]
            sent = ag_sent[part][0]
            if rest[0] == "start":
                for view in views:
                    remote(view(0), view(0), sent, full, right).start()
                    remote(view(0), view(0), sent, full, left).start()
            elif rest[0] == "mid":
                await_arrival(full, 2 * count)
                for view in views:
                    remote(view(3, 0), view(3, 0), sent, half, right).start()
                    remote(view(1, 1), view(1, 1), sent, half, left).start()
            else:
                await_arrival(half, count)

    spread = (
        lax.broadcasted_iota(jnp.int32, (16, 128), 1)
        == lax.broadcasted_iota(jnp.int32, (16, 128), 0) + 16 * (y * 2 + c)
    ).astype(F32)
    sm_y, sm_c, sm_z, sm_x = [(sem(), sem()) for _ in range(4)]

    cross = [(sem(), sem()) for _ in range(4)]
    seg_cross = remote(segs.at[0], segs.at[1], *cross[0], xp)
    cot_cross = remote(cotv.at[0], cotv.at[1], *cross[1], xp)
    act_cross = remote(act_out, act_hbm, *cross[2], xp)
    grad_cross = remote(grad_out, grad_hbm, *cross[3], xp)

    def small_one():
        segs[0] = jnp.broadcast_to(seg_ref[...].astype(F32), (8, ROWS))

        @pl.when(crossed)
        def _():
            seg_cross.start()

        sgb[...] = jnp.zeros_like(sgb)
        sgb[0:2, :] = gains_ref[...].astype(F32)
        sgb[2:12, :] = bias_ref[...].astype(F32)
        sb_y[0] = jnp.dot(sgb[...].astype(BF16), spread.astype(BF16), preferred_element_type=F32)
        for k in (1, 2, 3):
            small(sb_y.at[0], sb_y.at[k], sm_y, ys[k]).start()

    def small_two():
        rows = sb_y.at[pl.ds(1, 3)]
        small(rows, rows, sm_y, sib).wait_recv()
        sb_c[0] = sb_y[0] + sb_y[1] + sb_y[2] + sb_y[3]
        small(sb_c.at[0], sb_c.at[1], sm_c, sib).start()

    def small_three():
        small(sb_c.at[0], sb_c.at[1], sm_c, sib).wait_recv()
        sb_x[x, z] = sb_c[0] + sb_c[1]
        for k in (1, 2, 3):
            small(sb_x.at[x, z], sb_x.at[x, z], sm_z, zs[k]).start()

    def small_four():
        rows = sb_x.at[0, pl.ds(0, 3)]
        small(rows, rows, sm_z, sib).wait_recv()
        small(sb_x.at[x], sb_x.at[x], sm_x, xp).start()

    def small_five():
        small(sb_x.at[ox], sb_x.at[ox], sm_x, xp).wait_recv()
        for g in range(8):
            bf[:, g * 128 : (g + 1) * 128] = sb_x[g // 4, g % 4]
        qbias[:, 0:WIDTH] = bf[3:4, :]
        qbias[:, WIDTH : 2 * WIDTH] = jnp.zeros((1, WIDTH), F32)
        qbias[:, 2 * WIDTH :] = bf[4:5, :]

    def row(k):
        return bf[k : k + 1, :]

    def small_six():
        @pl.when(crossed)
        def _():
            seg_cross.wait()

        seg = jnp.broadcast_to(segs[rows_at][0:1], (ROWS, ROWS))
        qi = lax.broadcasted_iota(jnp.int32, (ROWS, ROWS), 0)
        ki = lax.broadcasted_iota(jnp.int32, (ROWS, ROWS), 1)
        allowed = (seg == seg.T) & (ki <= qi) & (lax.div(qi, 64) == lax.div(ki, 64))
        mask[...] = allowed.astype(F32)

    small_steps = {1: small_one, 2: small_two, 3: small_three, 4: small_four, 5: small_five, 6: small_six}

    for step in GATHER_ONE:
        gather(step)

    def from_sibling(part):
        await_arrival(ag_sib[part], 32 * SIZE[part])

    def fc_weights(j):
        return w[j // 2, 2 * (j % 2) : 2 * (j % 2) + 2, :, :, 4:8].reshape(WIDTH, WIDTH)

    def wout_weights(j):
        return w[:, :, :, :, 8 + j].reshape(WIDTH, WIDTH)

    halves = [pl.ds(0, 512), pl.ds(512, 512)]
    handed_on = [remote(act_out.at[:, k], hb.at[:, k], sem(), sem(), other_section) for k in halves]
    handed_back = remote(grad_out, hb, sem(), sem(), other_section)
    tok_in.wait()
    cot_in.wait()

    @pl.when(sec == 0)
    def _():
        xin[...] = datt[...].astype(F32)

    @pl.when(sec == 1)
    def _():
        for step in GATHER_TWO + GATHER_THREE:
            gather(step)

        @pl.when(crossed)
        def _():
            cot_cross.start()

        for part in PARTS:
            from_sibling(part)
        for j in range(4):
            rbuf[32 * j : 32 * j + 32] = wout_weights(j).T.reshape(32, 2, 16, WIDTH)
        rbuf[128:160] = fc_weights(0).T.reshape(32, 2, 16, WIDTH)
        for j in range(1, 4):
            turned[j - 1] = fc_weights(j).T
        for cp in handed_on:
            cp.wait_recv()
        xin[...] = hb[...].astype(F32)

    def norm(values, gain, shift):
        centre = values - jnp.mean(values, axis=-1, keepdims=True)
        rs = lax.rsqrt(jnp.mean(centre * centre, axis=-1, keepdims=True) + EPS)
        hat = centre * rs
        return hat, rs, (hat * gain + shift).astype(BF16)

    ex_sems = [(sem(), sem()) for _ in range(8)]

    def exchange(slot, src, dst):
        return remote(src, dst, *ex_sems[slot], sib)

    xh1[...], rs1[...], x1[0] = norm(xin[...], row(0), row(2))
    ex_first = exchange(0, x1.at[0], x1.at[1])
    ex_first.start()

    @pl.when(sec == 0)
    def _():
        from_sibling("Be")
        from_sibling("Ce")

    def qkv_weights(k):
        return w[k, :, :, :, 0:3].reshape(1536, WIDTH)

    for k in range(2):
        cols = slice(1536 * k, 1536 * (k + 1))
        mixed = lax.dot_general(x1[0], qkv_weights(k), NT, preferred_element_type=F32)
        qkv[:, cols] = (mixed + qbias[:, cols]).astype(BF16)

    low_lanes = lax.broadcasted_iota(jnp.int32, (ROWS, 128), 1) < HEAD
    zero = jnp.zeros((ROWS, 128), BF16)

    def pair(base, hp):
        return slice(base + hp * 128, base + hp * 128 + 128)

    def lanes_of(e):
        return low_lanes if e == 0 else ~low_lanes

    raw = []
    for hp in range(8):
        q, k = qkv[:, pair(0, hp)], qkv[:, pair(WIDTH, hp)]
        for e in range(2):
            raw.append(lax.dot_general(jnp.where(lanes_of(e), q, zero), k, NT, preferred_element_type=F32))
    seen = mask[...] > 0.5
    soft = []
    for scores in raw:
        scores = jnp.where(seen, scores * 0.125, -1e30)
        ex = jnp.exp(scores - jnp.max(scores, axis=-1, keepdims=True))
        soft.append(ex * (1.0 / jnp.sum(ex, axis=-1, keepdims=True)))
    for hp in range(8):
        v = qkv[:, pair(2 * WIDTH, hp)]
        parts = []
        for e in range(2):
            probs[2 * hp + e] = soft[2 * hp + e]
            parts.append(jnp.dot(soft[2 * hp + e].astype(BF16), v, preferred_element_type=F32))
        x2[0, :, pair(0, hp)] = jnp.where(low_lanes, parts[0], parts[1]).astype(BF16)
    ex_att = exchange(1, x2.at[0], x2.at[1])
    ex_att.start()

    def proj_weights():
        return w[:, :, :, :, 3].reshape(WIDTH, WIDTH)

    xin[...] = xin[...] + (lax.dot_general(x2[0], proj_weights(), NT, preferred_element_type=F32) + row(5))
    xh2[...], rs2[...], x3[0] = norm(xin[...], row(1), row(6))
    ex_second = exchange(2, x3.at[0], x3.at[1])
    ex_second.start()

    def up(j, pre):
        pre = pre + row(7 + j)
        square = pre * pre
        t = jnp.tanh(GC * (pre + 0.044715 * (square * pre)))
        half = 0.5 * (1.0 + t)
        x4[0, j] = (pre * half).astype(BF16)
        dgel[j] = half + (0.5 * GC) * pre * (1.0 - t * t) * (1.0 + 0.134145 * square)

    ex_act = exchange(3, x4.at[0], x4.at[1])

    @pl.when(sec == 0)
    def _():
        for step in GATHER_TWO:
            gather(step)
        for part in ("A1", "Bm", "Cm"):
            from_sibling(part)
        for j in range(4):
            up(j, lax.dot_general(x3[0], fc_weights(j), NT, preferred_element_type=F32))
        ex_act.start()
        for step in GATHER_THREE:
            gather(step)
        for part in ("A2", "Bl", "Cl"):
            from_sibling(part)
        for n in range(2):
            cols = slice(512 * n, 512 * (n + 1))
            result = xin[:, cols] + row(11)[:, cols]
            for j in range(4):
                half = w[n, :, :, :, 8 + j].reshape(512, WIDTH)
                result = result + lax.dot_general(x4[0, j], half, NT, preferred_element_type=F32)
            act_out[:, cols] = result.astype(BF16)
            handed_on[n].start()

    @pl.when(sec == 1)
    def _():
        for j in range(4):
            right = rbuf[128:160].reshape(WIDTH, WIDTH) if j == 0 else turned[j - 1]
            up(j, jnp.dot(x3[0], right, preferred_element_type=F32))
        ex_act.start()
        result = xin[...] + row(11)
        for j in range(4):
            right = rbuf[32 * j : 32 * j + 32].reshape(WIDTH, WIDTH)
            result = result + jnp.dot(x4[0, j], right, preferred_element_type=F32)
        act_out[...] = result.astype(BF16)

    for target in (ys[1], ys[3], zs[1], zs[3], xp):
        pl.semaphore_signal(room, 1, device_id=target, device_id_type=MESH)

    act_done = pltpu.make_async_copy(act_out, act_hbm, tok_sem)
    grad_done = pltpu.make_async_copy(grad_out, grad_hbm, cot_sem)

    @pl.when(crossed)
    def _():
        act_cross.start()

    @pl.when(~crossed)
    def _():
        act_done.start()

    for part in PARTS:
        await_sent(ag_sent[part][0], (30 if X_FIRST[part] else 15) * SIZE[part])
        await_sent(ag_sent[part][1], (1 if X_FIRST[part] else 16) * SIZE[part])
        await_sent(ag_sent[part][2], 32 * SIZE[part])
    rows = sb_y.at[pl.ds(1, 3)]
    small(rows, rows, sm_y, sib).wait_send()
    small(sb_c.at[0], sb_c.at[1], sm_c, sib).wait_send()
    small(rows, rows, sm_z, sib).wait_send()
    small(sb_x.at[x], sb_x.at[x], sm_x, xp).wait_send()

    @pl.when(sec == 0)
    def _():
        handed_back.wait_recv()
        gf[...] = hb[...]

    @pl.when(sec == 1)
    def _():
        @pl.when(crossed)
        def _():
            cot_cross.wait()

        gf[...] = cotv[rows_at]

    def column_sum(values):
        return jnp.sum(values.astype(F32), axis=0, keepdims=True)

    sbw[...] = jnp.zeros_like(sbw)
    sbw[11:12, :] = column_sum(gf[...])
    s_out[...] = gf[...].T.reshape(2, 4, 4, 2, 1, 16, ROWS)

    def swap(slot, src, dst):
        return exchange(slot, src.at[:, :, :, oc], dst)

    ex_gf = swap(4, s_out, t_out)
    ex_gf.start()
    for j in range(4):
        d_act = jnp.dot(gf[...], wout_weights(j), preferred_element_type=F32)
        d_pre = (dgel[j] * d_act).astype(BF16)
        dpre[j] = d_pre
        sbw[7 + j : 8 + j, :] = column_sum(d_pre)
        s_fc[j // 2, 2 * (j % 2) : 2 * (j % 2) + 2] = d_pre.T.reshape(2, 4, 2, 4, 16, ROWS)
    ex_dpre = swap(5, s_fc, t_fc)
    ex_dpre.start()
    ex_dbr = swap(6, s_proj, t_proj)
    ex_dmix = swap(7, s_qkv, t_qkv)

    def lhs(mine, theirs, rows):
        return jnp.concatenate([mine.reshape(rows, ROWS), theirs.reshape(rows, ROWS)], axis=1)

    def product(left, right):
        return jnp.dot(left, right, preferred_element_type=F32).astype(BF16)

    def grads_out(xx):
        left = lhs(s_out[xx, :, :, c], t_out[xx], 256)
        for j in range(4):
            w[xx, :, :, oc, 8 + j] = product(left, x4[:, j].reshape(2 * ROWS, WIDTH)).reshape(4, 4, 16, WIDTH)

    def grads_fc(xx):
        for k in range(2):
            zz = slice(2 * k, 2 * k + 2)
            left = lhs(s_fc[xx, zz, :, c], t_fc[xx, zz], 512)
            w[xx, zz, :, c, 8:12] = product(left, x3[...].reshape(2 * ROWS, WIDTH)).reshape(2, 4, 4, 16, WIDTH)

    def grads_att(xx):
        left = lhs(s_proj[xx, :, :, c], t_proj[xx], 256)
        w[xx, :, :, c, 7] = product(left, x2[...].reshape(2 * ROWS, WIDTH)).reshape(4, 4, 16, WIDTH)
        for k in range(2):
            zz = slice(2 * k, 2 * k + 2)
            left = lhs(s_qkv[xx, zz, :, c], t_qkv[xx, zz], 384)
            w[xx, zz, :, c, 4:7] = product(left, x1[...].reshape(2 * ROWS, WIDTH)).reshape(2, 4, 3, 16, WIDTH)

    def compute(name):
        if name == "gout1":
            ex_gf.wait_recv()
            ex_act.wait_recv()
            grads_out(ox)
        elif name == "gout0":
            grads_out(x)
        elif name == "gfc1":
            ex_dpre.wait_recv()
            ex_second.wait_recv()
            grads_fc(ox)
        elif name == "gfc0":
            grads_fc(x)
        elif name == "gatt1":
            ex_first.wait_recv()
            ex_att.wait_recv()
            ex_dbr.wait_recv()
            ex_dmix.wait_recv()
            grads_att(ox)
        elif name == "gatt0":
            grads_att(x)
        elif name == "first":
            pl.when(sec == 0)(back_first)

    rs_rings = {part: rings_of(part, True) for part in PARTS}
    rs_sem = {(part, name): (sem(), sem()) for part in PARTS for name in rs_rings[part]}
    rs_sent = {part: (sem(), sem()) for part in PARTS}
    rs_x = {part: (sem(),) if X_FIRST[part] else (sem(), sem(), sem()) for part in PARTS}
    rs_at, rs_x_at = {}, {}
    for part in PARTS:
        twin = "B" + part[1]
        for name, (views, size, _, _) in rs_rings[part].items():
            rs_at[part, name] = rs_at[twin, name] if BESIDE.get(part) else arrivals(3 * size * len(views))
        rs_x_at[part] = rs_x_at[twin] if BESIDE.get(part) else arrivals(1 if X_FIRST[part] else 16)

    def room_for(part, base, count=None):
        slabs = base if count is None else pl.ds(base, count)
        return rbuf.at[slabs] if SIZE[part] == 2 else rbuf.at[slabs, pl.ds(BESIDE[part], 1)]

    def add(view, *terms, out=None):
        if len(view.shape) > 3:
            for k in range(view.shape[0]):
                add(view.at[k], *(term.at[k] for term in terms))
            return
        total = view[...].astype(F32)
        for term in terms:
            total = total + term[...].astype(F32)
        if out is None:
            view[...] = total.astype(BF16)
        else:
            out[...] = total

    def leave(part):
        first = FIRST[part]
        for piece in range(first, first + SIZE[part]):
            if piece < 3:
                target = gqkv_hbm.at[piece]
            elif piece == 3:
                target = gproj_hbm.at[0]
            elif piece < 8:
                target = gfc_hbm.at[piece - 4]
            else:
                target = gwout_hbm.at[:, pl.ds(1024 * (piece - 8), 1024)]
            pltpu.make_async_copy(gsum.at[piece], target, own_sem).start()

    def own_sum(part):
        return gsum.at[pl.ds(FIRST[part], SIZE[part])]

    def summing(step):
        part, name, *rest = step.split(".")
        if part == "small":
            small_steps[int(name)]()
            return
        if part == "comp":
            compute(name)
            return
        ip, op, _, _ = axes(part)
        if name == "x" and rest[0] == "s":
            buf = room_for(part, rs_x_at[part])
            remote(slab(part, ox, ip[0], op[0], None, True), buf, rs_sent[part][1], rs_x[part][0], xp).start()
        elif name == "x":
            await_arrival(rs_x[part][0], SIZE[part])
            add(slab(part, x, ip[0], op[0], None, True), room_for(part, rs_x_at[part]), out=own_sum(part))
            leave(part)
        elif name in ("X", "XR"):
            stage = int(rest[0])
            if name == "XR":
                await_arrival(rs_x[part][stage], 4 * SIZE[part] * len(STAGES[stage]))
            for o in STAGES[stage]:
                buf = room_for(part, rs_x_at[part] + 4 * o, 4)
                if name == "X":
                    ref = line(part, ox, op[o], None, True)
                    remote(ref, buf, rs_sent[part][1], rs_x[part][stage], xp).start()
                else:
                    add(line(part, x, op[o], None, True), buf)
        else:
            views, size, left, right = rs_rings[part][name]
            count = size * len(views) * SIZE[part]
            half, full = rs_sem[part, name]
            sent = rs_sent[part][0]

            def arrived(k):
                base = rs_at[part, name] + 3 * size * k
                if size == 1:
                    fulls = [room_for(part, base + 1), room_for(part, base + 2)]
                    if SIZE[part] == 2:
                        return [rbuf.at[base, pl.ds(0, 1)], rbuf.at[base, pl.ds(1, 1)]] + fulls
                    piece = pl.ds(BESIDE[part], 1)
                    return [rbuf.at[base, piece, :, pl.ds(512 * k, 512)] for k in (0, 1)] + fulls
                return [room_for(part, base + 2 * k, 2) for k in (0, 1)] + [room_for(part, base + 4 * k, 4) for k in (1, 2)]

            if rest[0] == "start":
                for k, view in enumerate(views):
                    remote(view(2, 0), arrived(k)[0], sent, half, right).start()
                    remote(view(2, 1), arrived(k)[1], sent, half, left).start()
            elif rest[0] == "mid":
                await_arrival(half, count)
                for k, view in enumerate(views):
                    add(view(1, 0), arrived(k)[0])
                    remote(view(1), arrived(k)[2], sent, full, right).start()
                    add(view(3, 1), arrived(k)[1])
                    remote(view(3), arrived(k)[3], sent, full, left).start()
            else:
                await_arrival(full, 2 * count)
                last = name == "in0" and not X_FIRST[part]
                for k, view in enumerate(views):
                    add(view(0), arrived(k)[2], arrived(k)[3], out=own_sum(part) if last else None)
                if last:
                    leave(part)

    sm_core, sm_xs, sm_zs, sm_ys = [(sem(), sem()) for _ in range(4)]

    def small_seven():
        for g in range(8):
            sr[g // 4, g % 4] = sbw[:, g * 128 : (g + 1) * 128]
        small(sr, sr_c, sm_core, sib).start()

    def small_eight():
        small(sr, sr_c, sm_core, sib).wait()
        sr[...] = sr[...] + sr_c[...]
        small(sr.at[ox], sr_x, sm_xs, xp).start()

    def small_nine():
        small(sr.at[ox], sr_x, sm_xs, xp).wait_recv()
        sr[x] = sr[x] + sr_x[...]
        for k in (1, 2, 3):
            small(sr.at[x, zp[k]], sr_z.at[k - 1], sm_zs, zs[k]).start()

    def small_ten():
        small(sr_z, sr_z, sm_zs, sib).wait_recv()
        sr_y[0] = sr[x, z] + sr_z[0] + sr_z[1] + sr_z[2]
        for k in (1, 2, 3):
            small(sr_y.at[0], sr_y.at[k], sm_ys, ys[k]).start()

    def small_eleven():
        rows = sr_y.at[pl.ds(1, 3)]
        small(rows, rows, sm_ys, sib).wait_recv()
        total = sr_y[0] + sr_y[1] + sr_y[2] + sr_y[3]
        picked = lax.dot_general(total, spread, NT, preferred_element_type=F32, precision=lax.Precision.HIGHEST)
        ggain_out[...] = picked[0:2, :]
        for k in range(10):
            gbias_out[k] = picked[2 + k : 3 + k, :]

    small_steps.update({7: small_seven, 8: small_eight, 9: small_nine, 10: small_ten, 11: small_eleven})

    pl.semaphore_wait(room, 5)

    @pl.when(sec == 0)
    def _():
        for step in SUM_ONE:
            summing(step)

    d_second = jnp.zeros((ROWS, WIDTH), F32)
    for j in range(4):
        d_second = d_second + jnp.dot(dpre[j], fc_weights(j), preferred_element_type=F32)

    def norm_back(d_out, hat, rs, gain):
        d_hat = d_out * gain
        mean_one = jnp.mean(d_hat, axis=-1, keepdims=True)
        mean_two = jnp.mean(d_hat * hat, axis=-1, keepdims=True)
        return rs * (d_hat - mean_one - hat * mean_two)

    sbw[1:2, :] = column_sum(d_second * xh2[...])
    sbw[6:7, :] = column_sum(d_second)
    dmid[...] = gf[...].astype(F32) + norm_back(d_second, xh2[...], rs2[...], row(1))
    dbr[...] = dmid[...].astype(BF16)
    sbw[5:6, :] = column_sum(dbr[...])
    s_proj[...] = dbr[...].T.reshape(2, 4, 4, 2, 1, 16, ROWS)
    ex_dbr.start()

    @pl.when(sec == 0)
    def _():
        for step in SUM_TWO:
            summing(step)

    datt[...] = jnp.dot(dbr[...], proj_weights(), preferred_element_type=F32).astype(BF16)
    d_probs, masked_da = [], []
    for hp in range(8):
        da, v = datt[:, pair(0, hp)], qkv[:, pair(2 * WIDTH, hp)]
        for e in range(2):
            masked_da.append(jnp.where(lanes_of(e), da, zero))
            d_probs.append(lax.dot_general(masked_da[-1], v, NT, preferred_element_type=F32))
    d_scores = []
    for h in range(16):
        p, dp_ = probs[h], d_probs[h]
        d_scores.append((p * (dp_ - jnp.sum(dp_ * p, axis=-1, keepdims=True))).astype(BF16))
    for hp in range(8):
        q, k = qkv[:, pair(0, hp)], qkv[:, pair(WIDTH, hp)]
        dq, dk, dv = [], [], []
        for e in range(2):
            h = 2 * hp + e
            dv.append(jnp.dot(probs[h].astype(BF16).T, masked_da[h], preferred_element_type=F32))
            dq.append(jnp.dot(d_scores[h], k, preferred_element_type=F32))
            dk.append(jnp.dot(d_scores[h].T, jnp.where(lanes_of(e), q, zero), preferred_element_type=F32))
        dmix[:, pair(0, hp)] = (jnp.where(low_lanes, dq[0], dq[1]) * 0.125).astype(BF16)
        dmix[:, pair(WIDTH, hp)] = ((dk[0] + dk[1]) * 0.125).astype(BF16)
        dmix[:, pair(2 * WIDTH, hp)] = (dv[0] + dv[1]).astype(BF16)
    for k in range(2):
        s_qkv[k] = dmix[:, 1536 * k : 1536 * (k + 1)].T.reshape(4, 4, 2, 3, 16, ROWS)
    ex_dmix.start()
    sbw[3:4, :] = column_sum(dmix[:, 0:WIDTH])
    sbw[4:5, :] = column_sum(dmix[:, 2 * WIDTH :])

    def back_first():
        d_first = jnp.dot(dmix[:, 0:1536], qkv_weights(0), preferred_element_type=F32)
        d_first = d_first + jnp.dot(dmix[:, 1536:], qkv_weights(1), preferred_element_type=F32)
        sbw[0:1, :] = column_sum(d_first * xh1[...])
        sbw[2:3, :] = column_sum(d_first)
        grad_out[...] = (dmid[...] + norm_back(d_first, xh1[...], rs1[...], row(0))).astype(BF16)

        @pl.when(crossed)
        def _():
            grad_cross.start()

        @pl.when(~crossed)
        def _():
            grad_done.start()

    @pl.when(sec == 1)
    def _():
        back_first()
        handed_back.start()
        for step in SUM_ONE + SUM_TWO:
            summing(step)

    for step in SUM_THREE:
        summing(step)

    small_done = [
        pltpu.make_async_copy(ggain_out, ggain_hbm, sem()),
        pltpu.make_async_copy(gbias_out, gbias_hbm, sem()),
    ]
    for cp in small_done:
        cp.start()

    for part in PARTS:
        await_sent(rs_sent[part][0], (30 if X_FIRST[part] else 15) * SIZE[part])
        await_sent(rs_sent[part][1], (1 if X_FIRST[part] else 16) * SIZE[part])
    for cp in (ex_first, ex_att, ex_second, ex_act, ex_gf, ex_dpre, ex_dbr, ex_dmix):
        cp.wait_send()
    small(sr.at[ox], sr_x, sm_xs, xp).wait_send()
    small(sr_z, sr_z, sm_zs, sib).wait_send()
    rows = sr_y.at[pl.ds(1, 3)]
    small(rows, rows, sm_ys, sib).wait_send()

    @pl.when(sec == 0)
    def _():
        for cp in handed_on:
            cp.wait_send()

    @pl.when(sec == 1)
    def _():
        handed_back.wait_send()

    @pl.when(crossed)
    def _():
        act_cross.wait()
        grad_cross.wait()

    @pl.when(~crossed)
    def _():
        act_done.wait()
        grad_done.wait()

    pltpu.make_async_copy(gsum, gsum, own_sem).wait()
    for cp in small_done:
        cp.wait()
    if (taken[0], taken[1]) != (SEMAPHORES, ARRIVALS):
        raise ValueError(taken)


SEMAPHORES = 243
ARRIVALS = 186


def move(*refs):
    count = len(refs) // 3
    sems = refs[-1]
    into = [pltpu.make_async_copy(refs[k], refs[2 * count + k], sems.at[0, k]) for k in range(count)]
    out = [pltpu.make_async_copy(refs[2 * count + k], refs[count + k], sems.at[1, k]) for k in range(count)]
    for cp in into:
        cp.start()
    for k in range(count):
        into[k].wait()
        out[k].start()
    for cp in out:
        cp.wait()


def local(tokens, segment_ids, gains, biases, w_qkv, w_proj, w_fc, w_out, cotangent):
    vmem = pl.BlockSpec(memory_space=pltpu.VMEM)
    hbm = pl.BlockSpec(memory_space=pl.ANY)

    def shape(*dims, dtype=F32):
        return jax.ShapeDtypeStruct(dims, dtype)

    def v(*dims, dtype=BF16):
        return pltpu.VMEM(dims, dtype)

    scratch = [
        v(2, 4, 4, 2, 12, 16, WIDTH), v(ARRIVALS, 2, 16, WIDTH),
        v(ROWS, WIDTH), v(ROWS, WIDTH), v(12, 16, WIDTH, dtype=F32), v(2, 16, dtype=F32), v(10, 1, 16, dtype=F32),
        v(2, ROWS, WIDTH), v(2, 8, ROWS, dtype=F32),
        v(ROWS, WIDTH, dtype=F32), v(2, ROWS, WIDTH), v(2, ROWS, WIDTH), v(2, ROWS, WIDTH), v(2, 4, ROWS, WIDTH),
        v(ROWS, 3 * WIDTH), v(16, ROWS, ROWS, dtype=F32), v(ROWS, WIDTH, dtype=F32), v(ROWS, WIDTH, dtype=F32),
        v(ROWS, 1, dtype=F32), v(ROWS, 1, dtype=F32), v(4, ROWS, WIDTH, dtype=F32), v(ROWS, WIDTH),
        v(4, ROWS, WIDTH), v(ROWS, WIDTH), v(ROWS, WIDTH), v(ROWS, 3 * WIDTH), v(ROWS, WIDTH, dtype=F32),
        v(ROWS, ROWS, dtype=F32), v(1, 3 * WIDTH, dtype=F32),
        v(16, WIDTH, dtype=F32), v(16, 16, dtype=F32), v(4, 16, 128, dtype=F32), v(2, 16, 128, dtype=F32),
        v(2, 4, 16, 128, dtype=F32), v(16, WIDTH, dtype=F32), v(2, 4, 16, 128, dtype=F32),
        v(2, 4, 16, 128, dtype=F32), v(4, 16, 128, dtype=F32), v(3, 16, 128, dtype=F32), v(4, 16, 128, dtype=F32),
        v(2, 4, 4, 2, 1, 16, ROWS), v(2, 4, 4, 2, 4, 16, ROWS), v(2, 4, 4, 2, 1, 16, ROWS), v(2, 4, 4, 2, 3, 16, ROWS),
        v(2, 4, 4, 1, 16, ROWS), v(2, 4, 4, 4, 16, ROWS), v(2, 4, 4, 1, 16, ROWS), v(2, 4, 4, 3, 16, ROWS),
        v(ROWS, WIDTH), v(3, WIDTH, WIDTH),
        pltpu.SemaphoreType.REGULAR, pltpu.SemaphoreType.DMA((SEMAPHORES,)),
    ]
    results = (
        shape(ROWS, WIDTH, dtype=BF16), shape(ROWS, WIDTH, dtype=BF16), shape(2, 16), shape(10, 1, 16),
        shape(3, 16, WIDTH), shape(1, 16, WIDTH), shape(4, 16, WIDTH), shape(16, 4 * WIDTH),
    )
    out = pl.pallas_call(
        kernel,
        out_shape=results,
        in_specs=[vmem, vmem, vmem] + [hbm] * 6,
        out_specs=(hbm,) * 8,
        scratch_shapes=scratch,
        compiler_params=pltpu.CompilerParams(
            collective_id=0, has_side_effects=True, vmem_limit_bytes=127 * 2**19
        ),
        name="relay",
    )(
        segment_ids.reshape(1, ROWS),
        gains[0],
        biases[0],
        tokens,
        w_qkv[0].T.reshape(3, 16, WIDTH),
        w_proj[0].T.reshape(1, 16, WIDTH),
        w_fc[0].T.reshape(4, 16, WIDTH),
        w_out[0].T,
        cotangent,
    )
    out = pl.pallas_call(
        move,
        out_shape=results,
        in_specs=[hbm] * 8,
        out_specs=(hbm,) * 8,
        scratch_shapes=[pltpu.VMEM(r.shape, r.dtype) for r in results] + [pltpu.SemaphoreType.DMA((2, 8))],
        name="move",
    )(*out)
    activations, input_grads, g_gains, g_biases, g_qkv, g_proj, g_fc, g_out = out
    return (
        activations[None],
        input_grads[None],
        g_gains[None],
        g_biases.transpose(1, 0, 2),
        g_qkv.reshape(48, WIDTH).T[None],
        g_proj.reshape(16, WIDTH).T[None],
        g_fc.reshape(64, WIDTH).T[None],
        g_out.T[None],
    )


def solution(mesh):
    weight = P("section", None, "dp")
    rows = P("section", "dp", None)
    return jax.shard_map(
        local,
        mesh=mesh,
        in_specs=(P("dp", None), P("dp")) + (weight,) * 6 + (P("dp", None),),
        out_specs=(rows, rows) + (weight,) * 6,
        check_vma=False,
    )
```

```python
import jax
import jax.numpy as jnp
from jax import lax
from jax.experimental import pallas as pl
from jax.experimental.pallas import tpu as pltpu
from jax.sharding import PartitionSpec as P

MESH = pl.DeviceIdType.MESH
F32 = jnp.float32
BF16 = jnp.bfloat16
EPS = 1e-05
ROWS = 128
WIDTH = 1024
HEAD = 64
GC = 0.7978845608028654
NT = (((1,), (1,)), ((), ()))

PARTS = ("Be", "Ce", "A1", "Bm", "Cm", "A2", "Bl", "Cl")
FIRST = {"Be": 0, "Ce": 2, "A1": 4, "Bm": 6, "Cm": 7, "A2": 8, "Bl": 10, "Cl": 11}
SIZE = {"Be": 2, "Ce": 2, "A1": 2, "Bm": 1, "Cm": 1, "A2": 2, "Bl": 1, "Cl": 1}
INNER_IS_Y = {part: part[0] == "C" or part == "A1" for part in PARTS}
X_FIRST = {part: part[0] != "A" for part in PARTS}
GROUPS = {
    "g0": (0, (0,)), "g1": (1, (0,)), "g2": (0, (1, 3)), "g3": (0, (2,)), "g4": (1, (1, 3)), "g5": (1, (2,)),
    "gA": (0, (0, 1, 2, 3)), "gB": (1, (0, 1, 2, 3)),
}
FINE = ("g0", "g1", "g2", "g3", "g4", "g5")
COARSE = ("gA", "gB")
GATHER_GROUPS = {"Be": COARSE, "Ce": COARSE, "A1": FINE, "Bm": COARSE, "Cm": COARSE, "A2": FINE, "Bl": COARSE, "Cl": COARSE}
SUM_GROUPS = {"Be": COARSE, "Ce": COARSE, "A1": COARSE, "Bm": COARSE, "Cm": COARSE, "A2": COARSE, "Bl": COARSE, "Cl": COARSE}
STAGES = ((0,), (1, 3), (2,))
SUM_AT = {part: (0, FIRST[part] + 4) if FIRST[part] < 8 else (1, FIRST[part]) for part in PARTS}
BESIDE = {"Bm": 0, "Cm": 1, "Bl": 0, "Cl": 1}

GATHER_ONE = [
    "A2.in0.start", "A1.in0.start", "A2.X.g0.0", "Be.x.s", "Ce.in0.start", "A1.g0.start", "Be.in0.start",
    "Bl.in0.start", "Cm.x.s", "A2.g0.start", "Bl.x.s", "Cl.x.s", "A1.in0.mid", "Cm.in0.start", "small.1",
    "A2.in0.mid", "A2.g2.start", "A2.X.g2.0", "Be.x.r", "A1.g0.mid", "Be.in1.start", "A1.g2.start", "Ce.x.s",
    "Cm.x.r", "Cl.in0.start", "A2.g0.mid", "Bm.x.s", "A1.X.g0.1", "Cl.x.r", "Cm.in0.mid", "A1.X.g2.0", "A2.in0.end",
    "A2.g3.start", "Bm.in0.start", "Ce.in0.mid", "Be.in0.mid", "Bl.in0.mid", "Be.in1.mid", "Ce.x.r", "A2.g2.mid",
    "Ce.in1.start", "A1.in0.end", "A1.g2.mid", "A1.g3.start", "A2.g0.end", "Be.in0.end", "Be.sib.0.0", "A2.X.g0.1",
    "Cm.in0.end", "Cm.gA.start", "A1.X.g3.0", "A1.X.g0.0", "small.2", "Ce.in0.end", "Cl.in1.start", "Cm.in1.start",
    "Be.gA.start", "Cl.in0.mid", "Bl.x.r", "Bm.x.r", "Bm.in0.mid", "A2.sib.0.0", "Bm.in1.start", "Be.in1.end",
    "A2.X.g3.0", "Ce.gA.start", "A1.g3.mid", "A1.X.g2.1", "Cm.gA.mid", "A1.sib.0.1", "A1.sib.0.0", "Ce.in1.mid",
    "Cm.in1.mid", "Be.gB.start", "Ce.in1.end", "Be.gA.mid", "Bm.in1.mid", "Ce.sib.1.0", "small.3", "Bl.in0.end",
    "Bl.sib.0.0", "Be.sib.0.1", "A2.XR.0", "A1.X.g3.1", "A1.g2.end", "Ce.gB.start", "Ce.sib.0.0", "A2.g2.end",
    "Be.sib.1.0", "Bm.in0.end", "A2.g3.mid", "A1.XR.0", "Cl.in0.end", "Cm.sib.0.0", "A2.sib.0.1", "Cm.gA.end",
    "Ce.gA.mid", "Ce.sib.0.1", "A2.X.g2.1", "Bm.in1.end", "Be.gB.mid", "A1.g0.end", "A2.X.g3.1", "A1.g3.end",
    "Cm.sib.0.1", "small.4", "A2.sib.1.0", "Cl.in1.mid", "Cm.in1.end", "A2.X.g0.2", "Bm.gB.start", "A1.XR.1",
    "A1.sib.1.1", "Bm.gA.start", "Cl.sib.0.0", "Be.sib.1.1", "A1.sib.0.2", "A1.X.g2.2", "Bl.in1.start", "Ce.gB.mid",
    "A1.X.g0.2", "Cm.sib.1.0", "A2.g3.end", "Ce.sib.1.1", "Cl.in1.end", "Bl.gA.start", "Bl.in1.mid", "A2.sib.0.2",
    "Cm.gB.start", "Be.gB.end", "Be.sib.1.2", "small.5", "Cl.gA.start", "Ce.gA.end", "Ce.sib.0.2", "Be.gA.end",
    "Be.sib.0.2", "A1.X.g3.2", "A1.sib.1.0", "Ce.gB.end", "Bl.in1.end", "Bl.gB.start", "Ce.sib.1.2", "Cm.sib.0.2",
    "Bl.sib.1.0", "Bm.gB.mid", "A2.X.g2.2", "A2.XR.1", "Cl.sib.1.0", "Bm.sib.0.0", "A2.sib.1.1", "Cl.gB.start",
    "Bm.gA.mid", "Bm.sib.1.0", "Bm.sib.1.1", "Bm.sib.0.1", "Cm.gB.mid", "Cm.sib.1.1", "small.6",
]

GATHER_TWO = [
    "A1.XR.2", "A1.sib.1.2", "Cl.gA.mid", "Bl.gB.mid", "Bl.sib.1.1", "A2.X.g3.2", "Cl.sib.0.1", "Cl.gB.mid",
    "Bl.gA.mid", "Bl.sib.0.1", "Cm.gB.end", "Cm.sib.1.2", "Bm.gA.end", "Bm.gB.end", "Bm.sib.1.2", "Bm.sib.0.2",
    "Cl.sib.1.1", "Bl.gB.end", "A2.XR.2", "A2.sib.1.2", "Cl.gA.end", "Cl.sib.0.2", "Bl.sib.1.2", "Cl.gB.end",
    "Cl.sib.1.2", "Bl.gA.end", "Bl.sib.0.2",
]

GATHER_THREE = [

]

SUM_ONE = [
    "comp.gout1", "A2.X.2", "Bl.gB.start", "Cl.gB.start", "comp.gout0", "Cl.gA.start", "Bl.gA.start", "comp.gfc1",
    "Cm.gB.start", "Bm.gB.start", "Cl.gB.mid", "Bl.gB.mid", "A1.X.2",
]

SUM_TWO = [
    "Cl.gA.mid", "Bm.gB.mid",
]

SUM_THREE = [
    "Cm.gB.mid", "Cl.gB.end", "Cl.in1.start", "A2.XR.2", "A2.gA.start", "A2.X.1", "comp.gfc0", "Cm.gA.start",
    "Bm.gA.start", "comp.gatt1", "Ce.gB.start", "Cl.gA.end", "Cl.in1.mid", "Be.gB.start", "A1.X.1", "comp.gatt0",
    "Cm.gB.end", "comp.first", "small.7", "Bm.gB.end", "Ce.gA.start", "Be.gA.start", "Cl.in1.end", "Ce.gB.mid",
    "Be.gB.mid", "Bl.gA.mid", "A1.XR.2", "A1.X.0", "Ce.gA.mid", "A1.gA.start", "Ce.gB.end", "Bl.gB.end", "Be.gA.mid",
    "Be.gB.end", "small.8", "Bl.gA.end", "Cm.gA.mid", "Cm.in1.start", "Ce.in1.start", "Bm.in1.start", "A2.X.0",
    "Bm.gA.mid", "Bl.in1.start", "A1.XR.1", "A1.gA.mid", "Be.in1.start", "Be.gA.end", "Ce.gA.end", "A2.XR.1",
    "A2.gA.mid", "A1.XR.0", "Cl.x.s", "small.9", "Bl.in0.start", "Bm.gA.end", "Bm.in1.mid", "Bl.in1.mid",
    "Be.in0.start", "Cm.gA.end", "Cm.in0.start", "Ce.in0.start", "Cl.in0.start", "Cm.in1.mid", "A1.gA.end",
    "A1.in0.start", "Ce.in1.mid", "Be.in1.mid", "Bm.in0.start", "A2.XR.0", "small.10", "A2.gA.end", "A2.in0.start",
    "Bm.in1.end", "Bm.x.s", "Bl.in0.mid", "Bl.in1.end", "Ce.in0.mid", "Bl.x.s", "Cl.in0.mid", "Cm.in1.end", "Cm.x.s",
    "Be.in0.mid", "Be.in1.end", "Be.x.s", "Cm.in0.mid", "Bm.in0.mid", "A1.in0.mid", "small.11", "Ce.in1.end",
    "Ce.x.s", "A2.in0.mid", "Bl.in0.end", "Ce.in0.end", "Bl.x.r", "Bm.in0.end", "Cm.in0.end", "Be.in0.end", "Be.x.r",
    "Bm.x.r", "Cm.x.r", "Cl.in0.end", "Cl.x.r", "Ce.x.r", "A2.in0.end", "A1.in0.end",
]


def remote(src, dst, ssem, rsem, target):
    return pltpu.make_async_remote_copy(
        src_ref=src, dst_ref=dst, send_sem=ssem, recv_sem=rsem, device_id=target, device_id_type=MESH
    )


def kernel(
    seg_ref, gains_ref, bias_ref, tok_ref, qkv_ref, proj_ref, fc_ref, wout_ref, cot_ref,
    act_hbm, grad_hbm, ggain_hbm, gbias_hbm, gqkv_hbm, gproj_hbm, gfc_hbm, gwout_hbm,
    w, rbuf, act_out, grad_out, gsum, ggain_out, gbias_out, cotv, segs,
    xin, x1, x2, x3, x4, qkv, probs, xh1, xh2, rs1, rs2, dgel, gf, dpre, dbr, datt, dmix, dmid, mask, qbias,
    bf, sgb, sb_y, sb_c, sb_x, sbw, sr, sr_c, sr_x, sr_z, sr_y,
    s_out, s_fc, s_proj, s_qkv, t_out, t_fc, t_proj, t_qkv, hb, turned, room, sems,
):
    sec = lax.axis_index("section")
    dp = lax.axis_index("dp")
    c = lax.rem(dp, 2)
    y = lax.rem(lax.div(dp, 2), 4)
    z = lax.rem(lax.div(dp, 8), 4)
    x = lax.div(dp, 32)
    ox, oc = 1 - x, 1 - c
    yp = [lax.rem(y + k, 4) for k in range(4)]
    zp = [lax.rem(z + k, 4) for k in range(4)]

    def at(px, pz, py, pc):
        return (sec, ((px * 4 + pz) * 4 + py) * 2 + pc)

    ys = [at(x, z, yp[k], c) for k in range(4)]
    zs = [at(x, zp[k], y, c) for k in range(4)]
    xp = at(ox, z, y, c)
    sib = at(x, z, y, oc)
    other_section = (1 - sec, ((lax.rem(x + c, 2) * 4 + z) * 4 + y) * 2 + c)
    crossed = (sec == 1) & (c == 1)
    rows_at = sec * c

    taken = [0, 0]

    def sem():
        taken[0] += 1
        return sems.at[taken[0] - 1]

    def arrivals(slabs):
        taken[1] += slabs
        return taken[1] - slabs

    barrier = pltpu.get_barrier_semaphore()
    partners = ys[1:] + zs[1:] + [xp, sib, other_section]
    for target in partners:
        pl.semaphore_signal(barrier, 1, device_id=target, device_id_type=MESH)
    own = w.at[x, z, y, c]
    own_sem, tok_sem, cot_sem = sem(), sem(), sem()
    pltpu.make_async_copy(qkv_ref, own.at[pl.ds(0, 3)], own_sem).start()
    pltpu.make_async_copy(proj_ref, own.at[pl.ds(3, 1)], own_sem).start()
    pltpu.make_async_copy(fc_ref, own.at[pl.ds(4, 4)], own_sem).start()
    for j in range(4):
        pltpu.make_async_copy(wout_ref.at[:, pl.ds(1024 * j, 1024)], own.at[8 + j], own_sem).start()
    tok_in = pltpu.make_async_copy(tok_ref, datt, tok_sem)
    cot_in = pltpu.make_async_copy(cot_ref, cotv.at[0], cot_sem)
    tok_in.start()
    cot_in.start()
    pl.semaphore_wait(barrier, len(partners))
    pltpu.make_async_copy(own, own, own_sem).wait()

    def slab(part, xx, i, o, half=None, summing=False):
        core, base = c, FIRST[part]
        if summing:
            core, base = (oc if SUM_AT[part][0] else c), SUM_AT[part][1]
        pz, py = (o, i) if INNER_IS_Y[part] else (i, o)
        if half is None:
            return w.at[xx, pz, py, core, pl.ds(base, SIZE[part])]
        if SIZE[part] == 2:
            return w.at[xx, pz, py, core, pl.ds(base + half, 1)]
        return w.at[xx, pz, py, core, pl.ds(base, 1), :, pl.ds(512 * half, 512)]

    def bytes_of(pieces):
        for xs in (1, 2):
            for a in (1, 2, 3, 4):
                for b in (1, 2, 3, 4):
                    k = pieces // (xs * a * b)
                    if k <= 12 and xs * a * b * k == pieces:
                        return w.at[pl.ds(0, xs), pl.ds(0, a), pl.ds(0, b), 0, pl.ds(0, k)]

    def await_arrival(which, count):
        ref = bytes_of(count)
        remote(ref, ref, which, which, sib).wait_recv()

    def await_sent(which, count):
        ref = bytes_of(count)
        remote(ref, ref, which, which, sib).wait_send()

    def axes(part):
        return (yp, zp, ys, zs) if INNER_IS_Y[part] else (zp, yp, zs, ys)

    def line(part, xx, o, half=None, summing=False):
        core, base = c, FIRST[part]
        if summing:
            core, base = (oc if SUM_AT[part][0] else c), SUM_AT[part][1]
        inner = slice(None) if half is None else pl.ds(2 * half, 2)
        pz, py = (o, inner) if INNER_IS_Y[part] else (inner, o)
        return w.at[xx, pz, py, core, pl.ds(base, SIZE[part])]

    def rings_of(part, summing):
        ip, op, idev, odev = axes(part)
        found = {}

        def along_inner(xx):
            return lambda j, half=None: slab(part, xx, ip[j], op[0], half, summing)

        def along_outer(xx, i):
            return lambda j, half=None: slab(part, xx, ip[i], op[j], half, summing)

        def along_line(xx):
            return lambda j, half=None: line(part, xx, op[j], half, summing)

        for other in (0, 1) if X_FIRST[part] else (0,):
            found[f"in{other}"] = ([along_inner(ox if other else x)], 1, idev[3], idev[1])
        for g in (SUM_GROUPS if summing else GATHER_GROUPS)[part]:
            other, offsets = GROUPS[g]
            if X_FIRST[part] or not other:
                xx = ox if other else x
                if len(offsets) == 4:
                    found[g] = ([along_line(xx)], 4, odev[3], odev[1])
                else:
                    found[g] = ([along_outer(xx, i) for i in offsets], 1, odev[3], odev[1])
        return found

    def small(src, dst, sems_of, target):
        return remote(src, dst, sems_of[0], sems_of[1], target)

    ag_rings = {part: rings_of(part, False) for part in PARTS}
    ag_sem = {(part, name): (sem(), sem()) for part in PARTS for name in ag_rings[part]}
    ag_rings_sent, ag_x_sent, ag_sib_sent = (sem(), sem()), sem(), sem()
    ag_sent = {part: (ag_rings_sent[X_FIRST[part]], ag_x_sent, ag_sib_sent) for part in PARTS}
    ag_x = {part: (sem(),) if X_FIRST[part] else (sem(), sem(), sem()) for part in PARTS}
    ag_sib = {part: sem() for part in PARTS}

    def gather(step):
        part, name, *rest = step.split(".")
        if part == "small":
            small_steps[int(name)]()
            return
        ip, op, _, _ = axes(part)
        if name == "x" and rest[0] == "s":
            ref = slab(part, x, ip[0], op[0])
            remote(ref, ref, ag_sent[part][1], ag_x[part][0], xp).start()
        elif name == "x":
            await_arrival(ag_x[part][0], SIZE[part])
        elif name == "X":
            offsets = GROUPS[rest[0]][1]
            for o in STAGES[int(rest[1])]:
                whole = len(offsets) == 4
                for ref in [line(part, x, op[o])] if whole else [slab(part, x, ip[i], op[o]) for i in offsets]:
                    remote(ref, ref, ag_sent[part][1], ag_x[part][int(rest[1])], xp).start()
        elif name == "XR":
            await_arrival(ag_x[part][int(rest[0])], 4 * SIZE[part] * len(STAGES[int(rest[0])]))
        elif name == "sib":
            for o in STAGES[int(rest[1])]:
                ref = line(part, ox if int(rest[0]) else x, op[o])
                remote(ref, ref, ag_sent[part][2], ag_sib[part], sib).start()
        else:
            views, size, left, right = ag_rings[part][name]
            count = size * len(views) * SIZE[part]
            full, half = ag_sem[part, name]
            sent = ag_sent[part][0]
            if rest[0] == "start":
                for view in views:
                    remote(view(0), view(0), sent, full, right).start()
                    remote(view(0), view(0), sent, full, left).start()
            elif rest[0] == "mid":
                await_arrival(full, 2 * count)
                for view in views:
                    remote(view(3, 0), view(3, 0), sent, half, right).start()
                    remote(view(1, 1), view(1, 1), sent, half, left).start()
            else:
                await_arrival(half, count)

    spread = (
        lax.broadcasted_iota(jnp.int32, (16, 128), 1)
        == lax.broadcasted_iota(jnp.int32, (16, 128), 0) + 16 * (y * 2 + c)
    ).astype(F32)
    sm_y, sm_c, sm_z, sm_x = [(sem(), sem()) for _ in range(4)]

    cross = [(sem(), sem()) for _ in range(4)]
    seg_cross = remote(segs.at[0], segs.at[1], *cross[0], xp)
    cot_cross = remote(cotv.at[0], cotv.at[1], *cross[1], xp)
    act_cross = remote(act_out, act_hbm, *cross[2], xp)
    grad_cross = remote(grad_out, grad_hbm, *cross[3], xp)

    def small_one():
        segs[0] = jnp.broadcast_to(seg_ref[...].astype(F32), (8, ROWS))

        @pl.when(crossed)
        def _():
            seg_cross.start()

        sgb[...] = jnp.zeros_like(sgb)
        sgb[0:2, :] = gains_ref[...].astype(F32)
        sgb[2:12, :] = bias_ref[...].astype(F32)
        sb_y[0] = jnp.dot(sgb[...].astype(BF16), spread.astype(BF16), preferred_element_type=F32)
        for k in (1, 2, 3):
            small(sb_y.at[0], sb_y.at[k], sm_y, ys[k]).start()

    def small_two():
        rows = sb_y.at[pl.ds(1, 3)]
        small(rows, rows, sm_y, sib).wait_recv()
        sb_c[0] = sb_y[0] + sb_y[1] + sb_y[2] + sb_y[3]
        small(sb_c.at[0], sb_c.at[1], sm_c, sib).start()

    def small_three():
        small(sb_c.at[0], sb_c.at[1], sm_c, sib).wait_recv()
        sb_x[x, z] = sb_c[0] + sb_c[1]
        for k in (1, 2, 3):
            small(sb_x.at[x, z], sb_x.at[x, z], sm_z, zs[k]).start()

    def small_four():
        rows = sb_x.at[0, pl.ds(0, 3)]
        small(rows, rows, sm_z, sib).wait_recv()
        small(sb_x.at[x], sb_x.at[x], sm_x, xp).start()

    def small_five():
        small(sb_x.at[ox], sb_x.at[ox], sm_x, xp).wait_recv()
        for g in range(8):
            bf[:, g * 128 : (g + 1) * 128] = sb_x[g // 4, g % 4]
        qbias[:, 0:WIDTH] = bf[3:4, :]
        qbias[:, WIDTH : 2 * WIDTH] = jnp.zeros((1, WIDTH), F32)
        qbias[:, 2 * WIDTH :] = bf[4:5, :]

    def row(k):
        return bf[k : k + 1, :]

    def small_six():
        @pl.when(crossed)
        def _():
            seg_cross.wait()

        seg = jnp.broadcast_to(segs[rows_at][0:1], (ROWS, ROWS))
        qi = lax.broadcasted_iota(jnp.int32, (ROWS, ROWS), 0)
        ki = lax.broadcasted_iota(jnp.int32, (ROWS, ROWS), 1)
        allowed = (seg == seg.T) & (ki <= qi) & (lax.div(qi, 64) == lax.div(ki, 64))
        mask[...] = allowed.astype(F32)

    small_steps = {1: small_one, 2: small_two, 3: small_three, 4: small_four, 5: small_five, 6: small_six}

    for step in GATHER_ONE:
        gather(step)

    def from_sibling(part):
        await_arrival(ag_sib[part], 32 * SIZE[part])

    def fc_weights(j):
        return w[j // 2, 2 * (j % 2) : 2 * (j % 2) + 2, :, :, 4:8].reshape(WIDTH, WIDTH)

    def wout_weights(j):
        return w[:, :, :, :, 8 + j].reshape(WIDTH, WIDTH)

    halves = [pl.ds(0, 512), pl.ds(512, 512)]
    handed_on = [remote(act_out.at[:, k], hb.at[:, k], sem(), sem(), other_section) for k in halves]
    handed_back = remote(grad_out, hb, sem(), sem(), other_section)
    tok_in.wait()
    cot_in.wait()

    @pl.when(sec == 0)
    def _():
        xin[...] = datt[...].astype(F32)

    @pl.when(sec == 1)
    def _():
        for step in GATHER_TWO + GATHER_THREE:
            gather(step)

        @pl.when(crossed)
        def _():
            cot_cross.start()

        for part in PARTS:
            from_sibling(part)
        for j in range(4):
            rbuf[32 * j : 32 * j + 32] = wout_weights(j).T.reshape(32, 2, 16, WIDTH)
        rbuf[128:160] = fc_weights(0).T.reshape(32, 2, 16, WIDTH)
        for j in range(1, 4):
            turned[j - 1] = fc_weights(j).T
        for cp in handed_on:
            cp.wait_recv()
        xin[...] = hb[...].astype(F32)

    def norm(values, gain, shift):
        centre = values - jnp.mean(values, axis=-1, keepdims=True)
        rs = lax.rsqrt(jnp.mean(centre * centre, axis=-1, keepdims=True) + EPS)
        hat = centre * rs
        return hat, rs, (hat * gain + shift).astype(BF16)

    ex_sems = [(sem(), sem()) for _ in range(8)]

    def exchange(slot, src, dst):
        return remote(src, dst, *ex_sems[slot], sib)

    xh1[...], rs1[...], x1[0] = norm(xin[...], row(0), row(2))
    ex_first = exchange(0, x1.at[0], x1.at[1])
    ex_first.start()

    @pl.when(sec == 0)
    def _():
        from_sibling("Be")
        from_sibling("Ce")

    def qkv_weights(k):
        return w[k, :, :, :, 0:3].reshape(1536, WIDTH)

    for k in range(2):
        cols = slice(1536 * k, 1536 * (k + 1))
        mixed = lax.dot_general(x1[0], qkv_weights(k), NT, preferred_element_type=F32)
        qkv[:, cols] = (mixed + qbias[:, cols]).astype(BF16)

    low_lanes = lax.broadcasted_iota(jnp.int32, (ROWS, 128), 1) < HEAD
    zero = jnp.zeros((ROWS, 128), BF16)

    def pair(base, hp):
        return slice(base + hp * 128, base + hp * 128 + 128)

    def lanes_of(e):
        return low_lanes if e == 0 else ~low_lanes

    raw = []
    for hp in range(8):
        q, k = qkv[:, pair(0, hp)], qkv[:, pair(WIDTH, hp)]
        for e in range(2):
            raw.append(lax.dot_general(jnp.where(lanes_of(e), q, zero), k, NT, preferred_element_type=F32))
    seen = mask[...] > 0.5
    soft = []
    for scores in raw:
        scores = jnp.where(seen, scores * 0.125, -1e30)
        ex = jnp.exp(scores - jnp.max(scores, axis=-1, keepdims=True))
        soft.append(ex * (1.0 / jnp.sum(ex, axis=-1, keepdims=True)))
    for hp in range(8):
        v = qkv[:, pair(2 * WIDTH, hp)]
        parts = []
        for e in range(2):
            probs[2 * hp + e] = soft[2 * hp + e]
            parts.append(jnp.dot(soft[2 * hp + e].astype(BF16), v, preferred_element_type=F32))
        x2[0, :, pair(0, hp)] = jnp.where(low_lanes, parts[0], parts[1]).astype(BF16)
    ex_att = exchange(1, x2.at[0], x2.at[1])
    ex_att.start()

    def proj_weights():
        return w[:, :, :, :, 3].reshape(WIDTH, WIDTH)

    xin[...] = xin[...] + (lax.dot_general(x2[0], proj_weights(), NT, preferred_element_type=F32) + row(5))
    xh2[...], rs2[...], x3[0] = norm(xin[...], row(1), row(6))
    ex_second = exchange(2, x3.at[0], x3.at[1])
    ex_second.start()

    def up(j, pre):
        pre = pre + row(7 + j)
        square = pre * pre
        t = jnp.tanh(GC * (pre + 0.044715 * (square * pre)))
        half = 0.5 * (1.0 + t)
        x4[0, j] = (pre * half).astype(BF16)
        dgel[j] = half + (0.5 * GC) * pre * (1.0 - t * t) * (1.0 + 0.134145 * square)

    ex_act = exchange(3, x4.at[0], x4.at[1])

    @pl.when(sec == 0)
    def _():
        for step in GATHER_TWO:
            gather(step)
        for part in ("A1", "Bm", "Cm"):
            from_sibling(part)
        for j in range(4):
            up(j, lax.dot_general(x3[0], fc_weights(j), NT, preferred_element_type=F32))
        ex_act.start()
        for step in GATHER_THREE:
            gather(step)
        for part in ("A2", "Bl", "Cl"):
            from_sibling(part)
        for n in range(2):
            cols = slice(512 * n, 512 * (n + 1))
            result = xin[:, cols] + row(11)[:, cols]
            for j in range(4):
                half = w[n, :, :, :, 8 + j].reshape(512, WIDTH)
                result = result + lax.dot_general(x4[0, j], half, NT, preferred_element_type=F32)
            act_out[:, cols] = result.astype(BF16)
            handed_on[n].start()

    @pl.when(sec == 1)
    def _():
        for j in range(4):
            right = rbuf[128:160].reshape(WIDTH, WIDTH) if j == 0 else turned[j - 1]
            up(j, jnp.dot(x3[0], right, preferred_element_type=F32))
        ex_act.start()
        result = xin[...] + row(11)
        for j in range(4):
            right = rbuf[32 * j : 32 * j + 32].reshape(WIDTH, WIDTH)
            result = result + jnp.dot(x4[0, j], right, preferred_element_type=F32)
        act_out[...] = result.astype(BF16)

    for target in (ys[1], ys[3], zs[1], zs[3], xp):
        pl.semaphore_signal(room, 1, device_id=target, device_id_type=MESH)

    act_done = pltpu.make_async_copy(act_out, act_hbm, tok_sem)
    grad_done = pltpu.make_async_copy(grad_out, grad_hbm, cot_sem)

    @pl.when(crossed)
    def _():
        act_cross.start()

    @pl.when(~crossed)
    def _():
        act_done.start()

    by_x = [sum(SIZE[part] for part in PARTS if X_FIRST[part] == first) for first in (False, True)]
    await_sent(ag_rings_sent[0], 15 * by_x[0])
    await_sent(ag_rings_sent[1], 30 * by_x[1])
    await_sent(ag_x_sent, 16 * by_x[0] + by_x[1])
    await_sent(ag_sib_sent, 32 * 12)
    rows = sb_y.at[pl.ds(1, 3)]
    small(rows, rows, sm_y, sib).wait_send()
    small(sb_c.at[0], sb_c.at[1], sm_c, sib).wait_send()
    small(rows, rows, sm_z, sib).wait_send()
    small(sb_x.at[x], sb_x.at[x], sm_x, xp).wait_send()

    @pl.when(sec == 0)
    def _():
        handed_back.wait_recv()
        gf[...] = hb[...]

    @pl.when(sec == 1)
    def _():
        @pl.when(crossed)
        def _():
            cot_cross.wait()

        gf[...] = cotv[rows_at]

    def column_sum(values):
        return jnp.sum(values.astype(F32), axis=0, keepdims=True)

    sbw[...] = jnp.zeros_like(sbw)
    sbw[11:12, :] = column_sum(gf[...])
    s_out[...] = gf[...].T.reshape(2, 4, 4, 2, 1, 16, ROWS)

    def swap(slot, src, dst):
        return exchange(slot, src.at[:, :, :, oc], dst)

    ex_gf = swap(4, s_out, t_out)
    ex_gf.start()
    for j in range(4):
        d_act = jnp.dot(gf[...], wout_weights(j), preferred_element_type=F32)
        d_pre = (dgel[j] * d_act).astype(BF16)
        dpre[j] = d_pre
        sbw[7 + j : 8 + j, :] = column_sum(d_pre)
        s_fc[j // 2, 2 * (j % 2) : 2 * (j % 2) + 2] = d_pre.T.reshape(2, 4, 2, 4, 16, ROWS)
    ex_dpre = swap(5, s_fc, t_fc)
    ex_dpre.start()
    ex_dbr = swap(6, s_proj, t_proj)
    ex_dmix = swap(7, s_qkv, t_qkv)

    def lhs(mine, theirs, rows):
        return jnp.concatenate([mine.reshape(rows, ROWS), theirs.reshape(rows, ROWS)], axis=1)

    def product(left, right):
        return jnp.dot(left, right, preferred_element_type=F32).astype(BF16)

    def grads_out(xx):
        left = lhs(s_out[xx, :, :, c], t_out[xx], 256)
        for j in range(4):
            w[xx, :, :, oc, 8 + j] = product(left, x4[:, j].reshape(2 * ROWS, WIDTH)).reshape(4, 4, 16, WIDTH)

    def grads_fc(xx):
        for k in range(2):
            zz = slice(2 * k, 2 * k + 2)
            left = lhs(s_fc[xx, zz, :, c], t_fc[xx, zz], 512)
            w[xx, zz, :, c, 8:12] = product(left, x3[...].reshape(2 * ROWS, WIDTH)).reshape(2, 4, 4, 16, WIDTH)

    def grads_att(xx):
        left = lhs(s_proj[xx, :, :, c], t_proj[xx], 256)
        w[xx, :, :, c, 7] = product(left, x2[...].reshape(2 * ROWS, WIDTH)).reshape(4, 4, 16, WIDTH)
        for k in range(2):
            zz = slice(2 * k, 2 * k + 2)
            left = lhs(s_qkv[xx, zz, :, c], t_qkv[xx, zz], 384)
            w[xx, zz, :, c, 4:7] = product(left, x1[...].reshape(2 * ROWS, WIDTH)).reshape(2, 4, 3, 16, WIDTH)

    def compute(name):
        if name == "gout1":
            ex_gf.wait_recv()
            ex_act.wait_recv()
            grads_out(ox)
        elif name == "gout0":
            grads_out(x)
        elif name == "gfc1":
            ex_dpre.wait_recv()
            ex_second.wait_recv()
            grads_fc(ox)
        elif name == "gfc0":
            grads_fc(x)
        elif name == "gatt1":
            ex_first.wait_recv()
            ex_att.wait_recv()
            ex_dbr.wait_recv()
            ex_dmix.wait_recv()
            grads_att(ox)
        elif name == "gatt0":
            grads_att(x)
        elif name == "first":

            @pl.when(sec == 0)
            def _():
                back_first(grad_done.start)

    rs_rings = {part: rings_of(part, True) for part in PARTS}
    rs_sem = {(part, name): (sem(), sem()) for part in PARTS for name in rs_rings[part]}
    rs_rings_sent, rs_x_sent = (sem(), sem()), sem()
    rs_sent = {part: (rs_rings_sent[X_FIRST[part]], rs_x_sent) for part in PARTS}
    rs_x = {part: (sem(),) if X_FIRST[part] else (sem(), sem(), sem()) for part in PARTS}
    rs_at, rs_x_at = {}, {}
    for part in PARTS:
        twin = "B" + part[1]
        for name, (views, size, _, _) in rs_rings[part].items():
            rs_at[part, name] = rs_at[twin, name] if BESIDE.get(part) else arrivals(3 * size * len(views))
        rs_x_at[part] = rs_x_at[twin] if BESIDE.get(part) else arrivals(1 if X_FIRST[part] else 16)

    def room_for(part, base, count=None):
        slabs = base if count is None else pl.ds(base, count)
        return rbuf.at[slabs] if SIZE[part] == 2 else rbuf.at[slabs, pl.ds(BESIDE[part], 1)]

    def add(view, *terms, out=None):
        if len(view.shape) > 3:
            for k in range(view.shape[0]):
                add(view.at[k], *(term.at[k] for term in terms))
            return
        total = view[...].astype(F32)
        for term in terms:
            total = total + term[...].astype(F32)
        if out is None:
            view[...] = total.astype(BF16)
        else:
            out[...] = total

    def leave(part):
        first = FIRST[part]
        for piece in range(first, first + SIZE[part]):
            if piece < 3:
                target = gqkv_hbm.at[piece]
            elif piece == 3:
                target = gproj_hbm.at[0]
            elif piece < 8:
                target = gfc_hbm.at[piece - 4]
            else:
                target = gwout_hbm.at[:, pl.ds(1024 * (piece - 8), 1024)]
            pltpu.make_async_copy(gsum.at[piece], target, own_sem).start()

    def own_sum(part):
        return gsum.at[pl.ds(FIRST[part], SIZE[part])]

    def summing(step):
        part, name, *rest = step.split(".")
        if part == "small":
            small_steps[int(name)]()
            return
        if part == "comp":
            compute(name)
            return
        ip, op, _, _ = axes(part)
        if name == "x" and rest[0] == "s":
            buf = room_for(part, rs_x_at[part])
            remote(slab(part, ox, ip[0], op[0], None, True), buf, rs_sent[part][1], rs_x[part][0], xp).start()
        elif name == "x":
            await_arrival(rs_x[part][0], SIZE[part])
            add(slab(part, x, ip[0], op[0], None, True), room_for(part, rs_x_at[part]), out=own_sum(part))
            leave(part)
        elif name in ("X", "XR"):
            stage = int(rest[0])
            if name == "XR":
                await_arrival(rs_x[part][stage], 4 * SIZE[part] * len(STAGES[stage]))
            for o in STAGES[stage]:
                buf = room_for(part, rs_x_at[part] + 4 * o, 4)
                if name == "X":
                    ref = line(part, ox, op[o], None, True)
                    remote(ref, buf, rs_sent[part][1], rs_x[part][stage], xp).start()
                else:
                    add(line(part, x, op[o], None, True), buf)
        else:
            views, size, left, right = rs_rings[part][name]
            count = size * len(views) * SIZE[part]
            half, full = rs_sem[part, name]
            sent = rs_sent[part][0]

            def arrived(k):
                base = rs_at[part, name] + 3 * size * k
                if size == 1:
                    fulls = [room_for(part, base + 1), room_for(part, base + 2)]
                    if SIZE[part] == 2:
                        return [rbuf.at[base, pl.ds(0, 1)], rbuf.at[base, pl.ds(1, 1)]] + fulls
                    piece = pl.ds(BESIDE[part], 1)
                    return [rbuf.at[base, piece, :, pl.ds(512 * k, 512)] for k in (0, 1)] + fulls
                return [room_for(part, base + 2 * k, 2) for k in (0, 1)] + [room_for(part, base + 4 * k, 4) for k in (1, 2)]

            if rest[0] == "start":
                for k, view in enumerate(views):
                    remote(view(2, 0), arrived(k)[0], sent, half, right).start()
                    remote(view(2, 1), arrived(k)[1], sent, half, left).start()
            elif rest[0] == "mid":
                await_arrival(half, count)
                for k, view in enumerate(views):
                    add(view(1, 0), arrived(k)[0])
                    remote(view(1), arrived(k)[2], sent, full, right).start()
                    add(view(3, 1), arrived(k)[1])
                    remote(view(3), arrived(k)[3], sent, full, left).start()
            else:
                await_arrival(full, 2 * count)
                last = name == "in0" and not X_FIRST[part]
                for k, view in enumerate(views):
                    add(view(0), arrived(k)[2], arrived(k)[3], out=own_sum(part) if last else None)
                if last:
                    leave(part)

    sm_core, sm_xs, sm_zs, sm_ys = [(sem(), sem()) for _ in range(4)]

    def small_seven():
        for g in range(8):
            sr[g // 4, g % 4] = sbw[:, g * 128 : (g + 1) * 128]
        small(sr, sr_c, sm_core, sib).start()

    def small_eight():
        small(sr, sr_c, sm_core, sib).wait()
        sr[...] = sr[...] + sr_c[...]
        small(sr.at[ox], sr_x, sm_xs, xp).start()

    def small_nine():
        small(sr.at[ox], sr_x, sm_xs, xp).wait_recv()
        sr[x] = sr[x] + sr_x[...]
        for k in (1, 2, 3):
            small(sr.at[x, zp[k]], sr_z.at[k - 1], sm_zs, zs[k]).start()

    def small_ten():
        small(sr_z, sr_z, sm_zs, sib).wait_recv()
        sr_y[0] = sr[x, z] + sr_z[0] + sr_z[1] + sr_z[2]
        for k in (1, 2, 3):
            small(sr_y.at[0], sr_y.at[k], sm_ys, ys[k]).start()

    def small_eleven():
        rows = sr_y.at[pl.ds(1, 3)]
        small(rows, rows, sm_ys, sib).wait_recv()
        total = sr_y[0] + sr_y[1] + sr_y[2] + sr_y[3]
        picked = lax.dot_general(total, spread, NT, preferred_element_type=F32, precision=lax.Precision.HIGHEST)
        ggain_out[...] = picked[0:2, :]
        for k in range(10):
            gbias_out[k] = picked[2 + k : 3 + k, :]

    small_steps.update({7: small_seven, 8: small_eight, 9: small_nine, 10: small_ten, 11: small_eleven})

    pl.semaphore_wait(room, 5)

    @pl.when(sec == 0)
    def _():
        for step in SUM_ONE:
            summing(step)

    d_second = jnp.zeros((ROWS, WIDTH), F32)
    for j in range(4):
        d_second = d_second + jnp.dot(dpre[j], fc_weights(j), preferred_element_type=F32)

    def norm_back(d_out, hat, rs, gain):
        d_hat = d_out * gain
        mean_one = jnp.mean(d_hat, axis=-1, keepdims=True)
        mean_two = jnp.mean(d_hat * hat, axis=-1, keepdims=True)
        return rs * (d_hat - mean_one - hat * mean_two)

    sbw[1:2, :] = column_sum(d_second * xh2[...])
    sbw[6:7, :] = column_sum(d_second)
    dmid[...] = gf[...].astype(F32) + norm_back(d_second, xh2[...], rs2[...], row(1))
    dbr[...] = dmid[...].astype(BF16)
    sbw[5:6, :] = column_sum(dbr[...])
    s_proj[...] = dbr[...].T.reshape(2, 4, 4, 2, 1, 16, ROWS)
    ex_dbr.start()

    @pl.when(sec == 0)
    def _():
        for step in SUM_TWO:
            summing(step)

    datt[...] = jnp.dot(dbr[...], proj_weights(), preferred_element_type=F32).astype(BF16)
    d_probs, masked_da = [], []
    for hp in range(8):
        da, v = datt[:, pair(0, hp)], qkv[:, pair(2 * WIDTH, hp)]
        for e in range(2):
            masked_da.append(jnp.where(lanes_of(e), da, zero))
            d_probs.append(lax.dot_general(masked_da[-1], v, NT, preferred_element_type=F32))
    d_scores = []
    for h in range(16):
        p, dp_ = probs[h], d_probs[h]
        d_scores.append((p * (dp_ - jnp.sum(dp_ * p, axis=-1, keepdims=True))).astype(BF16))
    for hp in range(8):
        q, k = qkv[:, pair(0, hp)], qkv[:, pair(WIDTH, hp)]
        dq, dk, dv = [], [], []
        for e in range(2):
            h = 2 * hp + e
            dv.append(jnp.dot(probs[h].astype(BF16).T, masked_da[h], preferred_element_type=F32))
            dq.append(jnp.dot(d_scores[h], k, preferred_element_type=F32))
            dk.append(jnp.dot(d_scores[h].T, jnp.where(lanes_of(e), q, zero), preferred_element_type=F32))
        dmix[:, pair(0, hp)] = (jnp.where(low_lanes, dq[0], dq[1]) * 0.125).astype(BF16)
        dmix[:, pair(WIDTH, hp)] = ((dk[0] + dk[1]) * 0.125).astype(BF16)
        dmix[:, pair(2 * WIDTH, hp)] = (dv[0] + dv[1]).astype(BF16)
    for k in range(2):
        s_qkv[k] = dmix[:, 1536 * k : 1536 * (k + 1)].T.reshape(4, 4, 2, 3, 16, ROWS)
    ex_dmix.start()
    sbw[3:4, :] = column_sum(dmix[:, 0:WIDTH])
    sbw[4:5, :] = column_sum(dmix[:, 2 * WIDTH :])

    def back_first(then):
        d_first = jnp.dot(dmix[:, 0:1536], qkv_weights(0), preferred_element_type=F32)
        d_first = d_first + jnp.dot(dmix[:, 1536:], qkv_weights(1), preferred_element_type=F32)
        grad_out[...] = (dmid[...] + norm_back(d_first, xh1[...], rs1[...], row(0))).astype(BF16)
        then()
        sbw[0:1, :] = column_sum(d_first * xh1[...])
        sbw[2:3, :] = column_sum(d_first)

    @pl.when(sec == 1)
    def _():
        back_first(handed_back.start)
        summing(SUM_ONE[0])
        handed_back.wait_send()

        @pl.when(crossed)
        def _():
            grad_cross.start()

        @pl.when(~crossed)
        def _():
            grad_done.start()

        for step in SUM_ONE[1:] + SUM_TWO:
            summing(step)

    for step in SUM_THREE:
        summing(step)

    small_done = [
        pltpu.make_async_copy(ggain_out, ggain_hbm, sem()),
        pltpu.make_async_copy(gbias_out, gbias_hbm, sem()),
    ]
    for cp in small_done:
        cp.start()

    await_sent(rs_rings_sent[0], 15 * by_x[0])
    await_sent(rs_rings_sent[1], 30 * by_x[1])
    await_sent(rs_x_sent, 16 * by_x[0] + by_x[1])
    for cp in (ex_first, ex_att, ex_second, ex_act, ex_gf, ex_dpre, ex_dbr, ex_dmix):
        cp.wait_send()
    small(sr.at[ox], sr_x, sm_xs, xp).wait_send()
    small(sr_z, sr_z, sm_zs, sib).wait_send()
    rows = sr_y.at[pl.ds(1, 3)]
    small(rows, rows, sm_ys, sib).wait_send()

    @pl.when(sec == 0)
    def _():
        for cp in handed_on:
            cp.wait_send()

    @pl.when(crossed)
    def _():
        act_cross.wait()
        grad_cross.wait()

    @pl.when(~crossed)
    def _():
        act_done.wait()
        grad_done.wait()

    pltpu.make_async_copy(gsum, gsum, own_sem).wait()
    for cp in small_done:
        cp.wait()
    if (taken[0], taken[1]) != (SEMAPHORES, ARRIVALS):
        raise ValueError(taken)


SEMAPHORES = 210
ARRIVALS = 186


def move(*refs):
    count = len(refs) // 3
    sems = refs[-1]
    into = [pltpu.make_async_copy(refs[k], refs[2 * count + k], sems.at[0, k]) for k in range(count)]
    out = [pltpu.make_async_copy(refs[2 * count + k], refs[count + k], sems.at[1, k]) for k in range(count)]
    for cp in into:
        cp.start()
    for k in range(count):
        into[k].wait()
        out[k].start()
    for cp in out:
        cp.wait()


def local(tokens, segment_ids, gains, biases, w_qkv, w_proj, w_fc, w_out, cotangent):
    vmem = pl.BlockSpec(memory_space=pltpu.VMEM)
    hbm = pl.BlockSpec(memory_space=pl.ANY)

    def shape(*dims, dtype=F32):
        return jax.ShapeDtypeStruct(dims, dtype)

    def v(*dims, dtype=BF16):
        return pltpu.VMEM(dims, dtype)

    scratch = [
        v(2, 4, 4, 2, 12, 16, WIDTH), v(ARRIVALS, 2, 16, WIDTH),
        v(ROWS, WIDTH), v(ROWS, WIDTH), v(12, 16, WIDTH, dtype=F32), v(2, 16, dtype=F32), v(10, 1, 16, dtype=F32),
        v(2, ROWS, WIDTH), v(2, 8, ROWS, dtype=F32),
        v(ROWS, WIDTH, dtype=F32), v(2, ROWS, WIDTH), v(2, ROWS, WIDTH), v(2, ROWS, WIDTH), v(2, 4, ROWS, WIDTH),
        v(ROWS, 3 * WIDTH), v(16, ROWS, ROWS, dtype=F32), v(ROWS, WIDTH, dtype=F32), v(ROWS, WIDTH, dtype=F32),
        v(ROWS, 1, dtype=F32), v(ROWS, 1, dtype=F32), v(4, ROWS, WIDTH, dtype=F32), v(ROWS, WIDTH),
        v(4, ROWS, WIDTH), v(ROWS, WIDTH), v(ROWS, WIDTH), v(ROWS, 3 * WIDTH), v(ROWS, WIDTH, dtype=F32),
        v(ROWS, ROWS, dtype=F32), v(1, 3 * WIDTH, dtype=F32),
        v(16, WIDTH, dtype=F32), v(16, 16, dtype=F32), v(4, 16, 128, dtype=F32), v(2, 16, 128, dtype=F32),
        v(2, 4, 16, 128, dtype=F32), v(16, WIDTH, dtype=F32), v(2, 4, 16, 128, dtype=F32),
        v(2, 4, 16, 128, dtype=F32), v(4, 16, 128, dtype=F32), v(3, 16, 128, dtype=F32), v(4, 16, 128, dtype=F32),
        v(2, 4, 4, 2, 1, 16, ROWS), v(2, 4, 4, 2, 4, 16, ROWS), v(2, 4, 4, 2, 1, 16, ROWS), v(2, 4, 4, 2, 3, 16, ROWS),
        v(2, 4, 4, 1, 16, ROWS), v(2, 4, 4, 4, 16, ROWS), v(2, 4, 4, 1, 16, ROWS), v(2, 4, 4, 3, 16, ROWS),
        v(ROWS, WIDTH), v(3, WIDTH, WIDTH),
        pltpu.SemaphoreType.REGULAR, pltpu.SemaphoreType.DMA((SEMAPHORES,)),
    ]
    results = (
        shape(ROWS, WIDTH, dtype=BF16), shape(ROWS, WIDTH, dtype=BF16), shape(2, 16), shape(10, 1, 16),
        shape(3, 16, WIDTH), shape(1, 16, WIDTH), shape(4, 16, WIDTH), shape(16, 4 * WIDTH),
    )
    out = pl.pallas_call(
        kernel,
        out_shape=results,
        in_specs=[vmem, vmem, vmem] + [hbm] * 6,
        out_specs=(hbm,) * 8,
        scratch_shapes=scratch,
        compiler_params=pltpu.CompilerParams(
            collective_id=0, has_side_effects=True, vmem_limit_bytes=127 * 2**19
        ),
        name="relay",
    )(
        segment_ids.reshape(1, ROWS),
        gains[0],
        biases[0],
        tokens,
        w_qkv[0].T.reshape(3, 16, WIDTH),
        w_proj[0].T.reshape(1, 16, WIDTH),
        w_fc[0].T.reshape(4, 16, WIDTH),
        w_out[0].T,
        cotangent,
    )
    out = pl.pallas_call(
        move,
        out_shape=results,
        in_specs=[hbm] * 8,
        out_specs=(hbm,) * 8,
        scratch_shapes=[pltpu.VMEM(r.shape, r.dtype) for r in results] + [pltpu.SemaphoreType.DMA((2, 8))],
        name="move",
    )(*out)
    activations, input_grads, g_gains, g_biases, g_qkv, g_proj, g_fc, g_out = out
    return (
        activations[None],
        input_grads[None],
        g_gains[None],
        g_biases.transpose(1, 0, 2),
        g_qkv.reshape(48, WIDTH).T[None],
        g_proj.reshape(16, WIDTH).T[None],
        g_fc.reshape(64, WIDTH).T[None],
        g_out.T[None],
    )


def solution(mesh):
    weight = P("section", None, "dp")
    rows = P("section", "dp", None)
    return jax.shard_map(
        local,
        mesh=mesh,
        in_specs=(P("dp", None), P("dp")) + (weight,) * 6 + (P("dp", None),),
        out_specs=(rows, rows) + (weight,) * 6,
        check_vma=False,
    )
```

```python
import jax
import jax.numpy as jnp
from jax import lax
from jax.experimental import pallas as pl
from jax.experimental.pallas import tpu as pltpu
from jax.sharding import PartitionSpec as P

MESH = pl.DeviceIdType.MESH
F32 = jnp.float32
BF16 = jnp.bfloat16
EPS = 1e-05
ROWS = 128
WIDTH = 1024
HEAD = 64
GC = 0.7978845608028654
NT = (((1,), (1,)), ((), ()))

PARTS = ("Be", "Ce", "A1", "Bm", "Cm", "A2", "Bl", "Cl")
FIRST = {"Be": 0, "Ce": 2, "A1": 4, "Bm": 6, "Cm": 7, "A2": 8, "Bl": 10, "Cl": 11}
SIZE = {"Be": 2, "Ce": 2, "A1": 2, "Bm": 1, "Cm": 1, "A2": 2, "Bl": 1, "Cl": 1}
INNER_IS_Y = {part: part[0] == "C" or part == "A1" for part in PARTS}
X_FIRST = {part: part[0] != "A" for part in PARTS}
GROUPS = {
    "g0": (0, (0,)), "g1": (1, (0,)), "g2": (0, (1, 3)), "g3": (0, (2,)), "g4": (1, (1, 3)), "g5": (1, (2,)),
    "gA": (0, (0, 1, 2, 3)), "gB": (1, (0, 1, 2, 3)),
}
FINE = ("g0", "g1", "g2", "g3", "g4", "g5")
COARSE = ("gA", "gB")
GATHER_GROUPS = {"Be": COARSE, "Ce": COARSE, "A1": FINE, "Bm": COARSE, "Cm": COARSE, "A2": FINE, "Bl": COARSE, "Cl": COARSE}
SUM_GROUPS = {"Be": COARSE, "Ce": COARSE, "A1": COARSE, "Bm": COARSE, "Cm": COARSE, "A2": COARSE, "Bl": COARSE, "Cl": COARSE}
STAGES = ((0,), (1, 3), (2,))
SUM_AT = {part: (0, FIRST[part] + 4) if FIRST[part] < 8 else (1, FIRST[part]) for part in PARTS}
BESIDE = {"Bm": 0, "Cm": 1, "Bl": 0, "Cl": 1}

GATHER_ONE = [
    "A2.in0.start", "A1.in0.start", "A2.X.g0.0", "Be.x.s", "Ce.in0.start", "A1.g0.start", "Be.in0.start",
    "Bl.in0.start", "Cm.x.s", "A2.g0.start", "Bl.x.s", "Cl.x.s", "A1.in0.mid", "Cm.in0.start", "small.1",
    "A2.in0.mid", "A2.g2.start", "A2.X.g2.0", "Be.x.r", "A1.g0.mid", "Be.in1.start", "A1.g2.start", "Ce.x.s",
    "Cm.x.r", "Cl.in0.start", "A2.g0.mid", "Bm.x.s", "A1.X.g0.1", "Cl.x.r", "Cm.in0.mid", "A1.X.g2.0", "A2.in0.end",
    "A2.g3.start", "Bm.in0.start", "Ce.in0.mid", "Be.in0.mid", "Bl.in0.mid", "Be.in1.mid", "Ce.x.r", "A2.g2.mid",
    "Ce.in1.start", "A1.in0.end", "A1.g2.mid", "A1.g3.start", "A2.g0.end", "Be.in0.end", "Be.sib.0.0", "A2.X.g0.1",
    "Cm.in0.end", "Cm.gA.start", "A1.X.g3.0", "A1.X.g0.0", "small.2", "Ce.in0.end", "Cl.in1.start", "Cm.in1.start",
    "Be.gA.start", "Cl.in0.mid", "Bl.x.r", "Bm.x.r", "Bm.in0.mid", "A2.sib.0.0", "Bm.in1.start", "Be.in1.end",
    "A2.X.g3.0", "Ce.gA.start", "A1.g3.mid", "A1.X.g2.1", "Cm.gA.mid", "A1.sib.0.1", "A1.sib.0.0", "Ce.in1.mid",
    "Cm.in1.mid", "Be.gB.start", "Ce.in1.end", "Be.gA.mid", "Bm.in1.mid", "Ce.sib.1.0", "small.3", "Bl.in0.end",
    "Bl.sib.0.0", "Be.sib.0.1", "A2.XR.0", "A1.X.g3.1", "A1.g2.end", "Ce.gB.start", "Ce.sib.0.0", "A2.g2.end",
    "Be.sib.1.0", "Bm.in0.end", "A2.g3.mid", "A1.XR.0", "Cl.in0.end", "Cm.sib.0.0", "A2.sib.0.1", "Cm.gA.end",
    "Ce.gA.mid", "Ce.sib.0.1", "A2.X.g2.1", "Bm.in1.end", "Be.gB.mid", "A1.g0.end", "A2.X.g3.1", "A1.g3.end",
    "Cm.sib.0.1", "small.4", "A2.sib.1.0", "Cl.in1.mid", "Cm.in1.end", "A2.X.g0.2", "Bm.gB.start", "A1.XR.1",
    "A1.sib.1.1", "Bm.gA.start", "Cl.sib.0.0", "Be.sib.1.1", "A1.sib.0.2", "A1.X.g2.2", "Bl.in1.start", "Ce.gB.mid",
    "A1.X.g0.2", "Cm.sib.1.0", "A2.g3.end", "Ce.sib.1.1", "Cl.in1.end", "Bl.gA.start", "Bl.in1.mid", "A2.sib.0.2",
    "Cm.gB.start", "Be.gB.end", "Be.sib.1.2", "small.5", "Cl.gA.start", "Ce.gA.end", "Ce.sib.0.2", "Be.gA.end",
    "Be.sib.0.2", "A1.X.g3.2", "A1.sib.1.0", "Ce.gB.end", "Bl.in1.end", "Bl.gB.start", "Ce.sib.1.2", "Cm.sib.0.2",
    "Bl.sib.1.0", "Bm.gB.mid", "A2.X.g2.2", "A2.XR.1", "Cl.sib.1.0", "Bm.sib.0.0", "A2.sib.1.1", "Cl.gB.start",
    "Bm.gA.mid", "Bm.sib.1.0", "Bm.sib.1.1", "Bm.sib.0.1", "Cm.gB.mid", "Cm.sib.1.1", "small.6",
]

GATHER_TWO = [
    "A1.XR.2", "A1.sib.1.2", "Cl.gA.mid", "Bl.gB.mid", "Bl.sib.1.1", "A2.X.g3.2", "Cl.sib.0.1", "Cl.gB.mid",
    "Bl.gA.mid", "Bl.sib.0.1", "Cm.gB.end", "Cm.sib.1.2", "Bm.gA.end", "Bm.gB.end", "Bm.sib.1.2", "Bm.sib.0.2",
    "Cl.sib.1.1", "Bl.gB.end", "A2.XR.2", "A2.sib.1.2", "Cl.gA.end", "Cl.sib.0.2", "Bl.sib.1.2", "Cl.gB.end",
    "Cl.sib.1.2", "Bl.gA.end", "Bl.sib.0.2",
]

GATHER_THREE = [

]

SUM_ONE = [
    "comp.gout1", "A2.X.2", "Bl.gB.start", "Cl.gB.start", "comp.gout0", "Cl.gA.start", "Bl.gA.start", "comp.gfc1",
    "Cm.gB.start", "Bm.gB.start", "Cl.gB.mid", "Bl.gB.mid", "A1.X.2",
]

SUM_TWO = [
    "Cl.gA.mid", "Bm.gB.mid",
]

SUM_THREE = [
    "Cm.gB.mid", "Cl.gB.end", "Cl.in1.start", "A2.XR.2", "A2.gA.start", "A2.X.1", "comp.gfc0", "Cm.gA.start",
    "Bm.gA.start", "comp.gatt1", "Ce.gB.start", "Cl.gA.end", "Cl.in1.mid", "Be.gB.start", "A1.X.1", "comp.gatt0",
    "Cm.gB.end", "comp.first", "small.7", "Bm.gB.end", "Ce.gA.start", "Be.gA.start", "Cl.in1.end", "Ce.gB.mid",
    "Be.gB.mid", "Bl.gA.mid", "A1.XR.2", "A1.X.0", "Ce.gA.mid", "A1.gA.start", "Ce.gB.end", "Bl.gB.end", "Be.gA.mid",
    "Be.gB.end", "small.8", "Bl.gA.end", "Cm.gA.mid", "Cm.in1.start", "Ce.in1.start", "Bm.in1.start", "A2.X.0",
    "Bm.gA.mid", "Bl.in1.start", "A1.XR.1", "A1.gA.mid", "Be.in1.start", "Be.gA.end", "Ce.gA.end", "A2.XR.1",
    "A2.gA.mid", "A1.XR.0", "Cl.x.s", "small.9", "Bl.in0.start", "Bm.gA.end", "Bm.in1.mid", "Bl.in1.mid",
    "Be.in0.start", "Cm.gA.end", "Cm.in0.start", "Ce.in0.start", "Cl.in0.start", "Cm.in1.mid", "A1.gA.end",
    "A1.in0.start", "Ce.in1.mid", "Be.in1.mid", "Bm.in0.start", "A2.XR.0", "small.10", "A2.gA.end", "A2.in0.start",
    "Bm.in1.end", "Bm.x.s", "Bl.in0.mid", "Bl.in1.end", "Ce.in0.mid", "Bl.x.s", "Cl.in0.mid", "Cm.in1.end", "Cm.x.s",
    "Be.in0.mid", "Be.in1.end", "Be.x.s", "Cm.in0.mid", "Bm.in0.mid", "A1.in0.mid", "small.11", "Ce.in1.end",
    "Ce.x.s", "A2.in0.mid", "Bl.in0.end", "Ce.in0.end", "Bl.x.r", "Bm.in0.end", "Cm.in0.end", "Be.in0.end", "Be.x.r",
    "Bm.x.r", "Cm.x.r", "Cl.in0.end", "Cl.x.r", "Ce.x.r", "A2.in0.end", "A1.in0.end",
]


def remote(src, dst, ssem, rsem, target):
    return pltpu.make_async_remote_copy(
        src_ref=src, dst_ref=dst, send_sem=ssem, recv_sem=rsem, device_id=target, device_id_type=MESH
    )


def kernel(
    seg_ref, gains_ref, bias_ref, tok_ref, qkv_ref, proj_ref, fc_ref, wout_ref, cot_ref,
    act_hbm, grad_hbm, ggain_hbm, gbias_hbm, gqkv_hbm, gproj_hbm, gfc_hbm, gwout_hbm,
    w, rbuf, act_out, grad_out, gsum, ggain_out, gbias_out, cotv, segs,
    xin, x1, x2, x3, x4, qkv, probs, xh1, xh2, rs1, rs2, dgel, gf, dpre, dbr, datt, dmix, dmid, mask, qbias,
    bf, sgb, sb_y, sb_c, sb_x, sbw, sr, sr_c, sr_x, sr_z, sr_y,
    s_out, s_fc, s_proj, s_qkv, t_out, t_fc, t_proj, t_qkv, hb, turned, room, sems,
):
    sec = lax.axis_index("section")
    dp = lax.axis_index("dp")
    c = lax.rem(dp, 2)
    y = lax.rem(lax.div(dp, 2), 4)
    z = lax.rem(lax.div(dp, 8), 4)
    x = lax.div(dp, 32)
    ox, oc = 1 - x, 1 - c
    yp = [lax.rem(y + k, 4) for k in range(4)]
    zp = [lax.rem(z + k, 4) for k in range(4)]

    def at(px, pz, py, pc):
        return (sec, ((px * 4 + pz) * 4 + py) * 2 + pc)

    ys = [at(x, z, yp[k], c) for k in range(4)]
    zs = [at(x, zp[k], y, c) for k in range(4)]
    xp = at(ox, z, y, c)
    sib = at(x, z, y, oc)
    other_section = (1 - sec, ((lax.rem(x + c, 2) * 4 + z) * 4 + y) * 2 + c)
    crossed = (sec == 1) & (c == 1)
    rows_at = sec * c

    taken = [0, 0]

    def sem():
        taken[0] += 1
        return sems.at[taken[0] - 1]

    def arrivals(slabs):
        taken[1] += slabs
        return taken[1] - slabs

    barrier = pltpu.get_barrier_semaphore()
    partners = ys[1:] + zs[1:] + [xp, sib, other_section]
    for target in partners:
        pl.semaphore_signal(barrier, 1, device_id=target, device_id_type=MESH)
    own = w.at[x, z, y, c]
    own_sem, tok_sem, cot_sem = sem(), sem(), sem()
    pltpu.make_async_copy(qkv_ref, own.at[pl.ds(0, 3)], own_sem).start()
    pltpu.make_async_copy(proj_ref, own.at[pl.ds(3, 1)], own_sem).start()
    pltpu.make_async_copy(fc_ref, own.at[pl.ds(4, 4)], own_sem).start()
    for j in range(4):
        pltpu.make_async_copy(wout_ref.at[:, pl.ds(1024 * j, 1024)], own.at[8 + j], own_sem).start()
    tok_in = pltpu.make_async_copy(tok_ref, datt, tok_sem)
    cot_in = pltpu.make_async_copy(cot_ref, cotv.at[0], cot_sem)
    tok_in.start()
    cot_in.start()
    pl.semaphore_wait(barrier, len(partners))
    pltpu.make_async_copy(own, own, own_sem).wait()

    def slab(part, xx, i, o, half=None, summing=False):
        core, base = c, FIRST[part]
        if summing:
            core, base = (oc if SUM_AT[part][0] else c), SUM_AT[part][1]
        pz, py = (o, i) if INNER_IS_Y[part] else (i, o)
        if half is None:
            return w.at[xx, pz, py, core, pl.ds(base, SIZE[part])]
        if SIZE[part] == 2:
            return w.at[xx, pz, py, core, pl.ds(base + half, 1)]
        return w.at[xx, pz, py, core, pl.ds(base, 1), :, pl.ds(512 * half, 512)]

    def bytes_of(pieces):
        for xs in (1, 2):
            for a in (1, 2, 3, 4):
                for b in (1, 2, 3, 4):
                    k = pieces // (xs * a * b)
                    if k <= 12 and xs * a * b * k == pieces:
                        return w.at[pl.ds(0, xs), pl.ds(0, a), pl.ds(0, b), 0, pl.ds(0, k)]

    def await_arrival(which, count):
        ref = bytes_of(count)
        remote(ref, ref, which, which, sib).wait_recv()

    def await_sent(which, count):
        ref = bytes_of(count)
        remote(ref, ref, which, which, sib).wait_send()

    def axes(part):
        return (yp, zp, ys, zs) if INNER_IS_Y[part] else (zp, yp, zs, ys)

    def line(part, xx, o, half=None, summing=False):
        core, base = c, FIRST[part]
        if summing:
            core, base = (oc if SUM_AT[part][0] else c), SUM_AT[part][1]
        inner = slice(None) if half is None else pl.ds(2 * half, 2)
        pz, py = (o, inner) if INNER_IS_Y[part] else (inner, o)
        return w.at[xx, pz, py, core, pl.ds(base, SIZE[part])]

    def rings_of(part, summing):
        ip, op, idev, odev = axes(part)
        found = {}

        def along_inner(xx):
            return lambda j, half=None: slab(part, xx, ip[j], op[0], half, summing)

        def along_outer(xx, i):
            return lambda j, half=None: slab(part, xx, ip[i], op[j], half, summing)

        def along_line(xx):
            return lambda j, half=None: line(part, xx, op[j], half, summing)

        for other in (0, 1) if X_FIRST[part] else (0,):
            found[f"in{other}"] = ([along_inner(ox if other else x)], 1, idev[3], idev[1])
        for g in (SUM_GROUPS if summing else GATHER_GROUPS)[part]:
            other, offsets = GROUPS[g]
            if X_FIRST[part] or not other:
                xx = ox if other else x
                if len(offsets) == 4:
                    found[g] = ([along_line(xx)], 4, odev[3], odev[1])
                else:
                    found[g] = ([along_outer(xx, i) for i in offsets], 1, odev[3], odev[1])
        return found

    def small(src, dst, sems_of, target):
        return remote(src, dst, sems_of[0], sems_of[1], target)

    ag_rings = {part: rings_of(part, False) for part in PARTS}
    ag_sem = {(part, name): (sem(), sem()) for part in PARTS for name in ag_rings[part]}
    ag_rings_sent, ag_x_sent, ag_sib_sent = (sem(), sem()), sem(), sem()
    ag_sent = {part: (ag_rings_sent[X_FIRST[part]], ag_x_sent, ag_sib_sent) for part in PARTS}
    ag_x = {part: (sem(),) if X_FIRST[part] else (sem(), sem(), sem()) for part in PARTS}
    ag_sib = {part: sem() for part in PARTS}

    def gather(step):
        part, name, *rest = step.split(".")
        if part == "small":
            small_steps[int(name)]()
            return
        ip, op, _, _ = axes(part)
        if name == "x" and rest[0] == "s":
            ref = slab(part, x, ip[0], op[0])
            remote(ref, ref, ag_sent[part][1], ag_x[part][0], xp).start()
        elif name == "x":
            await_arrival(ag_x[part][0], SIZE[part])
        elif name == "X":
            offsets = GROUPS[rest[0]][1]
            for o in STAGES[int(rest[1])]:
                whole = len(offsets) == 4
                for ref in [line(part, x, op[o])] if whole else [slab(part, x, ip[i], op[o]) for i in offsets]:
                    remote(ref, ref, ag_sent[part][1], ag_x[part][int(rest[1])], xp).start()
        elif name == "XR":
            await_arrival(ag_x[part][int(rest[0])], 4 * SIZE[part] * len(STAGES[int(rest[0])]))
        elif name == "sib":
            for o in STAGES[int(rest[1])]:
                ref = line(part, ox if int(rest[0]) else x, op[o])
                remote(ref, ref, ag_sent[part][2], ag_sib[part], sib).start()
        else:
            views, size, left, right = ag_rings[part][name]
            count = size * len(views) * SIZE[part]
            full, half = ag_sem[part, name]
            sent = ag_sent[part][0]
            if rest[0] == "start":
                for view in views:
                    remote(view(0), view(0), sent, full, right).start()
                    remote(view(0), view(0), sent, full, left).start()
            elif rest[0] == "mid":
                await_arrival(full, 2 * count)
                for view in views:
                    remote(view(3, 0), view(3, 0), sent, half, right).start()
                    remote(view(1, 1), view(1, 1), sent, half, left).start()
            else:
                await_arrival(half, count)

    spread = (
        lax.broadcasted_iota(jnp.int32, (16, 128), 1)
        == lax.broadcasted_iota(jnp.int32, (16, 128), 0) + 16 * (y * 2 + c)
    ).astype(F32)
    sm_y, sm_c, sm_z, sm_x = [(sem(), sem()) for _ in range(4)]

    cross = [(sem(), sem()) for _ in range(4)]
    seg_cross = remote(segs.at[0], segs.at[1], *cross[0], xp)
    cot_cross = remote(cotv.at[0], cotv.at[1], *cross[1], xp)
    act_cross = remote(act_out, act_hbm, *cross[2], xp)
    grad_cross = remote(grad_out, grad_hbm, *cross[3], xp)

    def small_one():
        segs[0] = jnp.broadcast_to(seg_ref[...].astype(F32), (8, ROWS))

        @pl.when(crossed)
        def _():
            seg_cross.start()

        sgb[...] = jnp.zeros_like(sgb)
        sgb[0:2, :] = gains_ref[...].astype(F32)
        sgb[2:12, :] = bias_ref[...].astype(F32)
        sb_y[0] = jnp.dot(sgb[...].astype(BF16), spread.astype(BF16), preferred_element_type=F32)
        for k in (1, 2, 3):
            small(sb_y.at[0], sb_y.at[k], sm_y, ys[k]).start()

    def small_two():
        rows = sb_y.at[pl.ds(1, 3)]
        small(rows, rows, sm_y, sib).wait_recv()
        sb_c[0] = sb_y[0] + sb_y[1] + sb_y[2] + sb_y[3]
        small(sb_c.at[0], sb_c.at[1], sm_c, sib).start()

    def small_three():
        small(sb_c.at[0], sb_c.at[1], sm_c, sib).wait_recv()
        sb_x[x, z] = sb_c[0] + sb_c[1]
        for k in (1, 2, 3):
            small(sb_x.at[x, z], sb_x.at[x, z], sm_z, zs[k]).start()

    def small_four():
        rows = sb_x.at[0, pl.ds(0, 3)]
        small(rows, rows, sm_z, sib).wait_recv()
        small(sb_x.at[x], sb_x.at[x], sm_x, xp).start()

    def small_five():
        small(sb_x.at[ox], sb_x.at[ox], sm_x, xp).wait_recv()
        for g in range(8):
            bf[:, g * 128 : (g + 1) * 128] = sb_x[g // 4, g % 4]
        qbias[:, 0:WIDTH] = bf[3:4, :]
        qbias[:, WIDTH : 2 * WIDTH] = jnp.zeros((1, WIDTH), F32)
        qbias[:, 2 * WIDTH :] = bf[4:5, :]

    def row(k):
        return bf[k : k + 1, :]

    def small_six():
        @pl.when(crossed)
        def _():
            seg_cross.wait()

        seg = jnp.broadcast_to(segs[rows_at][0:1], (ROWS, ROWS))
        qi = lax.broadcasted_iota(jnp.int32, (ROWS, ROWS), 0)
        ki = lax.broadcasted_iota(jnp.int32, (ROWS, ROWS), 1)
        allowed = (seg == seg.T) & (ki <= qi) & (lax.div(qi, 64) == lax.div(ki, 64))
        mask[...] = allowed.astype(F32)

    small_steps = {1: small_one, 2: small_two, 3: small_three, 4: small_four, 5: small_five, 6: small_six}

    for step in GATHER_ONE:
        gather(step)

    by_x = [sum(SIZE[part] for part in PARTS if X_FIRST[part] == first) for first in (False, True)]

    def gather_sent():
        await_sent(ag_rings_sent[0], 15 * by_x[0])
        await_sent(ag_rings_sent[1], 30 * by_x[1])
        await_sent(ag_x_sent, 16 * by_x[0] + by_x[1])
        await_sent(ag_sib_sent, 32 * 12)
        rows = sb_y.at[pl.ds(1, 3)]
        small(rows, rows, sm_y, sib).wait_send()
        small(sb_c.at[0], sb_c.at[1], sm_c, sib).wait_send()
        small(rows, rows, sm_z, sib).wait_send()
        small(sb_x.at[x], sb_x.at[x], sm_x, xp).wait_send()

    def column_sum(values):
        return jnp.sum(values.astype(F32), axis=0, keepdims=True)

    ex_sems = [(sem(), sem()) for _ in range(8)]

    def exchange(slot, src, dst):
        return remote(src, dst, *ex_sems[slot], sib)

    def swap(slot, src, dst):
        return exchange(slot, src.at[:, :, :, oc], dst)

    ex_gf = swap(4, s_out, t_out)

    def start_back():
        sbw[...] = jnp.zeros_like(sbw)
        sbw[11:12, :] = column_sum(gf[...])
        s_out[...] = gf[...].T.reshape(2, 4, 4, 2, 1, 16, ROWS)
        ex_gf.start()

    def from_sibling(part):
        await_arrival(ag_sib[part], 32 * SIZE[part])

    def fc_weights(j):
        return w[j // 2, 2 * (j % 2) : 2 * (j % 2) + 2, :, :, 4:8].reshape(WIDTH, WIDTH)

    def wout_weights(j):
        return w[:, :, :, :, 8 + j].reshape(WIDTH, WIDTH)

    halves = [pl.ds(0, 512), pl.ds(512, 512)]
    handed_on = [remote(act_out.at[:, k], hb.at[:, k], sem(), sem(), other_section) for k in halves]
    handed_back = remote(grad_out, hb, sem(), sem(), other_section)
    tok_in.wait()
    cot_in.wait()

    @pl.when(sec == 0)
    def _():
        xin[...] = datt[...].astype(F32)

    @pl.when(sec == 1)
    def _():
        for step in GATHER_TWO + GATHER_THREE:
            gather(step)

        @pl.when(crossed)
        def _():
            cot_cross.start()

        for part in PARTS:
            from_sibling(part)
        for j in range(4):
            rbuf[32 * j : 32 * j + 32] = wout_weights(j).T.reshape(32, 2, 16, WIDTH)
        rbuf[128:160] = fc_weights(0).T.reshape(32, 2, 16, WIDTH)
        for j in range(1, 4):
            turned[j - 1] = fc_weights(j).T
        @pl.when(crossed)
        def _():
            cot_cross.wait()

        gf[...] = cotv[rows_at]
        start_back()
        gather_sent()
        for cp in handed_on:
            cp.wait_recv()
        xin[...] = hb[...].astype(F32)

    def norm(values, gain, shift):
        centre = values - jnp.mean(values, axis=-1, keepdims=True)
        rs = lax.rsqrt(jnp.mean(centre * centre, axis=-1, keepdims=True) + EPS)
        hat = centre * rs
        return hat, rs, (hat * gain + shift).astype(BF16)

    xh1[...], rs1[...], x1[0] = norm(xin[...], row(0), row(2))
    ex_first = exchange(0, x1.at[0], x1.at[1])
    ex_first.start()

    @pl.when(sec == 0)
    def _():
        from_sibling("Be")
        from_sibling("Ce")

    def qkv_weights(k):
        return w[k, :, :, :, 0:3].reshape(1536, WIDTH)

    for k in range(2):
        cols = slice(1536 * k, 1536 * (k + 1))
        mixed = lax.dot_general(x1[0], qkv_weights(k), NT, preferred_element_type=F32)
        qkv[:, cols] = (mixed + qbias[:, cols]).astype(BF16)

    low_lanes = lax.broadcasted_iota(jnp.int32, (ROWS, 128), 1) < HEAD
    zero = jnp.zeros((ROWS, 128), BF16)

    def pair(base, hp):
        return slice(base + hp * 128, base + hp * 128 + 128)

    def lanes_of(e):
        return low_lanes if e == 0 else ~low_lanes

    raw = []
    for hp in range(8):
        q, k = qkv[:, pair(0, hp)], qkv[:, pair(WIDTH, hp)]
        for e in range(2):
            raw.append(lax.dot_general(jnp.where(lanes_of(e), q, zero), k, NT, preferred_element_type=F32))
    seen = mask[...] > 0.5
    soft = []
    for scores in raw:
        scores = jnp.where(seen, scores * 0.125, -1e30)
        ex = jnp.exp(scores - jnp.max(scores, axis=-1, keepdims=True))
        soft.append(ex * (1.0 / jnp.sum(ex, axis=-1, keepdims=True)))
    for hp in range(8):
        v = qkv[:, pair(2 * WIDTH, hp)]
        parts = []
        for e in range(2):
            probs[2 * hp + e] = soft[2 * hp + e]
            parts.append(jnp.dot(soft[2 * hp + e].astype(BF16), v, preferred_element_type=F32))
        x2[0, :, pair(0, hp)] = jnp.where(low_lanes, parts[0], parts[1]).astype(BF16)
    ex_att = exchange(1, x2.at[0], x2.at[1])
    ex_att.start()

    def proj_weights():
        return w[:, :, :, :, 3].reshape(WIDTH, WIDTH)

    xin[...] = xin[...] + (lax.dot_general(x2[0], proj_weights(), NT, preferred_element_type=F32) + row(5))
    xh2[...], rs2[...], x3[0] = norm(xin[...], row(1), row(6))
    ex_second = exchange(2, x3.at[0], x3.at[1])
    ex_second.start()

    def up(j, pre):
        pre = pre + row(7 + j)
        square = pre * pre
        t = jnp.tanh(GC * (pre + 0.044715 * (square * pre)))
        half = 0.5 * (1.0 + t)
        x4[0, j] = (pre * half).astype(BF16)
        dgel[j] = half + (0.5 * GC) * pre * (1.0 - t * t) * (1.0 + 0.134145 * square)

    ex_act = exchange(3, x4.at[0], x4.at[1])

    @pl.when(sec == 0)
    def _():
        for step in GATHER_TWO:
            gather(step)
        for part in ("A1", "Bm", "Cm"):
            from_sibling(part)
        for j in range(4):
            up(j, lax.dot_general(x3[0], fc_weights(j), NT, preferred_element_type=F32))
        ex_act.start()
        for step in GATHER_THREE:
            gather(step)
        for part in ("A2", "Bl", "Cl"):
            from_sibling(part)
        for n in range(2):
            cols = slice(512 * n, 512 * (n + 1))
            result = xin[:, cols] + row(11)[:, cols]
            for j in range(4):
                half = w[n, :, :, :, 8 + j].reshape(512, WIDTH)
                result = result + lax.dot_general(x4[0, j], half, NT, preferred_element_type=F32)
            act_out[:, cols] = result.astype(BF16)
            handed_on[n].start()

    @pl.when(sec == 1)
    def _():
        for j in range(4):
            right = rbuf[128:160].reshape(WIDTH, WIDTH) if j == 0 else turned[j - 1]
            up(j, jnp.dot(x3[0], right, preferred_element_type=F32))
        ex_act.start()
        result = xin[...] + row(11)
        for j in range(4):
            right = rbuf[32 * j : 32 * j + 32].reshape(WIDTH, WIDTH)
            result = result + jnp.dot(x4[0, j], right, preferred_element_type=F32)
        act_out[...] = result.astype(BF16)

    for target in (ys[1], ys[3], zs[1], zs[3], xp):
        pl.semaphore_signal(room, 1, device_id=target, device_id_type=MESH)

    act_done = pltpu.make_async_copy(act_out, act_hbm, tok_sem)
    grad_done = pltpu.make_async_copy(grad_out, grad_hbm, cot_sem)

    @pl.when(crossed)
    def _():
        act_cross.start()

    @pl.when(~crossed)
    def _():
        act_done.start()

    @pl.when(sec == 0)
    def _():
        gather_sent()

    @pl.when(sec == 0)
    def _():
        handed_back.wait_recv()
        gf[...] = hb[...]
        start_back()

    for j in range(4):
        d_act = jnp.dot(gf[...], wout_weights(j), preferred_element_type=F32)
        d_pre = (dgel[j] * d_act).astype(BF16)
        dpre[j] = d_pre
        sbw[7 + j : 8 + j, :] = column_sum(d_pre)
        s_fc[j // 2, 2 * (j % 2) : 2 * (j % 2) + 2] = d_pre.T.reshape(2, 4, 2, 4, 16, ROWS)
    ex_dpre = swap(5, s_fc, t_fc)
    ex_dpre.start()
    ex_dbr = swap(6, s_proj, t_proj)
    ex_dmix = swap(7, s_qkv, t_qkv)

    def lhs(mine, theirs, rows):
        return jnp.concatenate([mine.reshape(rows, ROWS), theirs.reshape(rows, ROWS)], axis=1)

    def product(left, right):
        return jnp.dot(left, right, preferred_element_type=F32).astype(BF16)

    def grads_out(xx):
        left = lhs(s_out[xx, :, :, c], t_out[xx], 256)
        for j in range(4):
            w[xx, :, :, oc, 8 + j] = product(left, x4[:, j].reshape(2 * ROWS, WIDTH)).reshape(4, 4, 16, WIDTH)

    def grads_fc(xx):
        for k in range(2):
            zz = slice(2 * k, 2 * k + 2)
            left = lhs(s_fc[xx, zz, :, c], t_fc[xx, zz], 512)
            w[xx, zz, :, c, 8:12] = product(left, x3[...].reshape(2 * ROWS, WIDTH)).reshape(2, 4, 4, 16, WIDTH)

    def grads_att(xx):
        left = lhs(s_proj[xx, :, :, c], t_proj[xx], 256)
        w[xx, :, :, c, 7] = product(left, x2[...].reshape(2 * ROWS, WIDTH)).reshape(4, 4, 16, WIDTH)
        for k in range(2):
            zz = slice(2 * k, 2 * k + 2)
            left = lhs(s_qkv[xx, zz, :, c], t_qkv[xx, zz], 384)
            w[xx, zz, :, c, 4:7] = product(left, x1[...].reshape(2 * ROWS, WIDTH)).reshape(2, 4, 3, 16, WIDTH)

    def compute(name):
        if name == "gout1":
            ex_gf.wait_recv()
            ex_act.wait_recv()
            grads_out(ox)
        elif name == "gout0":
            grads_out(x)
        elif name == "gfc1":
            ex_dpre.wait_recv()
            ex_second.wait_recv()
            grads_fc(ox)
        elif name == "gfc0":
            grads_fc(x)
        elif name == "gatt1":
            ex_first.wait_recv()
            ex_att.wait_recv()
            ex_dbr.wait_recv()
            ex_dmix.wait_recv()
            grads_att(ox)
        elif name == "gatt0":
            grads_att(x)
        elif name == "first":

            @pl.when(sec == 0)
            def _():
                back_first(grad_done.start)

    rs_rings = {part: rings_of(part, True) for part in PARTS}
    rs_sem = {(part, name): (sem(), sem()) for part in PARTS for name in rs_rings[part]}
    rs_rings_sent, rs_x_sent = (sem(), sem()), sem()
    rs_sent = {part: (rs_rings_sent[X_FIRST[part]], rs_x_sent) for part in PARTS}
    rs_x = {part: (sem(),) if X_FIRST[part] else (sem(), sem(), sem()) for part in PARTS}
    rs_at, rs_x_at = {}, {}
    for part in PARTS:
        twin = "B" + part[1]
        for name, (views, size, _, _) in rs_rings[part].items():
            rs_at[part, name] = rs_at[twin, name] if BESIDE.get(part) else arrivals(3 * size * len(views))
        rs_x_at[part] = rs_x_at[twin] if BESIDE.get(part) else arrivals(1 if X_FIRST[part] else 16)

    def room_for(part, base, count=None):
        slabs = base if count is None else pl.ds(base, count)
        return rbuf.at[slabs] if SIZE[part] == 2 else rbuf.at[slabs, pl.ds(BESIDE[part], 1)]

    def add(view, *terms, out=None):
        if len(view.shape) > 3:
            for k in range(view.shape[0]):
                add(view.at[k], *(term.at[k] for term in terms))
            return
        total = view[...].astype(F32)
        for term in terms:
            total = total + term[...].astype(F32)
        if out is None:
            view[...] = total.astype(BF16)
        else:
            out[...] = total

    def leave(part):
        first = FIRST[part]
        for piece in range(first, first + SIZE[part]):
            if piece < 3:
                target = gqkv_hbm.at[piece]
            elif piece == 3:
                target = gproj_hbm.at[0]
            elif piece < 8:
                target = gfc_hbm.at[piece - 4]
            else:
                target = gwout_hbm.at[:, pl.ds(1024 * (piece - 8), 1024)]
            pltpu.make_async_copy(gsum.at[piece], target, own_sem).start()

    def own_sum(part):
        return gsum.at[pl.ds(FIRST[part], SIZE[part])]

    def summing(step):
        part, name, *rest = step.split(".")
        if part == "small":
            small_steps[int(name)]()
            return
        if part == "comp":
            compute(name)
            return
        ip, op, _, _ = axes(part)
        if name == "x" and rest[0] == "s":
            buf = room_for(part, rs_x_at[part])
            remote(slab(part, ox, ip[0], op[0], None, True), buf, rs_sent[part][1], rs_x[part][0], xp).start()
        elif name == "x":
            await_arrival(rs_x[part][0], SIZE[part])
            add(slab(part, x, ip[0], op[0], None, True), room_for(part, rs_x_at[part]), out=own_sum(part))
            leave(part)
        elif name in ("X", "XR"):
            stage = int(rest[0])
            if name == "XR":
                await_arrival(rs_x[part][stage], 4 * SIZE[part] * len(STAGES[stage]))
            for o in STAGES[stage]:
                buf = room_for(part, rs_x_at[part] + 4 * o, 4)
                if name == "X":
                    ref = line(part, ox, op[o], None, True)
                    remote(ref, buf, rs_sent[part][1], rs_x[part][stage], xp).start()
                else:
                    add(line(part, x, op[o], None, True), buf)
        else:
            views, size, left, right = rs_rings[part][name]
            count = size * len(views) * SIZE[part]
            half, full = rs_sem[part, name]
            sent = rs_sent[part][0]

            def arrived(k):
                base = rs_at[part, name] + 3 * size * k
                if size == 1:
                    fulls = [room_for(part, base + 1), room_for(part, base + 2)]
                    if SIZE[part] == 2:
                        return [rbuf.at[base, pl.ds(0, 1)], rbuf.at[base, pl.ds(1, 1)]] + fulls
                    piece = pl.ds(BESIDE[part], 1)
                    return [rbuf.at[base, piece, :, pl.ds(512 * k, 512)] for k in (0, 1)] + fulls
                return [room_for(part, base + 2 * k, 2) for k in (0, 1)] + [room_for(part, base + 4 * k, 4) for k in (1, 2)]

            if rest[0] == "start":
                for k, view in enumerate(views):
                    remote(view(2, 0), arrived(k)[0], sent, half, right).start()
                    remote(view(2, 1), arrived(k)[1], sent, half, left).start()
            elif rest[0] == "mid":
                await_arrival(half, count)
                for k, view in enumerate(views):
                    add(view(1, 0), arrived(k)[0])
                    remote(view(1), arrived(k)[2], sent, full, right).start()
                    add(view(3, 1), arrived(k)[1])
                    remote(view(3), arrived(k)[3], sent, full, left).start()
            else:
                await_arrival(full, 2 * count)
                last = name == "in0" and not X_FIRST[part]
                for k, view in enumerate(views):
                    add(view(0), arrived(k)[2], arrived(k)[3], out=own_sum(part) if last else None)
                if last:
                    leave(part)

    sm_core, sm_xs, sm_zs, sm_ys = [(sem(), sem()) for _ in range(4)]

    def small_seven():
        for g in range(8):
            sr[g // 4, g % 4] = sbw[:, g * 128 : (g + 1) * 128]
        small(sr, sr_c, sm_core, sib).start()

    def small_eight():
        small(sr, sr_c, sm_core, sib).wait()
        sr[...] = sr[...] + sr_c[...]
        small(sr.at[ox], sr_x, sm_xs, xp).start()

    def small_nine():
        small(sr.at[ox], sr_x, sm_xs, xp).wait_recv()
        sr[x] = sr[x] + sr_x[...]
        for k in (1, 2, 3):
            small(sr.at[x, zp[k]], sr_z.at[k - 1], sm_zs, zs[k]).start()

    def small_ten():
        small(sr_z, sr_z, sm_zs, sib).wait_recv()
        sr_y[0] = sr[x, z] + sr_z[0] + sr_z[1] + sr_z[2]
        for k in (1, 2, 3):
            small(sr_y.at[0], sr_y.at[k], sm_ys, ys[k]).start()

    def small_eleven():
        rows = sr_y.at[pl.ds(1, 3)]
        small(rows, rows, sm_ys, sib).wait_recv()
        total = sr_y[0] + sr_y[1] + sr_y[2] + sr_y[3]
        picked = lax.dot_general(total, spread, NT, preferred_element_type=F32, precision=lax.Precision.HIGHEST)
        ggain_out[...] = picked[0:2, :]
        for k in range(10):
            gbias_out[k] = picked[2 + k : 3 + k, :]

    small_steps.update({7: small_seven, 8: small_eight, 9: small_nine, 10: small_ten, 11: small_eleven})

    pl.semaphore_wait(room, 5)

    @pl.when(sec == 0)
    def _():
        for step in SUM_ONE:
            summing(step)

    d_second = jnp.zeros((ROWS, WIDTH), F32)
    for j in range(4):
        d_second = d_second + jnp.dot(dpre[j], fc_weights(j), preferred_element_type=F32)

    def norm_back(d_out, hat, rs, gain):
        d_hat = d_out * gain
        mean_one = jnp.mean(d_hat, axis=-1, keepdims=True)
        mean_two = jnp.mean(d_hat * hat, axis=-1, keepdims=True)
        return rs * (d_hat - mean_one - hat * mean_two)

    sbw[1:2, :] = column_sum(d_second * xh2[...])
    sbw[6:7, :] = column_sum(d_second)
    dmid[...] = gf[...].astype(F32) + norm_back(d_second, xh2[...], rs2[...], row(1))
    dbr[...] = dmid[...].astype(BF16)
    sbw[5:6, :] = column_sum(dbr[...])
    s_proj[...] = dbr[...].T.reshape(2, 4, 4, 2, 1, 16, ROWS)
    ex_dbr.start()

    @pl.when(sec == 0)
    def _():
        for step in SUM_TWO:
            summing(step)

    datt[...] = jnp.dot(dbr[...], proj_weights(), preferred_element_type=F32).astype(BF16)
    d_probs, masked_da = [], []
    for hp in range(8):
        da, v = datt[:, pair(0, hp)], qkv[:, pair(2 * WIDTH, hp)]
        for e in range(2):
            masked_da.append(jnp.where(lanes_of(e), da, zero))
            d_probs.append(lax.dot_general(masked_da[-1], v, NT, preferred_element_type=F32))
    d_scores = []
    for h in range(16):
        p, dp_ = probs[h], d_probs[h]
        d_scores.append((p * (dp_ - jnp.sum(dp_ * p, axis=-1, keepdims=True))).astype(BF16))
    for hp in range(8):
        q, k = qkv[:, pair(0, hp)], qkv[:, pair(WIDTH, hp)]
        dq, dk, dv = [], [], []
        for e in range(2):
            h = 2 * hp + e
            dv.append(jnp.dot(probs[h].astype(BF16).T, masked_da[h], preferred_element_type=F32))
            dq.append(jnp.dot(d_scores[h], k, preferred_element_type=F32))
            dk.append(jnp.dot(d_scores[h].T, jnp.where(lanes_of(e), q, zero), preferred_element_type=F32))
        dmix[:, pair(0, hp)] = (jnp.where(low_lanes, dq[0], dq[1]) * 0.125).astype(BF16)
        dmix[:, pair(WIDTH, hp)] = ((dk[0] + dk[1]) * 0.125).astype(BF16)
        dmix[:, pair(2 * WIDTH, hp)] = (dv[0] + dv[1]).astype(BF16)
    for k in range(2):
        s_qkv[k] = dmix[:, 1536 * k : 1536 * (k + 1)].T.reshape(4, 4, 2, 3, 16, ROWS)
    ex_dmix.start()
    sbw[3:4, :] = column_sum(dmix[:, 0:WIDTH])
    sbw[4:5, :] = column_sum(dmix[:, 2 * WIDTH :])

    def back_first(then):
        d_first = jnp.dot(dmix[:, 0:1536], qkv_weights(0), preferred_element_type=F32)
        d_first = d_first + jnp.dot(dmix[:, 1536:], qkv_weights(1), preferred_element_type=F32)
        grad_out[...] = (dmid[...] + norm_back(d_first, xh1[...], rs1[...], row(0))).astype(BF16)
        then()
        sbw[0:1, :] = column_sum(d_first * xh1[...])
        sbw[2:3, :] = column_sum(d_first)

    @pl.when(sec == 1)
    def _():
        back_first(handed_back.start)
        summing(SUM_ONE[0])
        handed_back.wait_send()

        @pl.when(crossed)
        def _():
            grad_cross.start()

        @pl.when(~crossed)
        def _():
            grad_done.start()

        for step in SUM_ONE[1:] + SUM_TWO:
            summing(step)

    for step in SUM_THREE:
        summing(step)

    small_done = [
        pltpu.make_async_copy(ggain_out, ggain_hbm, sem()),
        pltpu.make_async_copy(gbias_out, gbias_hbm, sem()),
    ]
    for cp in small_done:
        cp.start()

    await_sent(rs_rings_sent[0], 15 * by_x[0])
    await_sent(rs_rings_sent[1], 30 * by_x[1])
    await_sent(rs_x_sent, 16 * by_x[0] + by_x[1])
    for cp in (ex_first, ex_att, ex_second, ex_act, ex_gf, ex_dpre, ex_dbr, ex_dmix):
        cp.wait_send()
    small(sr.at[ox], sr_x, sm_xs, xp).wait_send()
    small(sr_z, sr_z, sm_zs, sib).wait_send()
    rows = sr_y.at[pl.ds(1, 3)]
    small(rows, rows, sm_ys, sib).wait_send()

    @pl.when(sec == 0)
    def _():
        for cp in handed_on:
            cp.wait_send()

    @pl.when(crossed)
    def _():
        act_cross.wait()
        grad_cross.wait()

    @pl.when(~crossed)
    def _():
        act_done.wait()
        grad_done.wait()

    pltpu.make_async_copy(gsum, gsum, own_sem).wait()
    for cp in small_done:
        cp.wait()
    if (taken[0], taken[1]) != (SEMAPHORES, ARRIVALS):
        raise ValueError(taken)


SEMAPHORES = 210
ARRIVALS = 186


def move(*refs):
    count = len(refs) // 3
    sems = refs[-1]
    into = [pltpu.make_async_copy(refs[k], refs[2 * count + k], sems.at[0, k]) for k in range(count)]
    out = [pltpu.make_async_copy(refs[2 * count + k], refs[count + k], sems.at[1, k]) for k in range(count)]
    for cp in into:
        cp.start()
    for k in range(count):
        into[k].wait()
        out[k].start()
    for cp in out:
        cp.wait()


def local(tokens, segment_ids, gains, biases, w_qkv, w_proj, w_fc, w_out, cotangent):
    vmem = pl.BlockSpec(memory_space=pltpu.VMEM)
    hbm = pl.BlockSpec(memory_space=pl.ANY)

    def shape(*dims, dtype=F32):
        return jax.ShapeDtypeStruct(dims, dtype)

    def v(*dims, dtype=BF16):
        return pltpu.VMEM(dims, dtype)

    scratch = [
        v(2, 4, 4, 2, 12, 16, WIDTH), v(ARRIVALS, 2, 16, WIDTH),
        v(ROWS, WIDTH), v(ROWS, WIDTH), v(12, 16, WIDTH, dtype=F32), v(2, 16, dtype=F32), v(10, 1, 16, dtype=F32),
        v(2, ROWS, WIDTH), v(2, 8, ROWS, dtype=F32),
        v(ROWS, WIDTH, dtype=F32), v(2, ROWS, WIDTH), v(2, ROWS, WIDTH), v(2, ROWS, WIDTH), v(2, 4, ROWS, WIDTH),
        v(ROWS, 3 * WIDTH), v(16, ROWS, ROWS, dtype=F32), v(ROWS, WIDTH, dtype=F32), v(ROWS, WIDTH, dtype=F32),
        v(ROWS, 1, dtype=F32), v(ROWS, 1, dtype=F32), v(4, ROWS, WIDTH, dtype=F32), v(ROWS, WIDTH),
        v(4, ROWS, WIDTH), v(ROWS, WIDTH), v(ROWS, WIDTH), v(ROWS, 3 * WIDTH), v(ROWS, WIDTH, dtype=F32),
        v(ROWS, ROWS, dtype=F32), v(1, 3 * WIDTH, dtype=F32),
        v(16, WIDTH, dtype=F32), v(16, 16, dtype=F32), v(4, 16, 128, dtype=F32), v(2, 16, 128, dtype=F32),
        v(2, 4, 16, 128, dtype=F32), v(16, WIDTH, dtype=F32), v(2, 4, 16, 128, dtype=F32),
        v(2, 4, 16, 128, dtype=F32), v(4, 16, 128, dtype=F32), v(3, 16, 128, dtype=F32), v(4, 16, 128, dtype=F32),
        v(2, 4, 4, 2, 1, 16, ROWS), v(2, 4, 4, 2, 4, 16, ROWS), v(2, 4, 4, 2, 1, 16, ROWS), v(2, 4, 4, 2, 3, 16, ROWS),
        v(2, 4, 4, 1, 16, ROWS), v(2, 4, 4, 4, 16, ROWS), v(2, 4, 4, 1, 16, ROWS), v(2, 4, 4, 3, 16, ROWS),
        v(ROWS, WIDTH), v(3, WIDTH, WIDTH),
        pltpu.SemaphoreType.REGULAR, pltpu.SemaphoreType.DMA((SEMAPHORES,)),
    ]
    results = (
        shape(ROWS, WIDTH, dtype=BF16), shape(ROWS, WIDTH, dtype=BF16), shape(2, 16), shape(10, 1, 16),
        shape(3, 16, WIDTH), shape(1, 16, WIDTH), shape(4, 16, WIDTH), shape(16, 4 * WIDTH),
    )
    out = pl.pallas_call(
        kernel,
        out_shape=results,
        in_specs=[vmem, vmem, vmem] + [hbm] * 6,
        out_specs=(hbm,) * 8,
        scratch_shapes=scratch,
        compiler_params=pltpu.CompilerParams(
            collective_id=0, has_side_effects=True, vmem_limit_bytes=127 * 2**19
        ),
        name="relay",
    )(
        segment_ids.reshape(1, ROWS),
        gains[0],
        biases[0],
        tokens,
        w_qkv[0].T.reshape(3, 16, WIDTH),
        w_proj[0].T.reshape(1, 16, WIDTH),
        w_fc[0].T.reshape(4, 16, WIDTH),
        w_out[0].T,
        cotangent,
    )
    out = pl.pallas_call(
        move,
        out_shape=results,
        in_specs=[hbm] * 8,
        out_specs=(hbm,) * 8,
        scratch_shapes=[pltpu.VMEM(r.shape, r.dtype) for r in results] + [pltpu.SemaphoreType.DMA((2, 8))],
        name="move",
    )(*out)
    activations, input_grads, g_gains, g_biases, g_qkv, g_proj, g_fc, g_out = out
    return (
        activations[None],
        input_grads[None],
        g_gains[None],
        g_biases.transpose(1, 0, 2),
        g_qkv.reshape(48, WIDTH).T[None],
        g_proj.reshape(16, WIDTH).T[None],
        g_fc.reshape(64, WIDTH).T[None],
        g_out.T[None],
    )


def solution(mesh):
    weight = P("section", None, "dp")
    rows = P("section", "dp", None)
    return jax.shard_map(
        local,
        mesh=mesh,
        in_specs=(P("dp", None), P("dp")) + (weight,) * 6 + (P("dp", None),),
        out_specs=(rows, rows) + (weight,) * 6,
        check_vma=False,
    )
```
